1024 devices in a mesh: segment: 16 (over z), dp: 64 (over x, y, core).
Axes of the slice: x: 4, y: 8, z: 16, core: 2. Of those that a mesh axis runs over, the one named last changes fastest.
Arguments:
- activations: bfloat16 [16, 2, 4, 256, 32, 128], P('segment', None, None, 'dp'), may hold values from -6 to 6
- pre_norm: bfloat16 [16, 2, 4, 256, 32, 128], P('segment', None, None, 'dp'), may hold values from -6 to 6
- cot_first: bfloat16 [16, 4, 256, 32, 128], P('segment', None, 'dp'), may hold values from -6 to 6
- loss_grad: bfloat16 [1, 4, 256, 32, 128], P(None, None, 'dp'), may hold values from -6 to 6
- frame_clip: int32 [16, 2, 64, 4], P('segment', None, 'dp'), may hold values from 0 to 4, as said below
- weight: bfloat16 [16, 3456, 128], P('segment'), may hold values from -0.109375 to 0.109375
- norm_gain: float32 [16, 128], P('segment'), may hold values from 0.5 to 2
- norm_shift: float32 [16, 128], P('segment'), may hold values from -3 to 3
Outputs:
- grad_inputs: bfloat16 [16, 2, 4, 256, 32, 128], P('segment', None, None, 'dp')
- grad_weight: float32 [16, 3456, 128], P('segment', 'dp')
- grad_gain: float32 [16, 128], P('segment', 'dp')
- grad_shift: float32 [16, 128], P('segment', 'dp')
The draws below stay inside these ranges and needn't reach their ends.
Inputs may be any that keep to these rules, and one draw needn't show every extreme that they name: `frame_clip`: for every section and turn the lists of all dp indices are equal. Each list starts with 0, live slots come first, their clip numbers never fall and rise by at most one from slot to slot, padding slots at the end carry 4; at least 2 slots are live.
All inputs are finite; a program needn't handle non-finite values.
Results may differ from the reference program's by a relative error of at most 0.0053.
Values may be sent and summed in bfloat16 or wider, within the bound.
No kernel may reach another device: no remote copies, remote signals or barrier semaphores. Data moves between devices by JAX's collectives and lax.ppermute only.
A program may use at most 32 MiB of HBM per device.

```python
import math
import jax
import jax.numpy as jnp
from jax import lax

CHANNELS = 128
NORM_GROUPS = 32
TAPS = 27
TURNS = 2
STRIP_ROWS = 4
FRAME_COLS = 32
PACK_FRAMES = 4
STRIPS = 64
ALL_ROWS = 256
N_SEGMENT = 16
N_DP = 64


def draw_frame_clip(key, part):
    group_count = N_DP // STRIPS
    key_starts, key_live = jax.random.split(key)
    starts = jax.random.randint(key_starts, (N_SEGMENT, TURNS, group_count, PACK_FRAMES), 0, 2)
    slot = jnp.arange(PACK_FRAMES, dtype=jnp.int32)
    starts = jnp.where(slot[None, None, None, :] == 0, 0, starts)
    numbers = jnp.cumsum(starts, axis=-1)
    live_count = jax.random.randint(key_live, (N_SEGMENT, TURNS, group_count, 1), PACK_FRAMES // 2, PACK_FRAMES + 1)
    group_ids = jnp.arange(group_count, dtype=jnp.int32)[None, None, :, None]
    segment_ids = jnp.arange(N_SEGMENT, dtype=jnp.int32)[:, None, None, None]
    live_count = jnp.where((group_ids == 0) & (segment_ids == 0), PACK_FRAMES // 2, live_count)
    numbers = jnp.where(slot[None, None, None, :] < live_count, numbers, PACK_FRAMES)
    return jnp.repeat(numbers, STRIPS, axis=2).astype(jnp.int32)


def draw_cot_first(key, part):
    key = jax.random.fold_in(key, 11)
    key_noise, key_offset = jax.random.split(key)
    shape = (N_SEGMENT, PACK_FRAMES, N_DP * STRIP_ROWS, FRAME_COLS, CHANNELS)
    noise = jax.random.normal(key_noise, shape, jnp.float32)
    offset = jax.random.uniform(key_offset, (CHANNELS,), jnp.float32, 0.3, 0.9)
    return jnp.clip(noise + offset, -6.0, 6.0).astype(jnp.bfloat16)


def draw_loss_grad(key, part):
    key = jax.random.fold_in(key, 12)
    key_noise, key_offset = jax.random.split(key)
    shape = (TURNS - 1, PACK_FRAMES, N_DP * STRIP_ROWS, FRAME_COLS, CHANNELS)
    noise = jax.random.normal(key_noise, shape, jnp.float32)
    offset = jax.random.uniform(key_offset, (CHANNELS,), jnp.float32, 0.3, 0.9)
    return jnp.clip(noise + offset, -6.0, 6.0).astype(jnp.bfloat16)


def steps_of(own_key, shape, cuts, smallest, high):
    loudness, own = 1.0, jax.random.fold_in(own_key, 6)
    for position, blocks in cuts:
        steps = jnp.exp(jax.random.uniform(jax.random.fold_in(own, position), (blocks,), jnp.float32, smallest / len(cuts), high / len(cuts)))
        loudness = loudness * jnp.repeat(steps, shape[position] // blocks).reshape([-1 if axis == position else 1 for axis in range(len(shape))])
    return loudness


def gaussian(rng, extent, width, bound, shards=(), held_as=jnp.bfloat16):
    factor_of = steps_of(rng, extent, shards, -0.22, 0.18) if shards else 1.0
    array = jax.random.normal(rng, extent, jnp.float32) * width * factor_of
    return jnp.minimum(jnp.maximum(array, -bound), bound).astype(held_as)


def setup_inputs(seed: int = 0) -> dict:
    streams_of = jax.random.split(jax.random.key(seed), 9)
    activations = gaussian(streams_of[0], (N_SEGMENT, TURNS, PACK_FRAMES, ALL_ROWS, FRAME_COLS, CHANNELS), 1.0, 6.0, ((0, 16), (3, 64)))
    pre_norm = gaussian(streams_of[1], (N_SEGMENT, TURNS, PACK_FRAMES, ALL_ROWS, FRAME_COLS, CHANNELS), 1.0, 6.0, ((0, 16), (3, 64)))
    cot_first = draw_cot_first(jax.random.fold_in(streams_of[8], 71), 0)
    loss_grad = draw_loss_grad(jax.random.fold_in(streams_of[8], 71), 0)
    frame_clip = draw_frame_clip(jax.random.fold_in(streams_of[8], 71), 0)
    weight = gaussian(streams_of[5], (N_SEGMENT, TAPS * CHANNELS, CHANNELS), (TAPS * CHANNELS) ** -0.5, 0.109375, ((0, 16),))
    norm_gain = jnp.clip(jnp.exp(math.log(2.0) - 1.3862944 * jax.random.uniform(streams_of[6], (N_SEGMENT, CHANNELS), jnp.float32) ** steps_of(streams_of[6], (N_SEGMENT, CHANNELS), ((0, 16),), -0.2, 0.2)), 0.5, 2.0)
    norm_shift = gaussian(streams_of[7], (N_SEGMENT, CHANNELS), 0.5, 3.0, ((0, 16),), jnp.float32)
    return {"activations": activations, "pre_norm": pre_norm, "cot_first": cot_first, "loss_grad": loss_grad, "frame_clip": frame_clip, "weight": weight, "norm_gain": norm_gain, "norm_shift": norm_shift}


epsilon = 1e-05

def layer_back(inputs, saved, incoming, clips, kernel, gain, shift_vec):
    group_count = N_DP // STRIPS
    height = STRIPS * STRIP_ROWS
    per_group = CHANNELS // NORM_GROUPS
    frames = PACK_FRAMES
    clip_cols = clips.T.astype(jnp.int32)
    live = clip_cols < frames
    onehot = (clip_cols[:, :, None] == jnp.arange(frames, dtype=jnp.int32)[None, None, :]).astype(jnp.float32)
    cells = float(height * FRAME_COLS * per_group)
    count = jnp.maximum(lax.optimization_barrier(jnp.sum(onehot, axis=0)) * cells, 1.0)[:, :, None]

    def to_clips(values):
        return jnp.einsum('fgc,fgk->gck', onehot, values, precision=lax.Precision.HIGHEST)

    def to_frames(values):
        spread = jnp.einsum('fgc,gck->fgk', onehot, values, precision=lax.Precision.HIGHEST)
        return spread[:, :, None, None, :, None]
    pre = saved.astype(jnp.float32).reshape(frames, group_count, height, FRAME_COLS, NORM_GROUPS, per_group)
    first = lax.optimization_barrier(jnp.sum(pre, axis=(2, 3, 5)))
    second = lax.optimization_barrier(jnp.sum(pre * pre, axis=(2, 3, 5)))
    mean_clip = to_clips(first) / count
    var_clip = to_clips(second) / count - mean_clip * mean_clip
    rstd_clip = 1.0 / jnp.sqrt(var_clip + epsilon)
    mean_frame = to_frames(mean_clip)
    rstd_frame = to_frames(rstd_clip)
    normed = (pre - mean_frame) * rstd_frame
    gain_grid = gain.reshape(NORM_GROUPS, per_group)
    shift_grid = shift_vec.reshape(NORM_GROUPS, per_group)
    act = normed * gain_grid + shift_grid
    sigm = jax.nn.sigmoid(act)
    live_mask = live[:, :, None, None, None, None]
    upstream = incoming.astype(jnp.float32).reshape(pre.shape)
    grad_act = jnp.where(live_mask, upstream * sigm * (1.0 + act * (1.0 - sigm)), 0.0)
    gain_grad = lax.optimization_barrier(jnp.sum(grad_act * normed, axis=(0, 1, 2, 3))).reshape(CHANNELS)
    shift_grad = lax.optimization_barrier(jnp.sum(grad_act, axis=(0, 1, 2, 3))).reshape(CHANNELS)
    scaled = grad_act * gain_grid
    avg_a = to_frames(to_clips(lax.optimization_barrier(jnp.sum(scaled, axis=(2, 3, 5)))) / count)
    avg_b = to_frames(to_clips(lax.optimization_barrier(jnp.sum(scaled * normed, axis=(2, 3, 5)))) / count)
    grad_pre = jnp.where(live_mask, rstd_frame * (scaled - avg_a - normed * avg_b), 0.0)
    grad_pre = grad_pre.astype(jnp.bfloat16).reshape(frames, group_count, height, FRAME_COLS, CHANNELS)
    inputs_grid = inputs.reshape(frames, group_count, height, FRAME_COLS, CHANNELS)
    earlier = jnp.concatenate([jnp.full((2, group_count), -1, jnp.int32), clip_cols], axis=0)
    grad_pad = jnp.pad(grad_pre, ((0, 2), (0, 0), (1, 1), (1, 1), (0, 0)))
    input_pad = jnp.pad(inputs_grid, ((2, 0), (0, 0), (1, 1), (1, 1), (0, 0)))
    zero_value = jnp.zeros((), grad_pre.dtype)
    total = jnp.zeros((frames * group_count * height * FRAME_COLS, CHANNELS), jnp.float32)
    blocks = []
    for time_tap in range(3):
        pair_ok = live & (earlier[2 - time_tap:2 - time_tap + frames] == clip_cols)
        kept = jnp.where(pair_ok[:, :, None, None, None], grad_pre, zero_value)
        pair_pad = jnp.concatenate([pair_ok, jnp.zeros((2, group_count), bool)], axis=0)
        kept_pad = jnp.where(pair_pad[:, :, None, None, None], grad_pad, zero_value)
        for row_tap in (-1, 0, 1):
            for col_tap in (-1, 0, 1):
                tap_index = time_tap * 9 + (row_tap + 1) * 3 + (col_tap + 1)
                kernel_tap = kernel[tap_index * CHANNELS:(tap_index + 1) * CHANNELS]
                shifted = kept_pad[time_tap:time_tap + frames, :, 1 - row_tap:1 - row_tap + height, 1 - col_tap:1 - col_tap + FRAME_COLS]
                total = total + jnp.dot(shifted.reshape(-1, CHANNELS), kernel_tap.T, preferred_element_type=jnp.float32)
                moved = input_pad[2 - time_tap:2 - time_tap + frames, :, 1 + row_tap:1 + row_tap + height, 1 + col_tap:1 + col_tap + FRAME_COLS]
                blocks.append(jnp.dot(moved.reshape(-1, CHANNELS).T, kept.reshape(-1, CHANNELS), preferred_element_type=jnp.float32))
    grad_in = total.astype(jnp.bfloat16).reshape(frames, group_count * height, FRAME_COLS, CHANNELS)
    return (grad_in, jnp.concatenate(blocks, axis=0), gain_grad, shift_grad)

def reference(activations, pre_norm, cot_first, loss_grad, frame_clip, weight, norm_gain, norm_shift):
    handed = [None] * N_SEGMENT
    results = [[None] * TURNS for segment_pos in range(N_SEGMENT)]
    weight_sums = [None] * N_SEGMENT
    gain_sums = [None] * N_SEGMENT
    shift_sums = [None] * N_SEGMENT
    for turn_index in range(TURNS):
        fresh = [None] * N_SEGMENT
        for segment_pos in range(N_SEGMENT):
            if turn_index == 0:
                incoming = cot_first[segment_pos]
            elif segment_pos == N_SEGMENT - 1:
                incoming = loss_grad[turn_index - 1]
            else:
                incoming = handed[segment_pos + 1]
            clips = frame_clip[segment_pos, turn_index, ::STRIPS]
            grad_in, weight_part, gain_part, shift_part = layer_back(activations[segment_pos, turn_index], pre_norm[segment_pos, turn_index], incoming, clips, weight[segment_pos], norm_gain[segment_pos], norm_shift[segment_pos])
            fresh[segment_pos] = grad_in
            results[segment_pos][turn_index] = grad_in
            if turn_index == 0:
                weight_sums[segment_pos] = weight_part
                gain_sums[segment_pos] = gain_part
                shift_sums[segment_pos] = shift_part
            else:
                weight_sums[segment_pos] = weight_sums[segment_pos] + weight_part
                gain_sums[segment_pos] = gain_sums[segment_pos] + gain_part
                shift_sums[segment_pos] = shift_sums[segment_pos] + shift_part
        handed = fresh
    scale = 1.0 / N_DP
    grad_inputs = jnp.stack([jnp.stack(row, axis=0) for row in results], axis=0)
    grad_weight = jnp.stack(weight_sums, axis=0) * scale
    grad_gain = jnp.stack(gain_sums, axis=0) * scale
    grad_shift = jnp.stack(shift_sums, axis=0) * scale
    return (grad_inputs, grad_weight, grad_gain, grad_shift)
```

```python
import functools
import jax
import jax.numpy as jnp
from jax import lax
from jax.experimental import pallas as pl
from jax.experimental.pallas import tpu as pltpu
from jax.sharding import PartitionSpec as P

F32, BF16 = jnp.float32, jnp.bfloat16
FRAMES, ROWS, COLS, CH = 4, 4, 32, 128
GROUPS, PER = 32, 4
TAPS = 27
EPS = 1e-05
VMEM = pl.BlockSpec(memory_space=pltpu.VMEM)
SMEM = pl.BlockSpec(memory_space=pltpu.SMEM)


def exact_dot(a, b):
    return jnp.dot(a, b, precision=lax.Precision.HIGHEST, preferred_element_type=F32)


def iota(dim, shape=(CH, CH)):
    return lax.broadcasted_iota(jnp.int32, shape, dim)


def pack_rows(per_frame):
    total = None
    for f in range(FRAMES):
        place = (iota(1) == f * GROUPS + (iota(0) >> 2)).astype(F32)
        term = exact_dot(per_frame[f], place)
        total = term if total is None else total + term
    return total


def unpack_rows(table, clips):
    slot = iota(0) >> 5
    clip_of_row = jnp.where(
        slot == 0, clips[0], jnp.where(slot == 1, clips[1], jnp.where(slot == 2, clips[2], clips[3]))
    )
    same_group = (iota(0) & (GROUPS - 1)) == (iota(1) >> 2)
    return [
        exact_dot(table, (same_group & (clip_of_row == clips[f])).astype(F32)) for f in range(FRAMES)
    ]


def counts(clips, cells):
    out = []
    for f in range(FRAMES):
        n = jnp.int32(0)
        for other in range(FRAMES):
            n = n + (clips[other] == clips[f]).astype(jnp.int32)
        out.append(n.astype(F32) * cells)
    return out


def clips_of(info_ref, turn):
    return [info_ref[turn * FRAMES + f] for f in range(FRAMES)]


def paired(clips, f, kt):
    ok = clips[f] < FRAMES
    if kt:
        ok = ok & (clips[f - kt] == clips[f])
    return ok


def colsum(x):
    return jnp.sum(x, axis=0, keepdims=True)


def flat(x):
    return x.reshape(-1, CH)


def statistics(table, clips, cells):
    total = unpack_rows(table, clips)
    count = counts(clips, cells)
    out = []
    for f in range(FRAMES):
        mean = total[f][0:1] / count[f]
        var = total[f][1:2] / count[f] - mean * mean
        out.append((mean, 1.0 / jnp.sqrt(var + EPS)))
    return out


def act_slope(normed, gain, shift):
    act = normed * gain + shift
    sigm = jax.nn.sigmoid(act)
    return sigm * (1.0 + act * (1.0 - sigm))


def sums_kernel(pre_ref, cot_ref, loss_ref, out_ref, head_ref, tail_ref):
    per_frame = []
    for f in range(FRAMES):
        rows = []
        for t in range(2):
            x = flat(pre_ref[t, f].astype(F32))
            rows += [colsum(x), colsum(x * x)]
        per_frame.append(jnp.concatenate(rows, axis=0))
    out_ref[...] = jnp.broadcast_to(pack_rows(per_frame)[None], out_ref.shape)
    for ref, two, one in ((head_ref, 0, 0), (tail_ref, ROWS - 2, ROWS - 1)):
        ref[:, 0:2] = pre_ref[0, :, two : two + 2]
        ref[:, 2:4] = cot_ref[:, two : two + 2]
        ref[:, 4:5] = pre_ref[1, :, one : one + 1]
        ref[:, 5:6] = loss_ref[:, one : one + 1]


def act_first_kernel(
    cells, info_ref, table_ref, pre_ref, cot_ref, up_ref, down_ref, gain_ref, shift_ref,
    out_ref, scaled_ref, normed_ref, stats_ref, parts_ref,
):
    table = jnp.sum(table_ref[...], axis=0)
    gain, shift = gain_ref[...], shift_ref[...]
    clips = clips_of(info_ref, 0)
    stats = statistics(table[0:2], clips, cells)
    later = statistics(table[2:4], clips_of(info_ref, 1), cells)
    per_frame = []
    gain_part = jnp.zeros((1, CH), F32)
    shift_part = jnp.zeros((1, CH), F32)
    for f in range(FRAMES):
        mean, rstd = stats[f]
        live = clips[f] < FRAMES
        sums = None
        for row, count, pre, cot in (
            (0, 2, up_ref[f, 0:2], up_ref[f, 2:4]),
            (2, ROWS, pre_ref[0, f], cot_ref[f]),
            (2 + ROWS, 2, down_ref[f, 0:2], down_ref[f, 2:4]),
        ):
            normed = (flat(pre.astype(F32)) - mean) * rstd
            grad_act = flat(cot.astype(F32)) * act_slope(normed, gain, shift)
            grad_act = jnp.where(live, grad_act, 0.0)
            if count == ROWS:
                sums = (colsum(grad_act), colsum(grad_act * normed))
            scaled_ref[f, row : row + count] = ((rstd * gain) * grad_act).reshape(count, COLS, CH)
            normed_ref[f, row : row + count] = (normed * rstd).reshape(count, COLS, CH)
        shift_part = shift_part + sums[0]
        gain_part = gain_part + sums[1]
        per_frame.append(jnp.concatenate([sums[0] * gain, sums[1] * gain], axis=0))
        stats_ref[f : f + 1] = rstd
        stats_ref[FRAMES + f : FRAMES + f + 1] = later[f][0]
        stats_ref[2 * FRAMES + f : 2 * FRAMES + f + 1] = later[f][1]
    parts_ref[0:1] = gain_part
    parts_ref[1:2] = shift_part
    out_ref[...] = jnp.broadcast_to(pack_rows(per_frame)[None], out_ref.shape)


def write_columns(columns_ref, info_ref, halo, clips, table, cells, scaled_ref, normed_ref, rstd_of):
    total = unpack_rows(table, clips)
    count = counts(clips, cells)
    rows = ROWS + 2 * halo
    place = iota(0, (rows * COLS, CH))
    column = place & (COLS - 1)
    row = place >> 5
    first = jnp.where(info_ref[2 * FRAMES] == 1, halo, 0)
    last = jnp.where(info_ref[2 * FRAMES + 1] == 1, halo + ROWS, rows)
    inside = (row >= first) & (row < last)
    for f in range(FRAMES):
        avg_a = total[f][0:1] / count[f]
        avg_b = total[f][1:2] / count[f]
        keep = inside & (clips[f] < FRAMES)
        value = flat(scaled_ref[f]) - rstd_of(f) * avg_a - flat(normed_ref[f]) * avg_b
        value = jnp.where(keep, value, 0.0)
        left = jnp.where(column == COLS - 1, 0.0, pltpu.roll(value, rows * COLS - 1, 0))
        right = jnp.where(column == 0, 0.0, pltpu.roll(value, 1, 0))
        columns_ref[f, :, 0:CH] = left.astype(BF16)
        columns_ref[f, :, CH : 2 * CH] = value.astype(BF16)
        columns_ref[f, :, 2 * CH : 3 * CH] = right.astype(BF16)


def conv_frame(columns_ref, weight_ref, clips, f, rows):
    total = None
    for kt in range(min(3, FRAMES - f)):
        part = None
        for dy in (-1, 0, 1):
            start = (1 - dy) * COLS
            term = jnp.dot(
                columns_ref[f + kt, start : start + rows * COLS],
                weight_ref[3 * kt + dy + 1],
                preferred_element_type=F32,
            )
            part = term if part is None else part + term
        part = jnp.where(paired(clips, f + kt, kt), part, 0.0)
        total = part if total is None else total + part
    return total.astype(BF16).reshape(rows, COLS, CH)


def kernel_terms(columns_ref, act_ref, clips, halo, kt, dy):
    count = FRAMES - kt
    start = (halo - dy) * COLS
    blocks = [
        jnp.where(paired(clips, f + kt, kt), act_ref[:, f * CH : (f + 1) * CH], jnp.zeros((), BF16))
        for f in range(count)
    ]
    columns = columns_ref[kt:FRAMES, start : start + ROWS * COLS, :].reshape(count * CH, 3 * CH)
    return jnp.dot(jnp.concatenate(blocks, axis=1), columns, preferred_element_type=F32)


def conv_first_kernel(
    cells, info_ref, table_ref, scaled_ref, normed_ref, stats_ref, weight_ref, grad_ref, columns_ref
):
    clips = clips_of(info_ref, 0)
    table = jnp.sum(table_ref[...], axis=0)
    write_columns(
        columns_ref, info_ref, 2, clips, table, cells, scaled_ref, normed_ref,
        lambda f: stats_ref[f : f + 1],
    )
    for f in range(FRAMES):
        grad_ref[f] = conv_frame(columns_ref, weight_ref, clips, f, ROWS + 2)


def weight_first_kernel(info_ref, columns_ref, act_ref, out_ref):
    clips = clips_of(info_ref, 0)
    for kt in range(3):
        for dy in (-1, 0, 1):
            terms = kernel_terms(columns_ref, act_ref, clips, 2, kt, dy)
            tap = 9 * kt + 3 * (dy + 1)
            for dx in range(3):
                out_ref[tap + dx] = terms[:, dx * CH : (dx + 1) * CH]


def act_second_kernel(
    info_ref, hand_ref, loss_ref, pre_ref, up_ref, down_ref, stats_ref, parts_ref, gain_ref, shift_ref,
    out_ref, scaled_ref, normed_ref,
):
    gain, shift = gain_ref[...], shift_ref[...]
    clips = clips_of(info_ref, 1)
    is_last = info_ref[2 * FRAMES + 2] == 1
    per_frame = []
    gain_part = parts_ref[0:1]
    shift_part = parts_ref[1:2]
    for f in range(FRAMES):
        mean = stats_ref[FRAMES + f : FRAMES + f + 1]
        rstd = stats_ref[2 * FRAMES + f : 2 * FRAMES + f + 1]
        live = clips[f] < FRAMES
        sums = None
        for row, count, pre, loss in (
            (0, 1, up_ref[f, 4:5], up_ref[f, 5:6]),
            (1, ROWS, pre_ref[1, f], loss_ref[f]),
            (1 + ROWS, 1, down_ref[f, 4:5], down_ref[f, 5:6]),
        ):
            normed = (flat(pre.astype(F32)) - mean) * rstd
            incoming = jnp.where(
                is_last, flat(loss.astype(F32)), flat(hand_ref[f, row : row + count].astype(F32))
            )
            grad_act = jnp.where(live, incoming * act_slope(normed, gain, shift), 0.0)
            if count == ROWS:
                sums = (colsum(grad_act), colsum(grad_act * normed))
            scaled_ref[f, row : row + count] = ((rstd * gain) * grad_act).reshape(count, COLS, CH)
            normed_ref[f, row : row + count] = (normed * rstd).reshape(count, COLS, CH)
        shift_part = shift_part + sums[0]
        gain_part = gain_part + sums[1]
        per_frame.append(jnp.concatenate([sums[0] * gain, sums[1] * gain], axis=0))
    rows = jnp.concatenate([pack_rows(per_frame), gain_part, shift_part], axis=0)
    out_ref[...] = jnp.broadcast_to(rows[None], out_ref.shape)


def weight_second_kernel(
    cells, scale, info_ref, table_ref, scaled_ref, normed_ref, stats_ref, act_ref, first_ref,
    out_ref, columns_ref, parts_ref, sum_ref,
):
    clips = clips_of(info_ref, 1)
    table = jnp.sum(table_ref[...], axis=0)
    parts_ref[...] = table[2:4] * scale
    write_columns(
        columns_ref, info_ref, 1, clips, table[0:2], cells, scaled_ref, normed_ref,
        lambda f: stats_ref[2 * FRAMES + f : 2 * FRAMES + f + 1],
    )
    for kt in range(3):
        for dy in (-1, 0, 1):
            terms = kernel_terms(columns_ref, act_ref, clips, 1, kt, dy)
            tap = 9 * kt + 3 * (dy + 1)
            for dx in range(3):
                at = (tap + dx) * CH
                sum_ref[at : at + CH] = first_ref[tap + dx] + terms[:, dx * CH : (dx + 1) * CH]
    cores, chips, chunk, _ = out_ref.shape
    for chip in range(chips):
        for core in range(cores):
            at = (chip * cores + core) * chunk
            out_ref[core, chip] = sum_ref[at : at + chunk].astype(BF16)


def conv_second_kernel(info_ref, columns_ref, weight_ref, first_ref, out_ref):
    clips = clips_of(info_ref, 1)
    for f in range(FRAMES):
        out_ref[0, f] = first_ref[f, 1 : 1 + ROWS]
        out_ref[1, f] = conv_frame(columns_ref, weight_ref, clips, f, ROWS)


def call(kernel, name, args, outs, scratch=(), flops=10_000_000):
    smem = [SMEM] if args[0].dtype == jnp.int32 else []
    size = sum(a.size * a.dtype.itemsize for a in list(args) + list(outs))
    return pl.pallas_call(
        kernel,
        out_shape=tuple(outs),
        in_specs=smem + [VMEM] * (len(args) - len(smem)),
        out_specs=tuple([VMEM] * len(outs)),
        scratch_shapes=list(scratch),
        compiler_params=pltpu.CompilerParams(vmem_limit_bytes=40 * 1024 * 1024),
        cost_estimate=pl.CostEstimate(flops=flops, bytes_accessed=size, transcendentals=0),
        name=name,
    )(*args)


def shape(dims, dtype=F32):
    return jax.ShapeDtypeStruct(dims, dtype)


def local(activations, pre_norm, cot_first, loss_grad, frame_clip, weight, norm_gain, norm_shift):
    dp = lax.axis_size("dp")
    me = lax.axis_index("dp")
    cells = float(dp * ROWS * COLS * PER)
    chips, chunk = dp // 2, TAPS * CH // dp
    flags = [me == 0, me == dp - 1, lax.axis_index("segment") == lax.axis_size("segment") - 1]
    info = jnp.concatenate([frame_clip.reshape(2 * FRAMES), jnp.stack(flags).astype(jnp.int32)])
    pre = pre_norm[0]
    cot, loss = cot_first[0], loss_grad[0]
    taps = weight[0].reshape(9, 3, CH, CH).transpose(0, 1, 3, 2).reshape(9, 3 * CH, CH)
    act = activations[0].reshape(2, FRAMES * ROWS * COLS, CH).transpose(0, 2, 1)

    def exchange(table):
        return lax.all_to_all(table, "dp", 0, 0, tiled=True)

    edge = (FRAMES, 6, COLS, CH)
    table, head, tail = call(
        sums_kernel, "sums", (pre, cot, loss),
        (shape((dp, 4, CH)), shape(edge, BF16), shape(edge, BF16)),
    )
    down = lax.ppermute(head, "dp", [(i + 1, i) for i in range(dp - 1)])
    up = lax.ppermute(tail, "dp", [(i, i + 1) for i in range(dp - 1)])
    table = exchange(table)

    wide = (FRAMES, ROWS + 4, COLS, CH)
    table, scaled, normed, stats, parts = call(
        functools.partial(act_first_kernel, cells), "act_first",
        (info, table, pre, cot, up, down, norm_gain, norm_shift),
        (shape((dp, 2, CH)), shape(wide), shape(wide), shape((3 * FRAMES, CH)), shape((2, CH))),
    )
    table = exchange(table)

    grad_first, columns = call(
        functools.partial(conv_first_kernel, cells), "conv_first",
        (info, table, scaled, normed, stats, taps),
        (shape((FRAMES, ROWS + 2, COLS, CH), BF16), shape((FRAMES, (ROWS + 4) * COLS, 3 * CH), BF16)),
        flops=700_000_000,
    )
    count = lax.axis_size("segment")
    hand = lax.ppermute(grad_first, "segment", [(i + 1, i) for i in range(count - 1)])
    (weight_first,) = call(
        weight_first_kernel, "weight_first", (info, columns, act[0]),
        (shape((TAPS, CH, CH)),), flops=450_000_000,
    )

    wide = (FRAMES, ROWS + 2, COLS, CH)
    table, scaled, normed = call(
        act_second_kernel, "act_second",
        (info, hand, loss, pre, up, down, stats, parts, norm_gain, norm_shift),
        (shape((dp, 4, CH)), shape(wide), shape(wide)),
    )
    table = exchange(table)

    terms, columns, parts = call(
        functools.partial(weight_second_kernel, cells, 1.0 / dp), "weight_second",
        (info, table, scaled, normed, stats, act[1], weight_first),
        (
            shape((2, chips, chunk, CH), BF16),
            shape((FRAMES, (ROWS + 2) * COLS, 3 * CH), BF16),
            shape((2, CH)),
        ),
        scratch=[pltpu.VMEM((TAPS * CH, CH), F32)],
        flops=450_000_000,
    )
    pairs = [[2 * i, 2 * i + 1] for i in range(chips)]
    terms = lax.all_to_all(terms, "dp", 0, 0, axis_index_groups=pairs, tiled=True)
    terms = jnp.sum(terms.astype(F32), axis=0).astype(BF16)
    sides = [[2 * i + core for i in range(chips)] for core in range(2)]
    terms = lax.all_to_all(terms, "dp", 0, 0, axis_index_groups=sides, tiled=True)
    grad_weight = jnp.sum(terms.astype(F32), axis=0) * (1.0 / dp)

    (grad_inputs,) = call(
        conv_second_kernel, "conv_second", (info, columns, taps, grad_first),
        (shape((2, FRAMES, ROWS, COLS, CH), BF16),), flops=450_000_000,
    )
    width = CH // dp
    own = lax.dynamic_slice_in_dim(parts, me * width, width, axis=1)
    return (grad_inputs[None], grad_weight[None], own[0:1], own[1:2])


def solution(mesh):
    in_specs = (
        P("segment", None, None, "dp", None, None),
        P("segment", None, None, "dp", None, None),
        P("segment", None, "dp", None, None),
        P(None, None, "dp", None, None),
        P("segment", None, "dp", None),
        P("segment", None, None),
        P("segment", None),
        P("segment", None),
    )
    out_specs = (
        P("segment", None, None, "dp", None, None),
        P("segment", "dp", None),
        P("segment", "dp"),
        P("segment", "dp"),
    )
    return jax.shard_map(local, mesh=mesh, in_specs=in_specs, out_specs=out_specs, check_vma=False)
```

```python
import functools
import jax
import jax.numpy as jnp
from jax import lax
from jax.experimental import pallas as pl
from jax.experimental.pallas import tpu as pltpu
from jax.sharding import PartitionSpec as P

F32, BF16 = jnp.float32, jnp.bfloat16
FRAMES, ROWS, COLS, CH = 4, 4, 32, 128
GROUPS, PER = 32, 4
TAPS = 27
EPS = 1e-05
VMEM = pl.BlockSpec(memory_space=pltpu.VMEM)
SMEM = pl.BlockSpec(memory_space=pltpu.SMEM)
HBM = pl.BlockSpec(memory_space=pltpu.HBM)

GAIN, SHIFT, CORE, LAST = 0, 1, 2, 3
TURN = 24
INV, LIVE, TOP, BOTTOM, PAIR1, PAIR2 = (8 + 4 * n for n in range(6))
OTHER_TOP, OTHER_BOTTOM = 56, 60
CLIPS = 64
OTHER_TURN = 16
PARAM_ROWS = 80
MEAN0, RSTD0, MEAN1, RSTD1, GAIN_PART, SHIFT_PART = 0, 4, 8, 12, 16, 17
STAT_ROWS = 24


def iota(dim, dims=(CH, CH)):
    return lax.broadcasted_iota(jnp.int32, dims, dim)


def split_dot(rows, marks):
    count = rows.shape[0]
    high = rows.astype(BF16)
    rest = rows - high.astype(F32)
    middle = rest.astype(BF16)
    low = (rest - middle.astype(F32)).astype(BF16)
    out = jnp.dot(
        jnp.concatenate([high.astype(F32), middle.astype(F32), low.astype(F32)], axis=0).astype(BF16),
        marks,
        preferred_element_type=F32,
    )
    return out[0:count] + out[count : 2 * count] + out[2 * count : 3 * count]


def pack_rows(per_frame):
    rows = jnp.concatenate(per_frame, axis=1)
    dims = (FRAMES * CH, CH)
    marks = (iota(1, dims) == (iota(0, dims) >> 2)).astype(F32).astype(BF16)
    return split_dot(rows, marks)


def unpack_rows(table, marks):
    total = split_dot(table, marks)
    return [total[:, f * CH : (f + 1) * CH] for f in range(FRAMES)]


def row(ref, at):
    return ref[at : at + 1]


def colsum(x):
    return jnp.sum(x, axis=0, keepdims=True)


def flat(x):
    return x.reshape(-1, CH)


def act_slope(normed, gain, shift):
    act = normed * gain + shift
    sigm = jax.nn.sigmoid(act)
    return sigm * (1.0 + act * (1.0 - sigm))


def copy_in(pairs, sems):
    copies = [pltpu.make_async_copy(src, dst, sems.at[n]) for n, (src, dst) in enumerate(pairs)]
    for copy in copies:
        copy.start()
    return copies


def sums_kernel(pre_ref, cot_ref, loss_ref, out_ref, head_ref, tail_ref, held_ref, sems):
    pairs = [(pre_ref, held_ref)]
    for ref, two, one in ((head_ref, 0, 0), (tail_ref, ROWS - 2, ROWS - 1)):
        pairs += [
            (pre_ref.at[0, :, two : two + 2], ref.at[:, 0:2]),
            (cot_ref.at[:, two : two + 2], ref.at[:, 2:4]),
            (pre_ref.at[1, :, one : one + 1], ref.at[:, 4:5]),
            (loss_ref.at[:, one : one + 1], ref.at[:, 5:6]),
        ]
    copies = copy_in(pairs, sems)
    copies[0].wait()
    per_frame = []
    for f in range(FRAMES):
        rows = []
        for t in range(2):
            x = flat(held_ref[t, f].astype(F32))
            rows += [colsum(x), colsum(x * x)]
        per_frame.append(jnp.concatenate(rows, axis=0))
    out_ref[...] = jnp.broadcast_to(pack_rows(per_frame)[None], out_ref.shape)
    for copy in copies[1:]:
        copy.wait()


def clip_marks(params_ref, turn):
    slot = iota(0) >> 5
    clips = [row(params_ref, CLIPS + FRAMES * turn + f) for f in range(FRAMES)]
    clip_of_row = jnp.where(
        slot == 0, clips[0], jnp.where(slot == 1, clips[1], jnp.where(slot == 2, clips[2], clips[3]))
    )
    same_group = (iota(0) & (GROUPS - 1)) == (iota(1) >> 2)
    blocks = [(same_group & (clip_of_row == clips[f])).astype(F32).astype(BF16) for f in range(FRAMES)]
    return jnp.concatenate(blocks, axis=1)


def prepare_kernel(
    cells, flag_ref, clip_hbm, pre_ref, cot_ref, gain_ref, shift_ref,
    own_ref, params_ref, clip_ref, held_pre, held_cot, sems,
):
    copies = copy_in(
        [
            (clip_hbm, clip_ref), (pre_ref, held_pre), (cot_ref, held_cot),
            (gain_ref, params_ref.at[GAIN : GAIN + 1]), (shift_ref, params_ref.at[SHIFT : SHIFT + 1]),
        ],
        sems,
    )

    def put(at, scalar):
        params_ref[at : at + 1] = jnp.full((1, CH), scalar, F32)

    put(CORE, flag_ref[4].astype(F32))
    put(LAST, flag_ref[5].astype(F32))
    params_ref[LAST + 1 : INV] = jnp.zeros((INV - LAST - 1, CH), F32)
    flag = [flag_ref[n].astype(F32) for n in range(4)]
    copies[0].wait()
    for t in range(2):
        clips = [clip_ref[0, t, 0, f] for f in range(FRAMES)]
        for f in range(FRAMES):
            count = jnp.int32(0)
            for other in range(FRAMES):
                count = count + (clips[other] == clips[f]).astype(jnp.int32)
            live = (clips[f] < FRAMES).astype(F32)
            base = TURN * t + f
            params_ref[base + INV : base + INV + 1] = 1.0 / jnp.full((1, CH), count.astype(F32) * cells, F32)
            put(base + LIVE, live)
            put(base + TOP, live * flag[0])
            put(base + BOTTOM, live * flag[1])
            put(CLIPS + FRAMES * t + f, clips[f].astype(F32))
            for kt, at in ((1, PAIR1), (2, PAIR2)):
                pair = live * (clips[f - kt] == clips[f]).astype(F32) if f >= kt else live * 0.0
                put(base + at, pair)
            put(OTHER_TURN * t + OTHER_TOP + f, live * flag[2])
            put(OTHER_TURN * t + OTHER_BOTTOM + f, live * flag[3])
    for copy in copies[1:]:
        copy.wait()
    own_ref[0] = held_pre[0].astype(F32)
    own_ref[1] = held_cot[...].astype(F32)


def act_first_kernel(table_ref, own_ref, params_ref, out_ref, stats_ref):
    table = jnp.sum(table_ref[...], axis=0)
    gain, shift = row(params_ref, GAIN), row(params_ref, SHIFT)
    for t, mean_at, rstd_at in ((0, MEAN0, RSTD0), (1, MEAN1, RSTD1)):
        total = unpack_rows(table[2 * t : 2 * t + 2], clip_marks(params_ref, t))
        for f in range(FRAMES):
            inverse = row(params_ref, TURN * t + INV + f)
            mean = total[f][0:1] * inverse
            var = total[f][1:2] * inverse - mean * mean
            stats_ref[mean_at + f : mean_at + f + 1] = mean
            stats_ref[rstd_at + f : rstd_at + f + 1] = 1.0 / jnp.sqrt(var + EPS)
    per_frame = []
    gain_part = jnp.zeros((1, CH), F32)
    shift_part = jnp.zeros((1, CH), F32)
    for f in range(FRAMES):
        normed = (flat(own_ref[0, f]) - row(stats_ref, MEAN0 + f)) * row(stats_ref, RSTD0 + f)
        grad_act = flat(own_ref[1, f]) * act_slope(normed, gain, shift)
        live = row(params_ref, LIVE + f)
        plain = colsum(grad_act) * live
        times = colsum(grad_act * normed) * live
        shift_part = shift_part + plain
        gain_part = gain_part + times
        per_frame.append(jnp.concatenate([plain * gain, times * gain], axis=0))
    stats_ref[GAIN_PART : GAIN_PART + 1] = gain_part
    stats_ref[SHIFT_PART : SHIFT_PART + 1] = shift_part
    stats_ref[SHIFT_PART + 1 :] = jnp.zeros((STAT_ROWS - SHIFT_PART - 1, CH), F32)
    out_ref[...] = jnp.broadcast_to(pack_rows(per_frame)[None], out_ref.shape)


def fields(pre, incoming, mean, rstd, gain, shift, mask):
    normed = (flat(pre.astype(F32)) - mean) * rstd
    scaled = flat(incoming.astype(F32)) * act_slope(normed, gain, shift) * gain
    rstd = rstd * mask
    return scaled * rstd, normed * rstd


def fields_first_kernel(
    up_ref, down_ref, params_ref, stats_ref, pre_ref, cot_ref, loss_ref, act_ref,
    out_ref, bundle_ref, loss_out_ref, held_pre, held_cot, held_loss, sems,
):
    pairs = [
        (pre_ref.at[0], held_pre), (cot_ref, held_cot), (loss_ref, held_loss),
        (act_ref.at[0], bundle_ref.at[:, 6 : 6 + ROWS]), (act_ref.at[1], bundle_ref.at[:, 6 + ROWS : 6 + 2 * ROWS]),
    ]
    for at, edge, own in ((0, 4, pre_ref.at[1]), (14, 1, pre_ref.at[0]), (20, 3, cot_ref)):
        below = 0 if at == 14 else 2 if at == 20 else 4
        pairs += [
            (up_ref.at[:, edge : edge + 1], bundle_ref.at[:, at : at + 1]),
            (own, bundle_ref.at[:, at + 1 : at + 1 + ROWS]),
            (down_ref.at[:, below : below + 1], bundle_ref.at[:, at + 1 + ROWS : at + 2 + ROWS]),
        ]
    copies = copy_in(pairs, sems)
    for copy in copies[:3]:
        copy.wait()
    gain, shift = row(params_ref, GAIN), row(params_ref, SHIFT)
    last = row(params_ref, LAST).reshape(1, 1, 1, CH)
    loss_out_ref[:, 0:1] = (up_ref[:, 5:6].astype(F32) * last).astype(BF16)
    loss_out_ref[:, 1 : 1 + ROWS] = (held_loss[...].astype(F32) * last).astype(BF16)
    loss_out_ref[:, 1 + ROWS : 2 + ROWS] = (down_ref[:, 5:6].astype(F32) * last).astype(BF16)
    for f in range(FRAMES):
        mean, rstd = row(stats_ref, MEAN0 + f), row(stats_ref, RSTD0 + f)
        for at, count, pre, cot, mask in (
            (0, 2, up_ref[f, 0:2], up_ref[f, 2:4], TOP),
            (2, ROWS, held_pre[f], held_cot[f], LIVE),
            (2 + ROWS, 2, down_ref[f, 0:2], down_ref[f, 2:4], BOTTOM),
        ):
            pair = fields(pre, cot, mean, rstd, gain, shift, row(params_ref, mask + f))
            for n in range(2):
                out_ref[n, f, at : at + count] = pair[n].reshape(count, COLS, CH)
    for copy in copies[3:]:
        copy.wait()


def write_columns(store, table, fields_ref, at_fields, params_ref, stats_ref, rstd_at, turn, halo, masks):
    total = unpack_rows(table, clip_marks(params_ref, turn))
    rows = ROWS + 2 * halo
    column = iota(0, (rows * COLS, CH)) & (COLS - 1)
    for f in range(FRAMES):
        inverse = row(params_ref, TURN * turn + INV + f)
        avg_a = total[f][0:1] * inverse * row(stats_ref, rstd_at + f)
        avg_b = total[f][1:2] * inverse
        pieces = []
        for mask, at, count in ((masks[0], 0, halo), (masks[1], halo, ROWS), (masks[2], halo + ROWS, halo)):
            scaled = flat(fields_ref[at_fields + (0, f, slice(at, at + count))])
            normed = flat(fields_ref[at_fields + (1, f, slice(at, at + count))])
            pieces.append(scaled - avg_a * row(params_ref, mask + f) - normed * avg_b)
        value = jnp.concatenate(pieces, axis=0)
        left = jnp.where(column == COLS - 1, 0.0, pltpu.roll(value, rows * COLS - 1, 0))
        right = jnp.where(column == 0, 0.0, pltpu.roll(value, 1, 0))
        store(f, left.astype(BF16), value.astype(BF16), right.astype(BF16))


def store_columns(ref, prefix=()):
    def store(f, left, value, right):
        for n, x in enumerate((left, value, right)):
            ref[prefix + (f, slice(None), slice(n * CH, (n + 1) * CH))] = x

    return store


def conv_frame(columns, weight_ref, params_ref, turn, f, rows):
    total = None
    for kt in range(min(3, FRAMES - f)):
        part = None
        for dy in (-1, 0, 1):
            start = (1 - dy) * COLS
            term = jnp.dot(
                columns(f + kt, start, rows * COLS), weight_ref[3 * kt + dy + 1], preferred_element_type=F32
            )
            part = term if part is None else part + term
        if kt:
            part = part * row(params_ref, TURN * turn + (PAIR1 if kt == 1 else PAIR2) + f + kt)
        total = part if total is None else total + part
    return total.astype(BF16).reshape(rows, COLS, CH)


def conv_first_kernel(
    table_ref, fields_ref, params_ref, stats_ref, taps_ref, grad_ref, value_hbm, columns_ref, weight_ref, value_ref, sems
):
    (copy,) = copy_in([(taps_ref, weight_ref)], sems)
    table = jnp.sum(table_ref[...], axis=0)
    fill = store_columns(columns_ref)

    def store(f, left, value, right):
        fill(f, left, value, right)
        value_ref[f] = value[COLS : COLS * (ROWS + 3)].reshape(ROWS + 2, COLS, CH)

    write_columns(
        store, table, fields_ref, (), params_ref, stats_ref, RSTD0, 0, 2, (TOP, LIVE, BOTTOM)
    )
    value_out = pltpu.make_async_copy(value_ref, value_hbm, sems.at[1])
    value_out.start()
    copy.wait()
    for f in range(FRAMES):
        grad_ref[f] = conv_frame(
            lambda g, start, size: columns_ref[g, start : start + size], weight_ref, params_ref, 0, f, ROWS + 2
        )
    value_out.wait()


def put_acts(turn, bundle_ref, other_ref, params_ref, out_ref):
    for strip, ref in enumerate((bundle_ref, other_ref)):
        for f in range(FRAMES):
            x = flat(ref[f, 6 + ROWS * turn : 6 + ROWS * (turn + 1)].astype(F32)).T
            for kt in range(min(3, FRAMES - f)):
                at = CH * (2 * sum(FRAMES - n for n in range(kt)) + strip * (FRAMES - kt) + f)
                y = x if kt == 0 else x * row(params_ref, TURN * turn + (PAIR1 if kt == 1 else PAIR2) + f + kt)
                out_ref[:, at : at + CH] = y.astype(BF16)


def kernel_terms(columns_ref, act_ref, kt, dy):
    count = FRAMES - kt
    start = (1 - dy) * COLS
    columns = columns_ref[:, kt:FRAMES, start : start + ROWS * COLS, :].reshape(2 * count * CH, 3 * CH)
    at = 2 * CH * sum(FRAMES - n for n in range(kt))
    return jnp.dot(act_ref[:, at : at + 2 * count * CH], columns, preferred_element_type=F32)


def act_second_kernel(hand_ref, loss_ref, slope_ref, params_ref, stats_ref, out_ref, incoming_ref):
    gain = row(params_ref, GAIN)
    per_frame = []
    gain_part = row(stats_ref, GAIN_PART)
    shift_part = row(stats_ref, SHIFT_PART)
    for f in range(FRAMES):
        incoming = hand_ref[f].astype(F32) + loss_ref[f].astype(F32)
        incoming_ref[f] = incoming.astype(BF16)
        grad_act = flat(incoming[1 : 1 + ROWS]) * flat(slope_ref[0, f])
        live = row(params_ref, TURN + LIVE + f)
        plain = colsum(grad_act) * live
        times = colsum(grad_act * flat(slope_ref[1, f])) * live
        shift_part = shift_part + plain
        gain_part = gain_part + times
        per_frame.append(jnp.concatenate([plain * gain, times * gain], axis=0))
    rows = jnp.concatenate([pack_rows(per_frame), gain_part, shift_part], axis=0)
    out_ref[...] = jnp.broadcast_to(rows[None], out_ref.shape)


def weight_first_kernel(
    table_ref, params_ref, stats_ref, value_hbm, bundle_hbm, other_hbm,
    slope_ref, act_hbm, first_hbm,
    columns_ref, act_first_ref, act_ref, first_ref, value_ref, bundle_ref, other_ref, fields_ref, sems,
):
    copies = copy_in([(bundle_hbm, bundle_ref), (other_hbm, other_ref), (value_hbm, value_ref)], sems)
    table = jnp.sum(table_ref[...], axis=0)
    gain, shift = row(params_ref, GAIN), row(params_ref, SHIFT)
    copies[0].wait()
    for f in range(FRAMES):
        normed = flat(bundle_ref[f, 1 : 1 + ROWS].astype(F32)) - row(stats_ref, MEAN1 + f)
        normed = normed * row(stats_ref, RSTD1 + f)
        slope_ref[0, f] = act_slope(normed, gain, shift).reshape(ROWS, COLS, CH)
        slope_ref[1, f] = normed.reshape(ROWS, COLS, CH)
    copies[1].wait()
    put_acts(0, bundle_ref, other_ref, params_ref, act_first_ref)
    put_acts(1, bundle_ref, other_ref, params_ref, act_ref)
    acts_out = pltpu.make_async_copy(act_ref, act_hbm, sems.at[3])
    acts_out.start()
    for f in range(FRAMES):
        mean, rstd = row(stats_ref, MEAN0 + f), row(stats_ref, RSTD0 + f)
        for at, count, mask in ((0, 1, OTHER_TOP), (1, ROWS, LIVE), (1 + ROWS, 1, OTHER_BOTTOM)):
            pair = fields(
                other_ref[f, 14 + at : 14 + at + count], other_ref[f, 20 + at : 20 + at + count], mean, rstd,
                gain, shift, row(params_ref, mask + f),
            )
            for n in range(2):
                fields_ref[n, f, at : at + count] = pair[n].reshape(count, COLS, CH)
    write_columns(
        store_columns(columns_ref, (1,)), table, fields_ref, (), params_ref, stats_ref, RSTD0, 0, 1,
        (OTHER_TOP, LIVE, OTHER_BOTTOM),
    )
    copies[2].wait()
    rows = ROWS + 2
    column = iota(0, (rows * COLS, CH)) & (COLS - 1)
    fill = store_columns(columns_ref, (0,))
    for f in range(FRAMES):
        value = flat(value_ref[f].astype(F32))
        left = jnp.where(column == COLS - 1, 0.0, pltpu.roll(value, rows * COLS - 1, 0))
        right = jnp.where(column == 0, 0.0, pltpu.roll(value, 1, 0))
        fill(f, left.astype(BF16), value.astype(BF16), right.astype(BF16))
    for kt in range(3):
        for dy in (-1, 0, 1):
            terms = kernel_terms(columns_ref, act_first_ref, kt, dy)
            tap = 9 * kt + 3 * (dy + 1)
            for dx in range(3):
                first_ref[tap + dx] = terms[:, dx * CH : (dx + 1) * CH]
    first_out = pltpu.make_async_copy(first_ref, first_hbm, sems.at[4])
    first_out.start()
    acts_out.wait()
    first_out.wait()


def fields_second_kernel(
    incoming_ref, arrived_ref, bundle_hbm, other_hbm, params_ref, stats_ref, out_ref, bundle_ref, other_ref, sems,
):
    pre_part = slice(0, ROWS + 2)
    copies = copy_in(
        [(bundle_hbm.at[:, pre_part], bundle_ref), (other_hbm.at[:, pre_part], other_ref)], sems
    )
    for copy in copies:
        copy.wait()
    gain, shift = row(params_ref, GAIN), row(params_ref, SHIFT)
    for f in range(FRAMES):
        mean, rstd = row(stats_ref, MEAN1 + f), row(stats_ref, RSTD1 + f)
        for strip, pre_ref, come_ref, top, bottom in (
            (0, bundle_ref, incoming_ref, TURN + TOP, TURN + BOTTOM),
            (1, other_ref, arrived_ref, OTHER_TURN + OTHER_TOP, OTHER_TURN + OTHER_BOTTOM),
        ):
            for at, count, mask in ((0, 1, top), (1, ROWS, TURN + LIVE), (1 + ROWS, 1, bottom)):
                pair = fields(
                    pre_ref[f, at : at + count], come_ref[f, at : at + count], mean, rstd, gain, shift,
                    row(params_ref, mask + f),
                )
                for n in range(2):
                    out_ref[strip, n, f, at : at + count] = pair[n].reshape(count, COLS, CH)


def weight_second_kernel(
    scale, chunk, table_ref, fields_ref, params_ref, stats_ref, first_hbm, act_hbm,
    out_hbm, own_hbm, parts_ref, columns_ref, sum_ref, act_ref, first_ref, out_ref, sems,
):
    copies = copy_in([(act_hbm, act_ref), (first_hbm, first_ref)], sems)
    table = jnp.sum(table_ref[...], axis=0)
    parts_ref[...] = table[2:4] * scale
    for strip, top, bottom in ((0, TURN + TOP, TURN + BOTTOM), (1, OTHER_TURN + OTHER_TOP, OTHER_TURN + OTHER_BOTTOM)):
        write_columns(
            store_columns(columns_ref, (strip,)), table[0:2], fields_ref, (strip,), params_ref, stats_ref,
            RSTD1, 1, 1, (top, TURN + LIVE, bottom),
        )
    copy_own = pltpu.make_async_copy(columns_ref.at[0], own_hbm, sems.at[2])
    copy_own.start()
    for copy in copies:
        copy.wait()
    second = row(params_ref, CORE) > 0.5
    filler = jnp.zeros((out_ref.shape[1] - chunk, CH), F32)
    chips = out_ref.shape[0]
    done = 0
    copies = [copy_own]
    for kt in range(3):
        for dy in (-1, 0, 1):
            terms = kernel_terms(columns_ref, act_ref, kt, dy)
            tap = 9 * kt + 3 * (dy + 1)
            for dx in range(3):
                at = (tap + dx) * CH
                sum_ref[at : at + CH] = first_ref[tap + dx] + terms[:, dx * CH : (dx + 1) * CH]
        begin = done
        while done < chips and 2 * (done + 1) * chunk <= 9 * (kt + 1) * CH:
            at = 2 * done * chunk
            mine = jnp.where(second, sum_ref[at + chunk : at + 2 * chunk], sum_ref[at : at + chunk])
            if filler.shape[0]:
                mine = jnp.concatenate([mine, filler], axis=0)
            out_ref[done] = mine.astype(BF16)
            done += 1
        if done > begin:
            send = pltpu.make_async_copy(out_ref.at[begin:done], out_hbm.at[begin:done], sems.at[3 + kt])
            send.start()
            copies.append(send)
    for copy in copies:
        copy.wait()


def conv_second_kernel(params_ref, columns_hbm, first_hbm, taps_ref, out_ref, weight_ref, columns_ref, first_ref, sems):
    for copy in copy_in([(columns_hbm, columns_ref), (first_hbm, first_ref), (taps_ref, weight_ref)], sems):
        copy.wait()
    for f in range(FRAMES):
        out_ref[0, f] = first_ref[f, 1 : 1 + ROWS]
        out_ref[1, f] = conv_frame(
            lambda g, start, size: columns_ref[g, start : start + size], weight_ref, params_ref, 1, f, ROWS
        )


def total_kernel(scale, terms_ref, out_ref):
    chunk = out_ref.shape[0]
    total = jnp.sum(terms_ref[...].astype(F32), axis=0)
    out_ref[...] = (total[0:chunk] * scale).reshape(chunk, 1, CH)


def call(kernel, name, args, outs, scratch=(), specs="", flops=1_000_000):
    specs = specs or "v" * len(args)
    size = sum(a.size * a.dtype.itemsize for a in args)
    space = {"k": pltpu.VMEM, "h": pltpu.HBM}
    args = [pltpu.with_memory_space_constraint(a, space[x]) if x in space else a for a, x in zip(args, specs)]
    return pl.pallas_call(
        kernel,
        out_shape=tuple(outs),
        in_specs=[{"v": VMEM, "k": VMEM, "s": SMEM, "h": HBM}[x] for x in specs],
        out_specs=tuple(HBM if getattr(o, "memory_space", None) is pltpu.HBM else VMEM for o in outs),
        scratch_shapes=list(scratch),
        compiler_params=pltpu.CompilerParams(vmem_limit_bytes=24 * 1024 * 1024),
        cost_estimate=pl.CostEstimate(flops=flops, bytes_accessed=size, transcendentals=0),
        name=name,
    )(*args)


def shape(dims, dtype=F32):
    return jax.ShapeDtypeStruct(dims, dtype)


def kept(dims, dtype=F32):
    return pltpu.VMEM(dims, dtype)


def in_hbm(dims, dtype=F32):
    return pltpu.HBM(dims, dtype)


def local(activations, pre_norm, cot_first, loss_grad, frame_clip, weight, norm_gain, norm_shift):
    dp = lax.axis_size("dp")
    me = lax.axis_index("dp")
    cells = float(dp * ROWS * COLS * PER)
    chips, chunk = dp // 2, TAPS * CH // dp
    padded = -(-chunk // 8) * 8
    other = me ^ 1
    last = lax.axis_index("segment") == lax.axis_size("segment") - 1
    flags = [me != 0, me != dp - 1, other != 0, other != dp - 1, me & 1, last]
    flags = jnp.stack([x.astype(jnp.int32) for x in flags])
    pre, act = pre_norm[0], activations[0]
    cot, loss = cot_first[0], loss_grad[0]
    taps = weight[0].reshape(9, 3, CH, CH).transpose(0, 1, 3, 2).reshape(9, 3 * CH, CH)
    edge = (FRAMES, ROWS + 2, COLS, CH)
    strip = (FRAMES, ROWS, COLS, CH)
    bundled = (FRAMES, 3 * (ROWS + 2) + 2 * ROWS, COLS, CH)
    mates = [(i, i ^ 1) for i in range(dp)]
    columns_of = lambda rows: (FRAMES, rows * COLS, 3 * CH)
    sems = lambda n: pltpu.SemaphoreType.DMA((n,))

    def exchange(table):
        return lax.all_to_all(table, "dp", 0, 0, tiled=True)

    table, head, tail = call(
        sums_kernel, "sums", (pre, cot, loss), (shape((dp, 4, CH)), shape(edge, BF16), shape(edge, BF16)),
        scratch=[pltpu.VMEM((2,) + strip, BF16), sems(9)], specs="hhh",
    )
    table = exchange(table)
    down = lax.ppermute(head, "dp", [(i + 1, i) for i in range(dp - 1)])
    up = lax.ppermute(tail, "dp", [(i, i + 1) for i in range(dp - 1)])

    own, params = call(
        functools.partial(prepare_kernel, cells), "prepare", (flags, frame_clip, pre, cot, norm_gain, norm_shift),
        (kept((2,) + strip), kept((PARAM_ROWS, CH))),
        scratch=[
            pltpu.SMEM((1, 2, 1, FRAMES), jnp.int32), pltpu.VMEM((2,) + strip, BF16), pltpu.VMEM(strip, BF16), sems(5)
        ],
        specs="shhhhh",
    )
    table, stats = call(
        act_first_kernel, "act_first", (table, own, params), (shape((dp, 2, CH)), kept((STAT_ROWS, CH))), specs="vkk"
    )
    table = exchange(table)

    first_fields, bundle, loss_rows = call(
        fields_first_kernel, "fields_first", (up, down, params, stats, pre, cot, loss, act),
        (
            kept((2, FRAMES, ROWS + 4, COLS, CH)), in_hbm(bundled, BF16),
            kept(edge, BF16),
        ),
        scratch=[pltpu.VMEM(strip, BF16)] * 3 + [sems(14)],
        specs="vvkkhhhh",
    )
    other_bundle = lax.ppermute(bundle, "dp", mates)

    weights = pltpu.VMEM((9, 3 * CH, CH), BF16)
    grad_first, value = call(
        conv_first_kernel, "conv_first", (table, first_fields, params, stats, taps),
        (shape(edge, BF16), in_hbm(edge, BF16)),
        scratch=[pltpu.VMEM(columns_of(ROWS + 4), BF16), weights, pltpu.VMEM(edge, BF16), sems(2)],
        specs="vkkkh", flops=20_000_000_000,
    )
    count = lax.axis_size("segment")
    hand = lax.ppermute(grad_first, "segment", [(i + 1, i) for i in range(count - 1)])

    both = pltpu.VMEM((2,) + columns_of(ROWS + 2), BF16)
    acts_dims, taps_dims = (CH, 2 * 9 * CH), (TAPS, CH, CH)
    slope, acts, weight_first = call(
        weight_first_kernel, "weight_first", (table, params, stats, value, bundle, other_bundle),
        (kept((2,) + strip), in_hbm(acts_dims, BF16), in_hbm(taps_dims)),
        scratch=[both, pltpu.VMEM(acts_dims, BF16), pltpu.VMEM(acts_dims, BF16), pltpu.VMEM(taps_dims, F32)]
        + [pltpu.VMEM(edge, BF16)] + [pltpu.VMEM(bundled, BF16)] * 2 + [pltpu.VMEM((2,) + edge, F32), sems(5)],
        specs="vkkhhh",
    )

    table, incoming = call(
        act_second_kernel, "act_second", (hand, loss_rows, slope, params, stats),
        (shape((dp, 4, CH)), shape(edge, BF16)), specs="vkkkk",
    )
    table = exchange(table)
    arrived = lax.ppermute(incoming, "dp", mates)
    (second_fields,) = call(
        fields_second_kernel, "fields_second", (incoming, arrived, bundle, other_bundle, params, stats),
        (kept((2, 2) + edge),), scratch=[pltpu.VMEM(edge, BF16)] * 2 + [sems(2)], specs="vvhhkk",
    )

    terms, columns, parts = call(
        functools.partial(weight_second_kernel, 1.0 / dp, chunk), "weight_second",
        (table, second_fields, params, stats, weight_first, acts),
        (in_hbm((chips, padded, CH), BF16), in_hbm(columns_of(ROWS + 2), BF16), shape((2, CH))),
        scratch=[
            both, pltpu.VMEM((TAPS * CH, CH), F32), pltpu.VMEM(acts_dims, BF16), pltpu.VMEM(taps_dims, F32),
            pltpu.VMEM((chips, padded, CH), BF16), sems(6),
        ],
        specs="vkkkhh",
    )
    sides = [[2 * i + core for i in range(chips)] for core in range(2)]
    terms = lax.all_to_all(terms, "dp", 0, 0, axis_index_groups=sides, tiled=True)
    (grad_weight,) = call(
        functools.partial(total_kernel, 1.0 / dp), "total", (terms,), (shape((chunk, 1, CH)),)
    )
    (grad_inputs,) = call(
        conv_second_kernel, "conv_second", (params, columns, grad_first, taps),
        (shape((2, FRAMES, ROWS, COLS, CH), BF16),),
        scratch=[weights, pltpu.VMEM(columns_of(ROWS + 2), BF16), pltpu.VMEM(edge, BF16), sems(3)], specs="khhh",
    )
    width = CH // dp
    mine = lax.dynamic_slice_in_dim(parts, me * width, width, axis=1)
    return (grad_inputs[None], grad_weight.transpose(1, 0, 2), mine[0:1], mine[1:2])


def solution(mesh):
    in_specs = (
        P("segment", None, None, "dp", None, None),
        P("segment", None, None, "dp", None, None),
        P("segment", None, "dp", None, None),
        P(None, None, "dp", None, None),
        P("segment", None, "dp", None),
        P("segment", None, None),
        P("segment", None),
        P("segment", None),
    )
    out_specs = (
        P("segment", None, None, "dp", None, None),
        P("segment", "dp", None),
        P("segment", "dp"),
        P("segment", "dp"),
    )
    return jax.shard_map(local, mesh=mesh, in_specs=in_specs, out_specs=out_specs, check_vma=False)
```

```python
import functools
import jax
import jax.numpy as jnp
from jax import lax
from jax.experimental import pallas as pl
from jax.experimental.pallas import tpu as pltpu
from jax.sharding import PartitionSpec as P

F32, BF16 = jnp.float32, jnp.bfloat16
FRAMES, ROWS, COLS, CH = 4, 4, 32, 128
GROUPS, PER = 32, 4
TAPS = 27
EPS = 1e-05
VMEM = pl.BlockSpec(memory_space=pltpu.VMEM)
SMEM = pl.BlockSpec(memory_space=pltpu.SMEM)
HBM = pl.BlockSpec(memory_space=pltpu.HBM)

GAIN, SHIFT, CORE, LAST = 0, 1, 2, 3
TURN = 24
INV, LIVE, TOP, BOTTOM, PAIR1, PAIR2 = (8 + 4 * n for n in range(6))
OTHER_TOP, OTHER_BOTTOM = 56, 60
CLIPS = 64
OTHER_TURN = 16
PARAM_ROWS = 80
MEAN0, RSTD0, MEAN1, RSTD1, GAIN_PART, SHIFT_PART = 0, 4, 8, 12, 16, 17
STAT_ROWS = 24


def iota(dim, dims=(CH, CH)):
    return lax.broadcasted_iota(jnp.int32, dims, dim)


def split_dot(rows, marks):
    count = rows.shape[0]
    high = rows.astype(BF16)
    rest = rows - high.astype(F32)
    middle = rest.astype(BF16)
    low = (rest - middle.astype(F32)).astype(BF16)
    out = jnp.dot(
        jnp.concatenate([high.astype(F32), middle.astype(F32), low.astype(F32)], axis=0).astype(BF16),
        marks,
        preferred_element_type=F32,
    )
    return out[0:count] + out[count : 2 * count] + out[2 * count : 3 * count]


def pack_rows(per_frame):
    rows = jnp.concatenate(per_frame, axis=1)
    dims = (FRAMES * CH, CH)
    marks = (iota(1, dims) == (iota(0, dims) >> 2)).astype(F32).astype(BF16)
    return split_dot(rows, marks)


def unpack_rows(table, marks):
    total = split_dot(table, marks)
    return [total[:, f * CH : (f + 1) * CH] for f in range(FRAMES)]


def row(ref, at):
    return ref[at : at + 1]


def colsum(x):
    return jnp.sum(x, axis=0, keepdims=True)


def flat(x):
    return x.reshape(-1, CH)


def act_slope(normed, gain, shift):
    act = normed * gain + shift
    sigm = jax.nn.sigmoid(act)
    return sigm * (1.0 + act * (1.0 - sigm))


def copy_in(pairs, sems):
    copies = [pltpu.make_async_copy(src, dst, sems.at[n]) for n, (src, dst) in enumerate(pairs)]
    for copy in copies:
        copy.start()
    return copies


def sums_kernel(pre_ref, cot_ref, loss_ref, out_ref, head_ref, tail_ref, held_ref, sems):
    pairs = [(pre_ref, held_ref)]
    for ref, two, one in ((head_ref, 0, 0), (tail_ref, ROWS - 2, ROWS - 1)):
        pairs += [
            (pre_ref.at[0, :, two : two + 2], ref.at[:, 0:2]),
            (cot_ref.at[:, two : two + 2], ref.at[:, 2:4]),
            (pre_ref.at[1, :, one : one + 1], ref.at[:, 4:5]),
            (loss_ref.at[:, one : one + 1], ref.at[:, 5:6]),
        ]
    copies = copy_in(pairs, sems)
    copies[0].wait()
    per_frame = []
    for f in range(FRAMES):
        rows = []
        for t in range(2):
            x = flat(held_ref[t, f].astype(F32))
            rows += [colsum(x), colsum(x * x)]
        per_frame.append(jnp.concatenate(rows, axis=0))
    out_ref[...] = jnp.broadcast_to(pack_rows(per_frame)[None], out_ref.shape)
    for copy in copies[1:]:
        copy.wait()


def clip_marks(params_ref, turn):
    slot = iota(0) >> 5
    clips = [row(params_ref, CLIPS + FRAMES * turn + f) for f in range(FRAMES)]
    clip_of_row = jnp.where(
        slot == 0, clips[0], jnp.where(slot == 1, clips[1], jnp.where(slot == 2, clips[2], clips[3]))
    )
    same_group = (iota(0) & (GROUPS - 1)) == (iota(1) >> 2)
    blocks = [(same_group & (clip_of_row == clips[f])).astype(F32).astype(BF16) for f in range(FRAMES)]
    return jnp.concatenate(blocks, axis=1)


def prepare_kernel(
    cells, flag_ref, clip_hbm, pre_ref, cot_ref, gain_ref, shift_ref,
    own_ref, params_ref, clip_ref, held_pre, held_cot, sems,
):
    copies = copy_in(
        [
            (clip_hbm, clip_ref), (pre_ref, held_pre), (cot_ref, held_cot),
            (gain_ref, params_ref.at[GAIN : GAIN + 1]), (shift_ref, params_ref.at[SHIFT : SHIFT + 1]),
        ],
        sems,
    )

    def put(at, scalar):
        params_ref[at : at + 1] = jnp.full((1, CH), scalar, F32)

    put(CORE, flag_ref[4].astype(F32))
    put(LAST, flag_ref[5].astype(F32))
    params_ref[LAST + 1 : INV] = jnp.zeros((INV - LAST - 1, CH), F32)
    flag = [flag_ref[n].astype(F32) for n in range(4)]
    copies[0].wait()
    for t in range(2):
        clips = [clip_ref[0, t, 0, f] for f in range(FRAMES)]
        for f in range(FRAMES):
            count = jnp.int32(0)
            for other in range(FRAMES):
                count = count + (clips[other] == clips[f]).astype(jnp.int32)
            live = (clips[f] < FRAMES).astype(F32)
            base = TURN * t + f
            params_ref[base + INV : base + INV + 1] = 1.0 / jnp.full((1, CH), count.astype(F32) * cells, F32)
            put(base + LIVE, live)
            put(base + TOP, live * flag[0])
            put(base + BOTTOM, live * flag[1])
            put(CLIPS + FRAMES * t + f, clips[f].astype(F32))
            for kt, at in ((1, PAIR1), (2, PAIR2)):
                pair = live * (clips[f - kt] == clips[f]).astype(F32) if f >= kt else live * 0.0
                put(base + at, pair)
            put(OTHER_TURN * t + OTHER_TOP + f, live * flag[2])
            put(OTHER_TURN * t + OTHER_BOTTOM + f, live * flag[3])
    for copy in copies[1:]:
        copy.wait()
    own_ref[0] = held_pre[0].astype(F32)
    own_ref[1] = held_cot[...].astype(F32)


def act_first_kernel(table_ref, own_ref, params_ref, out_ref, stats_ref):
    table = jnp.sum(table_ref[...], axis=0)
    gain, shift = row(params_ref, GAIN), row(params_ref, SHIFT)
    for t, mean_at, rstd_at in ((0, MEAN0, RSTD0), (1, MEAN1, RSTD1)):
        total = unpack_rows(table[2 * t : 2 * t + 2], clip_marks(params_ref, t))
        for f in range(FRAMES):
            inverse = row(params_ref, TURN * t + INV + f)
            mean = total[f][0:1] * inverse
            var = total[f][1:2] * inverse - mean * mean
            stats_ref[mean_at + f : mean_at + f + 1] = mean
            stats_ref[rstd_at + f : rstd_at + f + 1] = 1.0 / jnp.sqrt(var + EPS)
    per_frame = []
    gain_part = jnp.zeros((1, CH), F32)
    shift_part = jnp.zeros((1, CH), F32)
    for f in range(FRAMES):
        normed = (flat(own_ref[0, f]) - row(stats_ref, MEAN0 + f)) * row(stats_ref, RSTD0 + f)
        grad_act = flat(own_ref[1, f]) * act_slope(normed, gain, shift)
        live = row(params_ref, LIVE + f)
        plain = colsum(grad_act) * live
        times = colsum(grad_act * normed) * live
        shift_part = shift_part + plain
        gain_part = gain_part + times
        per_frame.append(jnp.concatenate([plain * gain, times * gain], axis=0))
    stats_ref[GAIN_PART : GAIN_PART + 1] = gain_part
    stats_ref[SHIFT_PART : SHIFT_PART + 1] = shift_part
    stats_ref[SHIFT_PART + 1 :] = jnp.zeros((STAT_ROWS - SHIFT_PART - 1, CH), F32)
    out_ref[...] = jnp.broadcast_to(pack_rows(per_frame)[None], out_ref.shape)


def fields(pre, incoming, mean, rstd, gain, shift, mask):
    normed = (flat(pre.astype(F32)) - mean) * rstd
    scaled = flat(incoming.astype(F32)) * act_slope(normed, gain, shift) * gain
    rstd = rstd * mask
    return scaled * rstd, normed * rstd


def fields_first_kernel(
    up_ref, down_ref, params_ref, stats_ref, pre_ref, cot_ref, loss_ref, act_ref,
    out_ref, bundle_hbm, loss_out_ref, bundle_ref, held_loss, sems,
):
    copies = copy_in(
        [
            (pre_ref.at[0], bundle_ref.at[:, 15 : 15 + ROWS]), (cot_ref, bundle_ref.at[:, 21 : 21 + ROWS]),
            (loss_ref, held_loss), (pre_ref.at[1], bundle_ref.at[:, 1 : 1 + ROWS]),
            (act_ref.at[0], bundle_ref.at[:, 6 : 6 + ROWS]),
            (act_ref.at[1], bundle_ref.at[:, 6 + ROWS : 6 + 2 * ROWS]),
        ],
        sems,
    )
    for at, edge, below in ((0, 4, 4), (14, 1, 0), (20, 3, 2)):
        bundle_ref[:, at : at + 1] = up_ref[:, edge : edge + 1]
        bundle_ref[:, at + 1 + ROWS : at + 2 + ROWS] = down_ref[:, below : below + 1]
    for copy in copies:
        copy.wait()
    bundle_out = pltpu.make_async_copy(bundle_ref, bundle_hbm, sems.at[6])
    bundle_out.start()
    gain, shift = row(params_ref, GAIN), row(params_ref, SHIFT)
    last = row(params_ref, LAST).reshape(1, 1, 1, CH)
    loss_out_ref[:, 0:1] = (up_ref[:, 5:6].astype(F32) * last).astype(BF16)
    loss_out_ref[:, 1 : 1 + ROWS] = (held_loss[...].astype(F32) * last).astype(BF16)
    loss_out_ref[:, 1 + ROWS : 2 + ROWS] = (down_ref[:, 5:6].astype(F32) * last).astype(BF16)
    for f in range(FRAMES):
        mean, rstd = row(stats_ref, MEAN0 + f), row(stats_ref, RSTD0 + f)
        for at, count, pre, cot, mask in (
            (0, 2, up_ref[f, 0:2], up_ref[f, 2:4], TOP),
            (2, ROWS, bundle_ref[f, 15 : 15 + ROWS], bundle_ref[f, 21 : 21 + ROWS], LIVE),
            (2 + ROWS, 2, down_ref[f, 0:2], down_ref[f, 2:4], BOTTOM),
        ):
            pair = fields(pre, cot, mean, rstd, gain, shift, row(params_ref, mask + f))
            for n in range(2):
                out_ref[n, f, at : at + count] = pair[n].reshape(count, COLS, CH)
    bundle_out.wait()


def write_columns(store, table, fields_ref, at_fields, params_ref, stats_ref, rstd_at, turn, halo, masks):
    total = unpack_rows(table, clip_marks(params_ref, turn))
    rows = ROWS + 2 * halo
    column = iota(0, (rows * COLS, CH)) & (COLS - 1)
    for f in range(FRAMES):
        inverse = row(params_ref, TURN * turn + INV + f)
        avg_a = total[f][0:1] * inverse * row(stats_ref, rstd_at + f)
        avg_b = total[f][1:2] * inverse
        pieces = []
        for mask, at, count in ((masks[0], 0, halo), (masks[1], halo, ROWS), (masks[2], halo + ROWS, halo)):
            scaled = flat(fields_ref[at_fields + (0, f, slice(at, at + count))])
            normed = flat(fields_ref[at_fields + (1, f, slice(at, at + count))])
            pieces.append(scaled - avg_a * row(params_ref, mask + f) - normed * avg_b)
        value = jnp.concatenate(pieces, axis=0)
        left = jnp.where(column == COLS - 1, 0.0, pltpu.roll(value, rows * COLS - 1, 0))
        right = jnp.where(column == 0, 0.0, pltpu.roll(value, 1, 0))
        store(f, left.astype(BF16), value.astype(BF16), right.astype(BF16))


def store_columns(ref, prefix=()):
    def store(f, left, value, right):
        for n, x in enumerate((left, value, right)):
            ref[prefix + (f, slice(None), slice(n * CH, (n + 1) * CH))] = x

    return store


def conv_frame(columns, weight_ref, params_ref, turn, f, rows):
    total = None
    for kt in range(min(3, FRAMES - f)):
        part = None
        for dy in (-1, 0, 1):
            start = (1 - dy) * COLS
            term = jnp.dot(
                columns(f + kt, start, rows * COLS), weight_ref[3 * kt + dy + 1], preferred_element_type=F32
            )
            part = term if part is None else part + term
        if kt:
            part = part * row(params_ref, TURN * turn + (PAIR1 if kt == 1 else PAIR2) + f + kt)
        total = part if total is None else total + part
    return total.astype(BF16).reshape(rows, COLS, CH)


def conv_first_kernel(
    table_ref, fields_ref, params_ref, stats_ref, taps_ref, grad_ref, value_hbm, columns_ref, weight_ref, value_ref, sems
):
    (copy,) = copy_in([(taps_ref, weight_ref)], sems)
    table = jnp.sum(table_ref[...], axis=0)
    fill = store_columns(columns_ref)

    def store(f, left, value, right):
        fill(f, left, value, right)
        value_ref[f] = value[COLS : COLS * (ROWS + 3)].reshape(ROWS + 2, COLS, CH)

    write_columns(
        store, table, fields_ref, (), params_ref, stats_ref, RSTD0, 0, 2, (TOP, LIVE, BOTTOM)
    )
    value_out = pltpu.make_async_copy(value_ref, value_hbm, sems.at[1])
    value_out.start()
    copy.wait()
    for f in range(FRAMES):
        grad_ref[f] = conv_frame(
            lambda g, start, size: columns_ref[g, start : start + size], weight_ref, params_ref, 0, f, ROWS + 2
        )
    value_out.wait()


def put_acts(turn, bundle_ref, other_ref, params_ref, out_ref):
    for strip, ref in enumerate((bundle_ref, other_ref)):
        for f in range(FRAMES):
            x = flat(ref[f, 6 + ROWS * turn : 6 + ROWS * (turn + 1)].astype(F32)).T
            for kt in range(min(3, FRAMES - f)):
                at = CH * (2 * sum(FRAMES - n for n in range(kt)) + strip * (FRAMES - kt) + f)
                y = x if kt == 0 else x * row(params_ref, TURN * turn + (PAIR1 if kt == 1 else PAIR2) + f + kt)
                out_ref[:, at : at + CH] = y.astype(BF16)


def kernel_terms(columns_ref, act_ref, kt, dy):
    count = FRAMES - kt
    start = (1 - dy) * COLS
    columns = columns_ref[:, kt:FRAMES, start : start + ROWS * COLS, :].reshape(2 * count * CH, 3 * CH)
    at = 2 * CH * sum(FRAMES - n for n in range(kt))
    return jnp.dot(act_ref[:, at : at + 2 * count * CH], columns, preferred_element_type=F32)


def act_second_kernel(hand_ref, loss_ref, slope_ref, params_ref, stats_ref, out_ref, incoming_ref):
    gain = row(params_ref, GAIN)
    per_frame = []
    gain_part = row(stats_ref, GAIN_PART)
    shift_part = row(stats_ref, SHIFT_PART)
    for f in range(FRAMES):
        incoming = hand_ref[f].astype(F32) + loss_ref[f].astype(F32)
        incoming_ref[f] = incoming.astype(BF16)
        grad_act = flat(incoming[1 : 1 + ROWS]) * flat(slope_ref[0, f])
        live = row(params_ref, TURN + LIVE + f)
        plain = colsum(grad_act) * live
        times = colsum(grad_act * flat(slope_ref[1, f])) * live
        shift_part = shift_part + plain
        gain_part = gain_part + times
        per_frame.append(jnp.concatenate([plain * gain, times * gain], axis=0))
    rows = jnp.concatenate([pack_rows(per_frame), gain_part, shift_part], axis=0)
    out_ref[...] = jnp.broadcast_to(rows[None], out_ref.shape)


def weight_first_kernel(
    table_ref, params_ref, stats_ref, value_hbm, bundle_hbm, other_hbm,
    slope_ref, act_hbm, first_hbm,
    columns_ref, act_first_ref, act_ref, first_ref, value_ref, bundle_ref, other_ref, fields_ref, sems,
):
    copies = copy_in([(bundle_hbm, bundle_ref), (other_hbm, other_ref), (value_hbm, value_ref)], sems)
    table = jnp.sum(table_ref[...], axis=0)
    gain, shift = row(params_ref, GAIN), row(params_ref, SHIFT)
    copies[0].wait()
    for f in range(FRAMES):
        normed = flat(bundle_ref[f, 1 : 1 + ROWS].astype(F32)) - row(stats_ref, MEAN1 + f)
        normed = normed * row(stats_ref, RSTD1 + f)
        slope_ref[0, f] = act_slope(normed, gain, shift).reshape(ROWS, COLS, CH)
        slope_ref[1, f] = normed.reshape(ROWS, COLS, CH)
    copies[1].wait()
    put_acts(0, bundle_ref, other_ref, params_ref, act_first_ref)
    put_acts(1, bundle_ref, other_ref, params_ref, act_ref)
    acts_out = pltpu.make_async_copy(act_ref, act_hbm, sems.at[3])
    acts_out.start()
    for f in range(FRAMES):
        mean, rstd = row(stats_ref, MEAN0 + f), row(stats_ref, RSTD0 + f)
        for at, count, mask in ((0, 1, OTHER_TOP), (1, ROWS, LIVE), (1 + ROWS, 1, OTHER_BOTTOM)):
            pair = fields(
                other_ref[f, 14 + at : 14 + at + count], other_ref[f, 20 + at : 20 + at + count], mean, rstd,
                gain, shift, row(params_ref, mask + f),
            )
            for n in range(2):
                fields_ref[n, f, at : at + count] = pair[n].reshape(count, COLS, CH)
    write_columns(
        store_columns(columns_ref, (1,)), table, fields_ref, (), params_ref, stats_ref, RSTD0, 0, 1,
        (OTHER_TOP, LIVE, OTHER_BOTTOM),
    )
    copies[2].wait()
    rows = ROWS + 2
    column = iota(0, (rows * COLS, CH)) & (COLS - 1)
    fill = store_columns(columns_ref, (0,))
    for f in range(FRAMES):
        value = flat(value_ref[f].astype(F32))
        left = jnp.where(column == COLS - 1, 0.0, pltpu.roll(value, rows * COLS - 1, 0))
        right = jnp.where(column == 0, 0.0, pltpu.roll(value, 1, 0))
        fill(f, left.astype(BF16), value.astype(BF16), right.astype(BF16))
    for kt in range(3):
        for dy in (-1, 0, 1):
            terms = kernel_terms(columns_ref, act_first_ref, kt, dy)
            tap = 9 * kt + 3 * (dy + 1)
            for dx in range(3):
                first_ref[tap + dx] = terms[:, dx * CH : (dx + 1) * CH]
    first_out = pltpu.make_async_copy(first_ref, first_hbm, sems.at[4])
    first_out.start()
    acts_out.wait()
    first_out.wait()


def fields_second_kernel(
    incoming_ref, arrived_ref, bundle_hbm, other_hbm, params_ref, stats_ref, out_ref, bundle_ref, other_ref, sems,
):
    pre_part = slice(0, ROWS + 2)
    copies = copy_in(
        [(bundle_hbm.at[:, pre_part], bundle_ref), (other_hbm.at[:, pre_part], other_ref)], sems
    )
    for copy in copies:
        copy.wait()
    gain, shift = row(params_ref, GAIN), row(params_ref, SHIFT)
    for f in range(FRAMES):
        mean, rstd = row(stats_ref, MEAN1 + f), row(stats_ref, RSTD1 + f)
        for strip, pre_ref, come_ref, top, bottom in (
            (0, bundle_ref, incoming_ref, TURN + TOP, TURN + BOTTOM),
            (1, other_ref, arrived_ref, OTHER_TURN + OTHER_TOP, OTHER_TURN + OTHER_BOTTOM),
        ):
            for at, count, mask in ((0, 1, top), (1, ROWS, TURN + LIVE), (1 + ROWS, 1, bottom)):
                pair = fields(
                    pre_ref[f, at : at + count], come_ref[f, at : at + count], mean, rstd, gain, shift,
                    row(params_ref, mask + f),
                )
                for n in range(2):
                    out_ref[strip, n, f, at : at + count] = pair[n].reshape(count, COLS, CH)


def weight_second_kernel(
    scale, chunk, table_ref, fields_ref, params_ref, stats_ref, first_hbm, act_hbm,
    out_hbm, own_hbm, parts_ref, columns_ref, sum_ref, act_ref, first_ref, out_ref, sems,
):
    copies = copy_in([(act_hbm, act_ref), (first_hbm, first_ref)], sems)
    table = jnp.sum(table_ref[...], axis=0)
    parts_ref[...] = table[2:4] * scale
    for strip, top, bottom in ((0, TURN + TOP, TURN + BOTTOM), (1, OTHER_TURN + OTHER_TOP, OTHER_TURN + OTHER_BOTTOM)):
        write_columns(
            store_columns(columns_ref, (strip,)), table[0:2], fields_ref, (strip,), params_ref, stats_ref,
            RSTD1, 1, 1, (top, TURN + LIVE, bottom),
        )
    copy_own = pltpu.make_async_copy(columns_ref.at[0], own_hbm, sems.at[2])
    copy_own.start()
    for copy in copies:
        copy.wait()
    second = row(params_ref, CORE) > 0.5
    filler = jnp.zeros((out_ref.shape[1] - chunk, CH), F32)
    chips = out_ref.shape[0]
    done = 0
    copies = [copy_own]
    for kt in range(3):
        for dy in (-1, 0, 1):
            terms = kernel_terms(columns_ref, act_ref, kt, dy)
            tap = 9 * kt + 3 * (dy + 1)
            for dx in range(3):
                at = (tap + dx) * CH
                sum_ref[at : at + CH] = first_ref[tap + dx] + terms[:, dx * CH : (dx + 1) * CH]
        begin = done
        while done < chips and 2 * (done + 1) * chunk <= 9 * (kt + 1) * CH:
            at = 2 * done * chunk
            mine = jnp.where(second, sum_ref[at + chunk : at + 2 * chunk], sum_ref[at : at + chunk])
            if filler.shape[0]:
                mine = jnp.concatenate([mine, filler], axis=0)
            out_ref[done] = mine.astype(BF16)
            done += 1
        if done > begin:
            send = pltpu.make_async_copy(out_ref.at[begin:done], out_hbm.at[begin:done], sems.at[3 + kt])
            send.start()
            copies.append(send)
    for copy in copies:
        copy.wait()


def conv_second_kernel(params_ref, columns_hbm, first_hbm, taps_ref, out_ref, weight_ref, columns_ref, first_ref, sems):
    for copy in copy_in([(columns_hbm, columns_ref), (first_hbm, first_ref), (taps_ref, weight_ref)], sems):
        copy.wait()
    for f in range(FRAMES):
        out_ref[0, f] = first_ref[f, 1 : 1 + ROWS]
        out_ref[1, f] = conv_frame(
            lambda g, start, size: columns_ref[g, start : start + size], weight_ref, params_ref, 1, f, ROWS
        )


def total_kernel(scale, terms_ref, out_ref):
    chunk = out_ref.shape[0]
    total = jnp.sum(terms_ref[...].astype(F32), axis=0)
    out_ref[...] = (total[0:chunk] * scale).reshape(chunk, 1, CH)


def call(kernel, name, args, outs, scratch=(), specs="", flops=1_000_000):
    specs = specs or "v" * len(args)
    size = sum(a.size * a.dtype.itemsize for a in args)
    space = {"k": pltpu.VMEM, "h": pltpu.HBM}
    args = [pltpu.with_memory_space_constraint(a, space[x]) if x in space else a for a, x in zip(args, specs)]
    return pl.pallas_call(
        kernel,
        out_shape=tuple(outs),
        in_specs=[{"v": VMEM, "k": VMEM, "s": SMEM, "h": HBM}[x] for x in specs],
        out_specs=tuple(HBM if getattr(o, "memory_space", None) is pltpu.HBM else VMEM for o in outs),
        scratch_shapes=list(scratch),
        compiler_params=pltpu.CompilerParams(vmem_limit_bytes=24 * 1024 * 1024),
        cost_estimate=pl.CostEstimate(flops=flops, bytes_accessed=size, transcendentals=0),
        name=name,
    )(*args)


def shape(dims, dtype=F32):
    return jax.ShapeDtypeStruct(dims, dtype)


def kept(dims, dtype=F32):
    return pltpu.VMEM(dims, dtype)


def in_hbm(dims, dtype=F32):
    return pltpu.HBM(dims, dtype)


def local(activations, pre_norm, cot_first, loss_grad, frame_clip, weight, norm_gain, norm_shift):
    dp = lax.axis_size("dp")
    me = lax.axis_index("dp")
    cells = float(dp * ROWS * COLS * PER)
    chips, chunk = dp // 2, TAPS * CH // dp
    padded = -(-chunk // 8) * 8
    other = me ^ 1
    last = lax.axis_index("segment") == lax.axis_size("segment") - 1
    flags = [me != 0, me != dp - 1, other != 0, other != dp - 1, me & 1, last]
    flags = jnp.stack([x.astype(jnp.int32) for x in flags])
    pre, act = pre_norm[0], activations[0]
    cot, loss = cot_first[0], loss_grad[0]
    taps = weight[0].reshape(9, 3, CH, CH).transpose(0, 1, 3, 2).reshape(9, 3 * CH, CH)
    edge = (FRAMES, ROWS + 2, COLS, CH)
    strip = (FRAMES, ROWS, COLS, CH)
    bundled = (FRAMES, 3 * (ROWS + 2) + 2 * ROWS, COLS, CH)
    mates = [(i, i ^ 1) for i in range(dp)]
    columns_of = lambda rows: (FRAMES, rows * COLS, 3 * CH)
    sems = lambda n: pltpu.SemaphoreType.DMA((n,))

    def exchange(table):
        return lax.all_to_all(table, "dp", 0, 0, tiled=True)

    table, head, tail = call(
        sums_kernel, "sums", (pre, cot, loss), (shape((dp, 4, CH)), shape(edge, BF16), shape(edge, BF16)),
        scratch=[pltpu.VMEM((2,) + strip, BF16), sems(9)], specs="hhh",
    )
    table = exchange(table)
    down = lax.ppermute(head, "dp", [(i + 1, i) for i in range(dp - 1)])
    up = lax.ppermute(tail, "dp", [(i, i + 1) for i in range(dp - 1)])

    own, params = call(
        functools.partial(prepare_kernel, cells), "prepare", (flags, frame_clip, pre, cot, norm_gain, norm_shift),
        (kept((2,) + strip), kept((PARAM_ROWS, CH))),
        scratch=[
            pltpu.SMEM((1, 2, 1, FRAMES), jnp.int32), pltpu.VMEM((2,) + strip, BF16), pltpu.VMEM(strip, BF16), sems(5)
        ],
        specs="shhhhh",
    )
    table, stats = call(
        act_first_kernel, "act_first", (table, own, params), (shape((dp, 2, CH)), kept((STAT_ROWS, CH))), specs="vkk"
    )
    table = exchange(table)

    first_fields, bundle, loss_rows = call(
        fields_first_kernel, "fields_first", (up, down, params, stats, pre, cot, loss, act),
        (
            kept((2, FRAMES, ROWS + 4, COLS, CH)), in_hbm(bundled, BF16),
            kept(edge, BF16),
        ),
        scratch=[pltpu.VMEM(bundled, BF16), pltpu.VMEM(strip, BF16), sems(7)],
        specs="vvkkhhhh",
    )
    other_bundle = lax.ppermute(bundle, "dp", mates)

    weights = pltpu.VMEM((9, 3 * CH, CH), BF16)
    grad_first, value = call(
        conv_first_kernel, "conv_first", (table, first_fields, params, stats, taps),
        (shape(edge, BF16), in_hbm(edge, BF16)),
        scratch=[pltpu.VMEM(columns_of(ROWS + 4), BF16), weights, pltpu.VMEM(edge, BF16), sems(2)],
        specs="vkkkh", flops=20_000_000_000,
    )
    count = lax.axis_size("segment")
    hand = lax.ppermute(grad_first, "segment", [(i + 1, i) for i in range(count - 1)])

    both = pltpu.VMEM((2,) + columns_of(ROWS + 2), BF16)
    acts_dims, taps_dims = (CH, 2 * 9 * CH), (TAPS, CH, CH)
    slope, acts, weight_first = call(
        weight_first_kernel, "weight_first", (table, params, stats, value, bundle, other_bundle),
        (kept((2,) + strip), in_hbm(acts_dims, BF16), in_hbm(taps_dims)),
        scratch=[both, pltpu.VMEM(acts_dims, BF16), pltpu.VMEM(acts_dims, BF16), pltpu.VMEM(taps_dims, F32)]
        + [pltpu.VMEM(edge, BF16)] + [pltpu.VMEM(bundled, BF16)] * 2 + [pltpu.VMEM((2,) + edge, F32), sems(5)],
        specs="vkkhhh",
    )

    table, incoming = call(
        act_second_kernel, "act_second", (hand, loss_rows, slope, params, stats),
        (shape((dp, 4, CH)), shape(edge, BF16)), specs="vkkkk",
    )
    table = exchange(table)
    arrived = lax.ppermute(incoming, "dp", mates)
    (second_fields,) = call(
        fields_second_kernel, "fields_second", (incoming, arrived, bundle, other_bundle, params, stats),
        (kept((2, 2) + edge),), scratch=[pltpu.VMEM(edge, BF16)] * 2 + [sems(2)], specs="vvhhkk",
    )

    terms, columns, parts = call(
        functools.partial(weight_second_kernel, 1.0 / dp, chunk), "weight_second",
        (table, second_fields, params, stats, weight_first, acts),
        (in_hbm((chips, padded, CH), BF16), in_hbm(columns_of(ROWS + 2), BF16), shape((2, CH))),
        scratch=[
            both, pltpu.VMEM((TAPS * CH, CH), F32), pltpu.VMEM(acts_dims, BF16), pltpu.VMEM(taps_dims, F32),
            pltpu.VMEM((chips, padded, CH), BF16), sems(6),
        ],
        specs="vkkkhh",
    )
    sides = [[2 * i + core for i in range(chips)] for core in range(2)]
    terms = lax.all_to_all(terms, "dp", 0, 0, axis_index_groups=sides, tiled=True)
    (grad_weight,) = call(
        functools.partial(total_kernel, 1.0 / dp), "total", (terms,), (shape((chunk, 1, CH)),)
    )
    (grad_inputs,) = call(
        conv_second_kernel, "conv_second", (params, columns, grad_first, taps),
        (shape((2, FRAMES, ROWS, COLS, CH), BF16),),
        scratch=[weights, pltpu.VMEM(columns_of(ROWS + 2), BF16), pltpu.VMEM(edge, BF16), sems(3)], specs="khhh",
    )
    width = CH // dp
    mine = lax.dynamic_slice_in_dim(parts, me * width, width, axis=1)
    return (grad_inputs[None], grad_weight.transpose(1, 0, 2), mine[0:1], mine[1:2])


def solution(mesh):
    in_specs = (
        P("segment", None, None, "dp", None, None),
        P("segment", None, None, "dp", None, None),
        P("segment", None, "dp", None, None),
        P(None, None, "dp", None, None),
        P("segment", None, "dp", None),
        P("segment", None, None),
        P("segment", None),
        P("segment", None),
    )
    out_specs = (
        P("segment", None, None, "dp", None, None),
        P("segment", "dp", None),
        P("segment", "dp"),
        P("segment", "dp"),
    )
    return jax.shard_map(local, mesh=mesh, in_specs=in_specs, out_specs=out_specs, check_vma=False)
```

```python
import functools
import jax
import jax.numpy as jnp
from jax import lax
from jax.experimental import pallas as pl
from jax.experimental.pallas import tpu as pltpu
from jax.sharding import PartitionSpec as P

F32, BF16 = jnp.float32, jnp.bfloat16
FRAMES, ROWS, COLS, CH = 4, 4, 32, 128
GROUPS, PER = 32, 4
TAPS = 27
EPS = 1e-05
VMEM = pl.BlockSpec(memory_space=pltpu.VMEM)
SMEM = pl.BlockSpec(memory_space=pltpu.SMEM)
HBM = pl.BlockSpec(memory_space=pltpu.HBM)

GAIN, SHIFT, CORE, LAST = 0, 1, 2, 3
TURN = 24
INV, LIVE, TOP, BOTTOM, PAIR1, PAIR2 = (8 + 4 * n for n in range(6))
OTHER_TOP, OTHER_BOTTOM = 56, 60
CLIPS = 64
OTHER_TURN = 16
PARAM_ROWS = 80
MEAN0, RSTD0, MEAN1, RSTD1, GAIN_PART, SHIFT_PART = 0, 4, 8, 12, 16, 17
STAT_ROWS = 24


def iota(dim, dims=(CH, CH)):
    return lax.broadcasted_iota(jnp.int32, dims, dim)


def split_dot(rows, marks):
    count = rows.shape[0]
    high = rows.astype(BF16)
    rest = rows - high.astype(F32)
    middle = rest.astype(BF16)
    low = (rest - middle.astype(F32)).astype(BF16)
    out = jnp.dot(
        jnp.concatenate([high.astype(F32), middle.astype(F32), low.astype(F32)], axis=0).astype(BF16),
        marks,
        preferred_element_type=F32,
    )
    return out[0:count] + out[count : 2 * count] + out[2 * count : 3 * count]


def pack_rows(per_frame):
    rows = jnp.concatenate(per_frame, axis=1)
    dims = (FRAMES * CH, CH)
    marks = (iota(1, dims) == (iota(0, dims) >> 2)).astype(F32).astype(BF16)
    return split_dot(rows, marks)


def unpack_rows(table, marks):
    total = split_dot(table, marks)
    return [total[:, f * CH : (f + 1) * CH] for f in range(FRAMES)]


def row(ref, at):
    return ref[at : at + 1]


def colsum(x):
    return jnp.sum(x, axis=0, keepdims=True)


def flat(x):
    return x.reshape(-1, CH)


def act_slope(normed, gain, shift):
    act = normed * gain + shift
    sigm = jax.nn.sigmoid(act)
    return sigm * (1.0 + act * (1.0 - sigm))


def copy_in(pairs, sems):
    copies = [pltpu.make_async_copy(src, dst, sems.at[n]) for n, (src, dst) in enumerate(pairs)]
    for copy in copies:
        copy.start()
    return copies


def sums_kernel(
    cells, clip_hbm, pre_ref, cot_ref, loss_ref, gain_ref, shift_ref,
    out_ref, head_ref, tail_ref, own_ref, params_ref, clip_ref, held_ref, held_cot, sems,
):
    pairs = [
        (clip_hbm, clip_ref), (pre_ref, held_ref), (cot_ref, held_cot),
        (gain_ref, params_ref.at[GAIN : GAIN + 1]), (shift_ref, params_ref.at[SHIFT : SHIFT + 1]),
    ]
    for ref, two, one in ((head_ref, 0, 0), (tail_ref, ROWS - 2, ROWS - 1)):
        pairs += [
            (pre_ref.at[0, :, two : two + 2], ref.at[:, 0:2]),
            (cot_ref.at[:, two : two + 2], ref.at[:, 2:4]),
            (pre_ref.at[1, :, one : one + 1], ref.at[:, 4:5]),
            (loss_ref.at[:, one : one + 1], ref.at[:, 5:6]),
        ]
    copies = copy_in(pairs, sems)
    params_ref[SHIFT + 1 :] = jnp.zeros((PARAM_ROWS - SHIFT - 1, CH), F32)

    def put(at, scalar):
        params_ref[at : at + 1] = jnp.full((1, CH), scalar, F32)

    copies[0].wait()
    for t in range(2):
        clips = [clip_ref[0, t, 0, f] for f in range(FRAMES)]
        for f in range(FRAMES):
            count = jnp.int32(0)
            for other in range(FRAMES):
                count = count + (clips[other] == clips[f]).astype(jnp.int32)
            live = (clips[f] < FRAMES).astype(F32)
            base = TURN * t + f
            params_ref[base + INV : base + INV + 1] = 1.0 / jnp.full((1, CH), count.astype(F32) * cells, F32)
            put(base + LIVE, live)
            put(CLIPS + FRAMES * t + f, clips[f].astype(F32))
            for kt, at in ((1, PAIR1), (2, PAIR2)):
                pair = live * (clips[f - kt] == clips[f]).astype(F32) if f >= kt else live * 0.0
                put(base + at, pair)
    copies[1].wait()
    per_frame = []
    for f in range(FRAMES):
        rows = []
        for t in range(2):
            x = flat(held_ref[t, f].astype(F32))
            if t == 0:
                own_ref[0, f] = x.reshape(ROWS, COLS, CH)
            rows += [colsum(x), colsum(x * x)]
        per_frame.append(jnp.concatenate(rows, axis=0))
    out_ref[...] = jnp.broadcast_to(pack_rows(per_frame)[None], out_ref.shape)
    copies[2].wait()
    own_ref[1] = held_cot[...].astype(F32)
    for copy in copies[3:]:
        copy.wait()


def clip_marks(params_ref, turn):
    slot = iota(0) >> 5
    clips = [row(params_ref, CLIPS + FRAMES * turn + f) for f in range(FRAMES)]
    clip_of_row = jnp.where(
        slot == 0, clips[0], jnp.where(slot == 1, clips[1], jnp.where(slot == 2, clips[2], clips[3]))
    )
    same_group = (iota(0) & (GROUPS - 1)) == (iota(1) >> 2)
    blocks = [(same_group & (clip_of_row == clips[f])).astype(F32).astype(BF16) for f in range(FRAMES)]
    return jnp.concatenate(blocks, axis=1)


def act_first_kernel(table_ref, own_ref, params_ref, out_ref, stats_ref):
    table = jnp.sum(table_ref[...], axis=0)
    gain, shift = row(params_ref, GAIN), row(params_ref, SHIFT)
    for t, mean_at, rstd_at in ((0, MEAN0, RSTD0), (1, MEAN1, RSTD1)):
        total = unpack_rows(table[2 * t : 2 * t + 2], clip_marks(params_ref, t))
        for f in range(FRAMES):
            inverse = row(params_ref, TURN * t + INV + f)
            mean = total[f][0:1] * inverse
            var = total[f][1:2] * inverse - mean * mean
            stats_ref[mean_at + f : mean_at + f + 1] = mean
            stats_ref[rstd_at + f : rstd_at + f + 1] = 1.0 / jnp.sqrt(var + EPS)
    per_frame = []
    gain_part = jnp.zeros((1, CH), F32)
    shift_part = jnp.zeros((1, CH), F32)
    for f in range(FRAMES):
        normed = (flat(own_ref[0, f]) - row(stats_ref, MEAN0 + f)) * row(stats_ref, RSTD0 + f)
        grad_act = flat(own_ref[1, f]) * act_slope(normed, gain, shift)
        live = row(params_ref, LIVE + f)
        plain = colsum(grad_act) * live
        times = colsum(grad_act * normed) * live
        shift_part = shift_part + plain
        gain_part = gain_part + times
        per_frame.append(jnp.concatenate([plain * gain, times * gain], axis=0))
    stats_ref[GAIN_PART : GAIN_PART + 1] = gain_part
    stats_ref[SHIFT_PART : SHIFT_PART + 1] = shift_part
    stats_ref[SHIFT_PART + 1 :] = jnp.zeros((STAT_ROWS - SHIFT_PART - 1, CH), F32)
    out_ref[...] = jnp.broadcast_to(pack_rows(per_frame)[None], out_ref.shape)


def fields(pre, incoming, mean, rstd, gain, shift, mask):
    normed = (flat(pre.astype(F32)) - mean) * rstd
    scaled = flat(incoming.astype(F32)) * act_slope(normed, gain, shift) * gain
    rstd = rstd * mask
    return scaled * rstd, normed * rstd


def fields_first_kernel(
    flag_ref, up_ref, down_ref, plain_ref, stats_ref, pre_ref, cot_ref, loss_ref, act_ref,
    out_ref, bundle_hbm, loss_out_ref, params_ref, bundle_ref, held_loss, sems,
):
    copies = copy_in(
        [
            (pre_ref.at[0], bundle_ref.at[:, 15 : 15 + ROWS]), (cot_ref, bundle_ref.at[:, 21 : 21 + ROWS]),
            (loss_ref, held_loss), (pre_ref.at[1], bundle_ref.at[:, 1 : 1 + ROWS]),
            (act_ref.at[0], bundle_ref.at[:, 6 : 6 + ROWS]),
            (act_ref.at[1], bundle_ref.at[:, 6 + ROWS : 6 + 2 * ROWS]),
        ],
        sems,
    )
    params_ref[...] = plain_ref[...]
    flag = [flag_ref[n].astype(F32) for n in range(6)]
    for at, n in ((CORE, 4), (LAST, 5)):
        params_ref[at : at + 1] = jnp.full((1, CH), flag[n], F32)
    for t in range(2):
        for f in range(FRAMES):
            live = plain_ref[TURN * t + LIVE + f : TURN * t + LIVE + f + 1]
            for at, n in (
                (TURN * t + TOP, 0), (TURN * t + BOTTOM, 1),
                (OTHER_TURN * t + OTHER_TOP, 2), (OTHER_TURN * t + OTHER_BOTTOM, 3),
            ):
                params_ref[at + f : at + f + 1] = live * flag[n]
    for at, edge, below in ((0, 4, 4), (14, 1, 0), (20, 3, 2)):
        bundle_ref[:, at : at + 1] = up_ref[:, edge : edge + 1]
        bundle_ref[:, at + 1 + ROWS : at + 2 + ROWS] = down_ref[:, below : below + 1]
    for copy in copies:
        copy.wait()
    bundle_out = pltpu.make_async_copy(bundle_ref, bundle_hbm, sems.at[6])
    bundle_out.start()
    gain, shift = row(params_ref, GAIN), row(params_ref, SHIFT)
    last = row(params_ref, LAST).reshape(1, 1, 1, CH)
    loss_out_ref[:, 0:1] = (up_ref[:, 5:6].astype(F32) * last).astype(BF16)
    loss_out_ref[:, 1 : 1 + ROWS] = (held_loss[...].astype(F32) * last).astype(BF16)
    loss_out_ref[:, 1 + ROWS : 2 + ROWS] = (down_ref[:, 5:6].astype(F32) * last).astype(BF16)
    for f in range(FRAMES):
        mean, rstd = row(stats_ref, MEAN0 + f), row(stats_ref, RSTD0 + f)
        for at, count, pre, cot, mask in (
            (0, 2, up_ref[f, 0:2], up_ref[f, 2:4], TOP),
            (2, ROWS, bundle_ref[f, 15 : 15 + ROWS], bundle_ref[f, 21 : 21 + ROWS], LIVE),
            (2 + ROWS, 2, down_ref[f, 0:2], down_ref[f, 2:4], BOTTOM),
        ):
            pair = fields(pre, cot, mean, rstd, gain, shift, row(params_ref, mask + f))
            for n in range(2):
                out_ref[n, f, at : at + count] = pair[n].reshape(count, COLS, CH)
    bundle_out.wait()


def write_columns(store, table, fields_ref, at_fields, params_ref, stats_ref, rstd_at, turn, halo, masks):
    total = unpack_rows(table, clip_marks(params_ref, turn))
    rows = ROWS + 2 * halo
    column = iota(0, (rows * COLS, CH)) & (COLS - 1)
    for f in range(FRAMES):
        inverse = row(params_ref, TURN * turn + INV + f)
        avg_a = total[f][0:1] * inverse * row(stats_ref, rstd_at + f)
        avg_b = total[f][1:2] * inverse
        pieces = []
        for mask, at, count in ((masks[0], 0, halo), (masks[1], halo, ROWS), (masks[2], halo + ROWS, halo)):
            scaled = flat(fields_ref[at_fields + (0, f, slice(at, at + count))])
            normed = flat(fields_ref[at_fields + (1, f, slice(at, at + count))])
            pieces.append(scaled - avg_a * row(params_ref, mask + f) - normed * avg_b)
        value = jnp.concatenate(pieces, axis=0)
        left = jnp.where(column == COLS - 1, 0.0, pltpu.roll(value, rows * COLS - 1, 0))
        right = jnp.where(column == 0, 0.0, pltpu.roll(value, 1, 0))
        store(f, left.astype(BF16), value.astype(BF16), right.astype(BF16))


def store_columns(ref, prefix=()):
    def store(f, left, value, right):
        for n, x in enumerate((left, value, right)):
            ref[prefix + (f, slice(None), slice(n * CH, (n + 1) * CH))] = x

    return store


def conv(columns_ref, weight_ref, params_ref, turn, rows, sum_ref):
    size = rows * COLS
    for kt in range(3):
        count = FRAMES - kt
        part = None
        for dy in (-1, 0, 1):
            start = (1 - dy) * COLS
            block = columns_ref[kt:FRAMES, start : start + size, :].reshape(count * size, 3 * CH)
            for dx in range(3):
                at = (9 * kt + 3 * (dy + 1) + dx) * CH
                term = lax.dot_general(
                    block[:, dx * CH : (dx + 1) * CH], weight_ref[at : at + CH], (((1,), (1,)), ((), ())),
                    preferred_element_type=F32,
                )
                part = term if part is None else part + term
        for f in range(count):
            mine = part[f * size : (f + 1) * size]
            if kt:
                mine = mine * row(params_ref, TURN * turn + (PAIR1 if kt == 1 else PAIR2) + f + kt)
                sum_ref[f] = sum_ref[f] + mine
            else:
                sum_ref[f] = mine


def conv_first_kernel(
    table_ref, fields_ref, params_ref, stats_ref, taps_ref, grad_ref, value_hbm,
    columns_ref, weight_ref, value_ref, sum_ref, sems,
):
    (copy,) = copy_in([(taps_ref, weight_ref)], sems)
    table = jnp.sum(table_ref[...], axis=0)
    fill = store_columns(columns_ref)

    def store(f, left, value, right):
        fill(f, left, value, right)
        value_ref[f] = value[COLS : COLS * (ROWS + 3)].reshape(ROWS + 2, COLS, CH)

    write_columns(
        store, table, fields_ref, (), params_ref, stats_ref, RSTD0, 0, 2, (TOP, LIVE, BOTTOM)
    )
    value_out = pltpu.make_async_copy(value_ref, value_hbm, sems.at[1])
    value_out.start()
    copy.wait()
    conv(columns_ref, weight_ref, params_ref, 0, ROWS + 2, sum_ref)
    grad_ref[...] = sum_ref[...].astype(BF16).reshape(grad_ref.shape)
    value_out.wait()


def put_acts(turn, bundle_ref, other_ref, params_ref, out_ref):
    for strip, ref in enumerate((bundle_ref, other_ref)):
        for f in range(FRAMES):
            x = flat(ref[f, 6 + ROWS * turn : 6 + ROWS * (turn + 1)].astype(F32)).T
            for kt in range(min(3, FRAMES - f)):
                at = CH * (2 * sum(FRAMES - n for n in range(kt)) + strip * (FRAMES - kt) + f)
                y = x if kt == 0 else x * row(params_ref, TURN * turn + (PAIR1 if kt == 1 else PAIR2) + f + kt)
                out_ref[:, at : at + CH] = y.astype(BF16)


def kernel_terms(columns_ref, act_ref, kt, dy):
    count = FRAMES - kt
    start = (1 - dy) * COLS
    columns = columns_ref[:, kt:FRAMES, start : start + ROWS * COLS, :].reshape(2 * count * CH, 3 * CH)
    at = 2 * CH * sum(FRAMES - n for n in range(kt))
    return jnp.dot(act_ref[:, at : at + 2 * count * CH], columns, preferred_element_type=F32)


def act_second_kernel(hand_ref, loss_ref, slope_ref, params_ref, stats_ref, out_ref, incoming_ref):
    gain = row(params_ref, GAIN)
    per_frame = []
    gain_part = row(stats_ref, GAIN_PART)
    shift_part = row(stats_ref, SHIFT_PART)
    for f in range(FRAMES):
        incoming = hand_ref[f].astype(F32) + loss_ref[f].astype(F32)
        incoming_ref[f] = incoming.astype(BF16)
        grad_act = flat(incoming[1 : 1 + ROWS]) * flat(slope_ref[0, f])
        live = row(params_ref, TURN + LIVE + f)
        plain = colsum(grad_act) * live
        times = colsum(grad_act * flat(slope_ref[1, f])) * live
        shift_part = shift_part + plain
        gain_part = gain_part + times
        per_frame.append(jnp.concatenate([plain * gain, times * gain], axis=0))
    rows = jnp.concatenate([pack_rows(per_frame), gain_part, shift_part], axis=0)
    out_ref[...] = jnp.broadcast_to(rows[None], out_ref.shape)


def weight_first_kernel(
    table_ref, params_ref, stats_ref, value_hbm, bundle_hbm, other_hbm,
    slope_ref, act_hbm, first_hbm,
    columns_ref, act_first_ref, act_ref, first_ref, value_ref, bundle_ref, other_ref, fields_ref, sems,
):
    copies = copy_in([(bundle_hbm, bundle_ref), (other_hbm, other_ref), (value_hbm, value_ref)], sems)
    table = jnp.sum(table_ref[...], axis=0)
    gain, shift = row(params_ref, GAIN), row(params_ref, SHIFT)
    copies[0].wait()
    for f in range(FRAMES):
        normed = flat(bundle_ref[f, 1 : 1 + ROWS].astype(F32)) - row(stats_ref, MEAN1 + f)
        normed = normed * row(stats_ref, RSTD1 + f)
        slope_ref[0, f] = act_slope(normed, gain, shift).reshape(ROWS, COLS, CH)
        slope_ref[1, f] = normed.reshape(ROWS, COLS, CH)
    copies[1].wait()
    put_acts(0, bundle_ref, other_ref, params_ref, act_first_ref)
    put_acts(1, bundle_ref, other_ref, params_ref, act_ref)
    acts_out = pltpu.make_async_copy(act_ref, act_hbm, sems.at[3])
    acts_out.start()
    for f in range(FRAMES):
        mean, rstd = row(stats_ref, MEAN0 + f), row(stats_ref, RSTD0 + f)
        for at, count, mask in ((0, 1, OTHER_TOP), (1, ROWS, LIVE), (1 + ROWS, 1, OTHER_BOTTOM)):
            pair = fields(
                other_ref[f, 14 + at : 14 + at + count], other_ref[f, 20 + at : 20 + at + count], mean, rstd,
                gain, shift, row(params_ref, mask + f),
            )
            for n in range(2):
                fields_ref[n, f, at : at + count] = pair[n].reshape(count, COLS, CH)
    write_columns(
        store_columns(columns_ref, (1,)), table, fields_ref, (), params_ref, stats_ref, RSTD0, 0, 1,
        (OTHER_TOP, LIVE, OTHER_BOTTOM),
    )
    copies[2].wait()
    rows = ROWS + 2
    column = iota(0, (rows * COLS, CH)) & (COLS - 1)
    fill = store_columns(columns_ref, (0,))
    for f in range(FRAMES):
        value = flat(value_ref[f].astype(F32))
        left = jnp.where(column == COLS - 1, 0.0, pltpu.roll(value, rows * COLS - 1, 0))
        right = jnp.where(column == 0, 0.0, pltpu.roll(value, 1, 0))
        fill(f, left.astype(BF16), value.astype(BF16), right.astype(BF16))
    for kt in range(3):
        for dy in (-1, 0, 1):
            terms = kernel_terms(columns_ref, act_first_ref, kt, dy)
            tap = 9 * kt + 3 * (dy + 1)
            for dx in range(3):
                first_ref[tap + dx] = terms[:, dx * CH : (dx + 1) * CH]
    first_out = pltpu.make_async_copy(first_ref, first_hbm, sems.at[4])
    first_out.start()
    acts_out.wait()
    first_out.wait()


def fields_second_kernel(
    incoming_ref, arrived_ref, bundle_hbm, other_hbm, params_ref, stats_ref, out_ref, bundle_ref, other_ref, sems,
):
    pre_part = slice(0, ROWS + 2)
    copies = copy_in(
        [(bundle_hbm.at[:, pre_part], bundle_ref), (other_hbm.at[:, pre_part], other_ref)], sems
    )
    for copy in copies:
        copy.wait()
    gain, shift = row(params_ref, GAIN), row(params_ref, SHIFT)
    for f in range(FRAMES):
        mean, rstd = row(stats_ref, MEAN1 + f), row(stats_ref, RSTD1 + f)
        for strip, pre_ref, come_ref, top, bottom in (
            (0, bundle_ref, incoming_ref, TURN + TOP, TURN + BOTTOM),
            (1, other_ref, arrived_ref, OTHER_TURN + OTHER_TOP, OTHER_TURN + OTHER_BOTTOM),
        ):
            for at, count, mask in ((0, 1, top), (1, ROWS, TURN + LIVE), (1 + ROWS, 1, bottom)):
                pair = fields(
                    pre_ref[f, at : at + count], come_ref[f, at : at + count], mean, rstd, gain, shift,
                    row(params_ref, mask + f),
                )
                for n in range(2):
                    out_ref[strip, n, f, at : at + count] = pair[n].reshape(count, COLS, CH)


def weight_second_kernel(
    scale, chunk, table_ref, fields_ref, params_ref, stats_ref, first_hbm, act_hbm,
    out_hbm, own_hbm, parts_ref, columns_ref, sum_ref, act_ref, first_ref, out_ref, sems,
):
    arrive = copy_in(
        [(act_hbm, act_ref)] + [(first_hbm.at[n : n + 3], first_ref.at[n : n + 3]) for n in range(0, TAPS, 3)], sems
    )
    table = jnp.sum(table_ref[...], axis=0)
    parts_ref[...] = table[2:4] * scale
    for strip, top, bottom in ((0, TURN + TOP, TURN + BOTTOM), (1, OTHER_TURN + OTHER_TOP, OTHER_TURN + OTHER_BOTTOM)):
        write_columns(
            store_columns(columns_ref, (strip,)), table[0:2], fields_ref, (strip,), params_ref, stats_ref,
            RSTD1, 1, 1, (top, TURN + LIVE, bottom),
        )
    copy_own = pltpu.make_async_copy(columns_ref.at[0], own_hbm, sems.at[10])
    copy_own.start()
    arrive[0].wait()
    second = row(params_ref, CORE) > 0.5
    filler = jnp.zeros((out_ref.shape[1] - chunk, CH), F32)
    chips = out_ref.shape[0]
    done = 0
    copies = [copy_own]
    for kt in range(3):
        for dy in (-1, 0, 1):
            terms = kernel_terms(columns_ref, act_ref, kt, dy)
            tap = 9 * kt + 3 * (dy + 1)
            arrive[1 + tap // 3].wait()
            for dx in range(3):
                at = (tap + dx) * CH
                sum_ref[at : at + CH] = first_ref[tap + dx] + terms[:, dx * CH : (dx + 1) * CH]
        begin = done
        while done < chips and 2 * (done + 1) * chunk <= 9 * (kt + 1) * CH:
            at = 2 * done * chunk
            mine = jnp.where(second, sum_ref[at + chunk : at + 2 * chunk], sum_ref[at : at + chunk])
            if filler.shape[0]:
                mine = jnp.concatenate([mine, filler], axis=0)
            out_ref[done] = mine.astype(BF16)
            done += 1
        if done > begin:
            send = pltpu.make_async_copy(out_ref.at[begin:done], out_hbm.at[begin:done], sems.at[11 + kt])
            send.start()
            copies.append(send)
    for copy in copies:
        copy.wait()


def conv_second_kernel(
    params_ref, columns_hbm, first_hbm, taps_ref, out_ref, weight_ref, columns_ref, first_ref, sum_ref, sems
):
    for copy in copy_in([(columns_hbm, columns_ref), (first_hbm, first_ref), (taps_ref, weight_ref)], sems):
        copy.wait()
    conv(columns_ref, weight_ref, params_ref, 1, ROWS, sum_ref)
    out_ref[0] = first_ref[:, 1 : 1 + ROWS]
    out_ref[1] = sum_ref[...].astype(BF16).reshape(first_ref[:, 1 : 1 + ROWS].shape)


def total_kernel(scale, terms_ref, out_ref):
    chunk = out_ref.shape[0]
    total = jnp.sum(terms_ref[...].astype(F32), axis=0)
    out_ref[...] = (total[0:chunk] * scale).reshape(chunk, 1, CH)


def call(kernel, name, args, outs, scratch=(), specs="", flops=1_000_000):
    specs = specs or "v" * len(args)
    size = sum(a.size * a.dtype.itemsize for a in args)
    space = {"k": pltpu.VMEM, "h": pltpu.HBM}
    args = [pltpu.with_memory_space_constraint(a, space[x]) if x in space else a for a, x in zip(args, specs)]
    return pl.pallas_call(
        kernel,
        out_shape=tuple(outs),
        in_specs=[{"v": VMEM, "k": VMEM, "s": SMEM, "h": HBM}[x] for x in specs],
        out_specs=tuple(HBM if getattr(o, "memory_space", None) is pltpu.HBM else VMEM for o in outs),
        scratch_shapes=list(scratch),
        compiler_params=pltpu.CompilerParams(vmem_limit_bytes=24 * 1024 * 1024),
        cost_estimate=pl.CostEstimate(flops=flops, bytes_accessed=size, transcendentals=0),
        name=name,
    )(*args)


def shape(dims, dtype=F32):
    return jax.ShapeDtypeStruct(dims, dtype)


def kept(dims, dtype=F32):
    return pltpu.VMEM(dims, dtype)


def in_hbm(dims, dtype=F32):
    return pltpu.HBM(dims, dtype)


def local(activations, pre_norm, cot_first, loss_grad, frame_clip, weight, norm_gain, norm_shift):
    dp = lax.axis_size("dp")
    me = lax.axis_index("dp")
    cells = float(dp * ROWS * COLS * PER)
    chips, chunk = dp // 2, TAPS * CH // dp
    padded = -(-chunk // 8) * 8
    other = me ^ 1
    last = lax.axis_index("segment") == lax.axis_size("segment") - 1
    flags = [me != 0, me != dp - 1, other != 0, other != dp - 1, me & 1, last]
    flags = jnp.stack([x.astype(jnp.int32) for x in flags])
    pre, act = pre_norm[0], activations[0]
    cot, loss = cot_first[0], loss_grad[0]
    taps = weight[0]
    edge = (FRAMES, ROWS + 2, COLS, CH)
    strip = (FRAMES, ROWS, COLS, CH)
    bundled = (FRAMES, 3 * (ROWS + 2) + 2 * ROWS, COLS, CH)
    mates = [(i, i ^ 1) for i in range(dp)]
    columns_of = lambda rows: (FRAMES, rows * COLS, 3 * CH)
    sems = lambda n: pltpu.SemaphoreType.DMA((n,))

    def exchange(table):
        return lax.all_to_all(table, "dp", 0, 0, tiled=True)

    table, head, tail, own, plain = call(
        functools.partial(sums_kernel, cells), "sums", (frame_clip, pre, cot, loss, norm_gain, norm_shift),
        (
            shape((dp, 4, CH)), shape(edge, BF16), shape(edge, BF16),
            kept((2,) + strip), kept((PARAM_ROWS, CH)),
        ),
        scratch=[
            pltpu.SMEM((1, 2, 1, FRAMES), jnp.int32), pltpu.VMEM((2,) + strip, BF16), pltpu.VMEM(strip, BF16), sems(13)
        ],
        specs="hhhhhh",
    )
    table = exchange(table)
    down = lax.ppermute(head, "dp", [(i + 1, i) for i in range(dp - 1)])
    up = lax.ppermute(tail, "dp", [(i, i + 1) for i in range(dp - 1)])

    table, stats = call(
        act_first_kernel, "act_first", (table, own, plain), (shape((dp, 2, CH)), kept((STAT_ROWS, CH))), specs="vkk"
    )
    table = exchange(table)

    first_fields, bundle, loss_rows, params = call(
        fields_first_kernel, "fields_first", (flags, up, down, plain, stats, pre, cot, loss, act),
        (
            kept((2, FRAMES, ROWS + 4, COLS, CH)), in_hbm(bundled, BF16),
            kept(edge, BF16), kept((PARAM_ROWS, CH)),
        ),
        scratch=[pltpu.VMEM(bundled, BF16), pltpu.VMEM(strip, BF16), sems(7)],
        specs="svvkkhhhh",
    )
    other_bundle = lax.ppermute(bundle, "dp", mates)

    weights = pltpu.VMEM((TAPS * CH, CH), BF16)
    grad_first, value = call(
        conv_first_kernel, "conv_first", (table, first_fields, params, stats, taps),
        (shape(edge, BF16), in_hbm(edge, BF16)),
        scratch=[
            pltpu.VMEM(columns_of(ROWS + 4), BF16), weights, pltpu.VMEM(edge, BF16),
            pltpu.VMEM((FRAMES, (ROWS + 2) * COLS, CH), F32), sems(2),
        ],
        specs="vkkkh", flops=20_000_000_000,
    )
    count = lax.axis_size("segment")
    hand = lax.ppermute(grad_first, "segment", [(i + 1, i) for i in range(count - 1)])

    both = pltpu.VMEM((2,) + columns_of(ROWS + 2), BF16)
    acts_dims, taps_dims = (CH, 2 * 9 * CH), (TAPS, CH, CH)
    slope, acts, weight_first = call(
        weight_first_kernel, "weight_first", (table, params, stats, value, bundle, other_bundle),
        (kept((2,) + strip), in_hbm(acts_dims, BF16), in_hbm(taps_dims)),
        scratch=[both, pltpu.VMEM(acts_dims, BF16), pltpu.VMEM(acts_dims, BF16), pltpu.VMEM(taps_dims, F32)]
        + [pltpu.VMEM(edge, BF16)] + [pltpu.VMEM(bundled, BF16)] * 2 + [pltpu.VMEM((2,) + edge, F32), sems(5)],
        specs="vkkhhh",
    )

    table, incoming = call(
        act_second_kernel, "act_second", (hand, loss_rows, slope, params, stats),
        (shape((dp, 4, CH)), shape(edge, BF16)), specs="vkkkk",
    )
    table = exchange(table)
    arrived = lax.ppermute(incoming, "dp", mates)
    (second_fields,) = call(
        fields_second_kernel, "fields_second", (incoming, arrived, bundle, other_bundle, params, stats),
        (kept((2, 2) + edge),), scratch=[pltpu.VMEM(edge, BF16)] * 2 + [sems(2)], specs="vvhhkk",
    )

    terms, columns, parts = call(
        functools.partial(weight_second_kernel, 1.0 / dp, chunk), "weight_second",
        (table, second_fields, params, stats, weight_first, acts),
        (in_hbm((chips, padded, CH), BF16), in_hbm(columns_of(ROWS + 2), BF16), shape((2, CH))),
        scratch=[
            both, pltpu.VMEM((TAPS * CH, CH), F32), pltpu.VMEM(acts_dims, BF16), pltpu.VMEM(taps_dims, F32),
            pltpu.VMEM((chips, padded, CH), BF16), sems(14),
        ],
        specs="vkkkhh",
    )
    sides = [[2 * i + core for i in range(chips)] for core in range(2)]
    terms = lax.all_to_all(terms, "dp", 0, 0, axis_index_groups=sides, tiled=True)
    (grad_weight,) = call(
        functools.partial(total_kernel, 1.0 / dp), "total", (terms,), (shape((chunk, 1, CH)),)
    )
    (grad_inputs,) = call(
        conv_second_kernel, "conv_second", (params, columns, grad_first, taps),
        (shape((2, FRAMES, ROWS, COLS, CH), BF16),),
        scratch=[
            weights, pltpu.VMEM(columns_of(ROWS + 2), BF16), pltpu.VMEM(edge, BF16),
            pltpu.VMEM((FRAMES, ROWS * COLS, CH), F32), sems(3),
        ],
        specs="khhh",
    )
    width = CH // dp
    mine = lax.dynamic_slice_in_dim(parts, me * width, width, axis=1)
    return (grad_inputs[None], grad_weight.transpose(1, 0, 2), mine[0:1], mine[1:2])


def solution(mesh):
    in_specs = (
        P("segment", None, None, "dp", None, None),
        P("segment", None, None, "dp", None, None),
        P("segment", None, "dp", None, None),
        P(None, None, "dp", None, None),
        P("segment", None, "dp", None),
        P("segment", None, None),
        P("segment", None),
        P("segment", None),
    )
    out_specs = (
        P("segment", None, None, "dp", None, None),
        P("segment", "dp", None),
        P("segment", "dp"),
        P("segment", "dp"),
    )
    return jax.shard_map(local, mesh=mesh, in_specs=in_specs, out_specs=out_specs, check_vma=False)
```

```python
import functools
import jax
import jax.numpy as jnp
from jax import lax
from jax.experimental import pallas as pl
from jax.experimental.pallas import tpu as pltpu
from jax.sharding import PartitionSpec as P

F32, BF16 = jnp.float32, jnp.bfloat16
FRAMES, ROWS, COLS, CH = 4, 4, 32, 128
GROUPS, PER = 32, 4
TAPS = 27
EPS = 1e-05
VMEM = pl.BlockSpec(memory_space=pltpu.VMEM)
SMEM = pl.BlockSpec(memory_space=pltpu.SMEM)
HBM = pl.BlockSpec(memory_space=pltpu.HBM)

GAIN, SHIFT, CORE, LAST = 0, 1, 2, 3
TURN = 24
INV, LIVE, TOP, BOTTOM, PAIR1, PAIR2 = (8 + 4 * n for n in range(6))
OTHER_TOP, OTHER_BOTTOM = 56, 60
CLIPS = 64
OTHER_TURN = 16
PARAM_ROWS = 80
MEAN0, RSTD0, MEAN1, RSTD1, GAIN_PART, SHIFT_PART = 0, 4, 8, 12, 16, 17
STAT_ROWS = 24


def iota(dim, dims=(CH, CH)):
    return lax.broadcasted_iota(jnp.int32, dims, dim)


def split_dot(rows, marks):
    count = rows.shape[0]
    high = rows.astype(BF16)
    rest = rows - high.astype(F32)
    middle = rest.astype(BF16)
    low = (rest - middle.astype(F32)).astype(BF16)
    out = jnp.dot(
        jnp.concatenate([high.astype(F32), middle.astype(F32), low.astype(F32)], axis=0).astype(BF16),
        marks,
        preferred_element_type=F32,
    )
    return out[0:count] + out[count : 2 * count] + out[2 * count : 3 * count]


def pack_rows(per_frame):
    rows = jnp.concatenate(per_frame, axis=1)
    dims = (FRAMES * CH, CH)
    marks = (iota(1, dims) == (iota(0, dims) >> 2)).astype(F32).astype(BF16)
    return split_dot(rows, marks)


def unpack_rows(table, marks):
    total = split_dot(table, marks)
    return [total[:, f * CH : (f + 1) * CH] for f in range(FRAMES)]


def row(ref, at):
    return ref[at : at + 1]


def colsum(x):
    return jnp.sum(x, axis=0, keepdims=True)


def flat(x):
    return x.reshape(-1, CH)


def act_slope(normed, gain, shift):
    act = normed * gain + shift
    sigm = jax.nn.sigmoid(act)
    return sigm * (1.0 + act * (1.0 - sigm))


def copy_in(pairs, sems):
    copies = [pltpu.make_async_copy(src, dst, sems.at[n]) for n, (src, dst) in enumerate(pairs)]
    for copy in copies:
        copy.start()
    return copies


def sums_kernel(
    cells, clip_hbm, pre_ref, cot_ref, loss_ref, gain_ref, shift_ref,
    out_ref, head_ref, tail_ref, own_ref, params_ref, clip_ref, held_ref, held_cot, sems,
):
    pairs = [
        (clip_hbm, clip_ref), (pre_ref, held_ref), (cot_ref, held_cot),
        (gain_ref, params_ref.at[GAIN : GAIN + 1]), (shift_ref, params_ref.at[SHIFT : SHIFT + 1]),
    ]
    for ref, two, one in ((head_ref, 0, 0), (tail_ref, ROWS - 2, ROWS - 1)):
        pairs += [
            (pre_ref.at[0, :, two : two + 2], ref.at[:, 0:2]),
            (cot_ref.at[:, two : two + 2], ref.at[:, 2:4]),
            (pre_ref.at[1, :, one : one + 1], ref.at[:, 4:5]),
            (loss_ref.at[:, one : one + 1], ref.at[:, 5:6]),
        ]
    copies = copy_in(pairs, sems)
    params_ref[SHIFT + 1 :] = jnp.zeros((PARAM_ROWS - SHIFT - 1, CH), F32)

    def put(at, scalar):
        params_ref[at : at + 1] = jnp.full((1, CH), scalar, F32)

    copies[0].wait()
    for t in range(2):
        clips = [clip_ref[0, t, 0, f] for f in range(FRAMES)]
        for f in range(FRAMES):
            count = jnp.int32(0)
            for other in range(FRAMES):
                count = count + (clips[other] == clips[f]).astype(jnp.int32)
            live = (clips[f] < FRAMES).astype(F32)
            base = TURN * t + f
            params_ref[base + INV : base + INV + 1] = 1.0 / jnp.full((1, CH), count.astype(F32) * cells, F32)
            put(base + LIVE, live)
            put(CLIPS + FRAMES * t + f, clips[f].astype(F32))
            for kt, at in ((1, PAIR1), (2, PAIR2)):
                pair = live * (clips[f - kt] == clips[f]).astype(F32) if f >= kt else live * 0.0
                put(base + at, pair)
    copies[1].wait()
    per_frame = []
    for f in range(FRAMES):
        rows = []
        for t in range(2):
            x = flat(held_ref[t, f].astype(F32))
            if t == 0:
                own_ref[0, f] = x.reshape(ROWS, COLS, CH)
            rows += [colsum(x), colsum(x * x)]
        per_frame.append(jnp.concatenate(rows, axis=0))
    out_ref[...] = jnp.broadcast_to(pack_rows(per_frame)[None], out_ref.shape)
    copies[2].wait()
    own_ref[1] = held_cot[...].astype(F32)
    for copy in copies[3:]:
        copy.wait()


def clip_marks(params_ref, turn):
    slot = iota(0) >> 5
    clips = [row(params_ref, CLIPS + FRAMES * turn + f) for f in range(FRAMES)]
    clip_of_row = jnp.where(
        slot == 0, clips[0], jnp.where(slot == 1, clips[1], jnp.where(slot == 2, clips[2], clips[3]))
    )
    same_group = (iota(0) & (GROUPS - 1)) == (iota(1) >> 2)
    blocks = [(same_group & (clip_of_row == clips[f])).astype(F32).astype(BF16) for f in range(FRAMES)]
    return jnp.concatenate(blocks, axis=1)


def act_first_kernel(table_ref, own_ref, params_ref, out_ref, stats_ref):
    table = jnp.sum(table_ref[...], axis=0)
    gain, shift = row(params_ref, GAIN), row(params_ref, SHIFT)
    for t, mean_at, rstd_at in ((0, MEAN0, RSTD0), (1, MEAN1, RSTD1)):
        total = unpack_rows(table[2 * t : 2 * t + 2], clip_marks(params_ref, t))
        for f in range(FRAMES):
            inverse = row(params_ref, TURN * t + INV + f)
            mean = total[f][0:1] * inverse
            var = total[f][1:2] * inverse - mean * mean
            stats_ref[mean_at + f : mean_at + f + 1] = mean
            stats_ref[rstd_at + f : rstd_at + f + 1] = 1.0 / jnp.sqrt(var + EPS)
    per_frame = []
    gain_part = jnp.zeros((1, CH), F32)
    shift_part = jnp.zeros((1, CH), F32)
    for f in range(FRAMES):
        normed = (flat(own_ref[0, f]) - row(stats_ref, MEAN0 + f)) * row(stats_ref, RSTD0 + f)
        grad_act = flat(own_ref[1, f]) * act_slope(normed, gain, shift)
        live = row(params_ref, LIVE + f)
        plain = colsum(grad_act) * live
        times = colsum(grad_act * normed) * live
        shift_part = shift_part + plain
        gain_part = gain_part + times
        per_frame.append(jnp.concatenate([plain * gain, times * gain], axis=0))
    stats_ref[GAIN_PART : GAIN_PART + 1] = gain_part
    stats_ref[SHIFT_PART : SHIFT_PART + 1] = shift_part
    stats_ref[SHIFT_PART + 1 :] = jnp.zeros((STAT_ROWS - SHIFT_PART - 1, CH), F32)
    out_ref[...] = jnp.broadcast_to(pack_rows(per_frame)[None], out_ref.shape)


def fields(pre, incoming, mean, rstd, gain, shift, mask):
    normed = (flat(pre.astype(F32)) - mean) * rstd
    scaled = flat(incoming.astype(F32)) * act_slope(normed, gain, shift) * gain
    rstd = rstd * mask
    return scaled * rstd, normed * rstd


def fields_first_kernel(
    flag_ref, up_ref, down_ref, plain_ref, stats_ref, pre_ref, cot_ref, loss_ref, act_ref,
    out_ref, bundle_hbm, loss_out_ref, params_ref, bundle_ref, held_loss, sems,
):
    copies = copy_in(
        [
            (pre_ref.at[0], bundle_ref.at[:, 15 : 15 + ROWS]), (cot_ref, bundle_ref.at[:, 21 : 21 + ROWS]),
            (loss_ref, held_loss), (pre_ref.at[1], bundle_ref.at[:, 1 : 1 + ROWS]),
            (act_ref.at[0], bundle_ref.at[:, 6 : 6 + ROWS]),
            (act_ref.at[1], bundle_ref.at[:, 6 + ROWS : 6 + 2 * ROWS]),
        ],
        sems,
    )
    params_ref[...] = plain_ref[...]
    flag = [flag_ref[n].astype(F32) for n in range(6)]
    for at, n in ((CORE, 4), (LAST, 5)):
        params_ref[at : at + 1] = jnp.full((1, CH), flag[n], F32)
    for t in range(2):
        for f in range(FRAMES):
            live = plain_ref[TURN * t + LIVE + f : TURN * t + LIVE + f + 1]
            for at, n in (
                (TURN * t + TOP, 0), (TURN * t + BOTTOM, 1),
                (OTHER_TURN * t + OTHER_TOP, 2), (OTHER_TURN * t + OTHER_BOTTOM, 3),
            ):
                params_ref[at + f : at + f + 1] = live * flag[n]
    for at, edge, below in ((0, 4, 4), (14, 1, 0), (20, 3, 2)):
        bundle_ref[:, at : at + 1] = up_ref[:, edge : edge + 1]
        bundle_ref[:, at + 1 + ROWS : at + 2 + ROWS] = down_ref[:, below : below + 1]
    for copy in copies:
        copy.wait()
    bundle_out = pltpu.make_async_copy(bundle_ref, bundle_hbm, sems.at[6])
    bundle_out.start()
    gain, shift = row(params_ref, GAIN), row(params_ref, SHIFT)
    last = row(params_ref, LAST).reshape(1, 1, 1, CH)
    loss_out_ref[:, 0:1] = (up_ref[:, 5:6].astype(F32) * last).astype(BF16)
    loss_out_ref[:, 1 : 1 + ROWS] = (held_loss[...].astype(F32) * last).astype(BF16)
    loss_out_ref[:, 1 + ROWS : 2 + ROWS] = (down_ref[:, 5:6].astype(F32) * last).astype(BF16)
    for f in range(FRAMES):
        mean, rstd = row(stats_ref, MEAN0 + f), row(stats_ref, RSTD0 + f)
        for at, count, pre, cot, mask in (
            (0, 2, up_ref[f, 0:2], up_ref[f, 2:4], TOP),
            (2, ROWS, bundle_ref[f, 15 : 15 + ROWS], bundle_ref[f, 21 : 21 + ROWS], LIVE),
            (2 + ROWS, 2, down_ref[f, 0:2], down_ref[f, 2:4], BOTTOM),
        ):
            pair = fields(pre, cot, mean, rstd, gain, shift, row(params_ref, mask + f))
            for n in range(2):
                out_ref[n, f, at : at + count] = pair[n].reshape(count, COLS, CH)
    bundle_out.wait()


def write_columns(store, table, fields_ref, at_fields, params_ref, stats_ref, rstd_at, turn, halo, masks):
    total = unpack_rows(table, clip_marks(params_ref, turn))
    rows = ROWS + 2 * halo
    column = iota(0, (rows * COLS, CH)) & (COLS - 1)
    for f in range(FRAMES):
        inverse = row(params_ref, TURN * turn + INV + f)
        avg_a = total[f][0:1] * inverse * row(stats_ref, rstd_at + f)
        avg_b = total[f][1:2] * inverse
        pieces = []
        for mask, at, count in ((masks[0], 0, halo), (masks[1], halo, ROWS), (masks[2], halo + ROWS, halo)):
            scaled = flat(fields_ref[at_fields + (0, f, slice(at, at + count))])
            normed = flat(fields_ref[at_fields + (1, f, slice(at, at + count))])
            pieces.append(scaled - avg_a * row(params_ref, mask + f) - normed * avg_b)
        value = jnp.concatenate(pieces, axis=0)
        left = jnp.where(column == COLS - 1, 0.0, pltpu.roll(value, rows * COLS - 1, 0))
        right = jnp.where(column == 0, 0.0, pltpu.roll(value, 1, 0))
        store(f, left.astype(BF16), value.astype(BF16), right.astype(BF16))


def store_columns(ref, prefix=()):
    def store(f, left, value, right):
        for n, x in enumerate((left, value, right)):
            ref[prefix + (f, slice(None), slice(n * CH, (n + 1) * CH))] = x

    return store


def conv(columns_ref, weight_ref, params_ref, turn, rows, sum_ref):
    size = rows * COLS
    for kt in range(3):
        count = FRAMES - kt
        blocks = [
            columns_ref[kt:FRAMES, start : start + size, :].reshape(count * size, 3 * CH)
            for start in (2 * COLS, COLS, 0)
        ]
        part = lax.dot_general(
            jnp.concatenate(blocks, axis=1), weight_ref[kt], (((1,), (1,)), ((), ())), preferred_element_type=F32
        )
        for f in range(count):
            mine = part[f * size : (f + 1) * size]
            if kt:
                mine = mine * row(params_ref, TURN * turn + (PAIR1 if kt == 1 else PAIR2) + f + kt)
                sum_ref[f] = sum_ref[f] + mine
            else:
                sum_ref[f] = mine


def weight_copies(taps_ref, weight_ref):
    return [(taps_ref.at[:, n], weight_ref.at[:, :, n * CH : (n + 1) * CH]) for n in range(9)]


def conv_first_kernel(
    table_ref, fields_ref, params_ref, stats_ref, taps_ref, grad_ref, value_hbm,
    columns_ref, weight_ref, value_ref, sum_ref, sems,
):
    copies = copy_in(weight_copies(taps_ref, weight_ref), sems)
    table = jnp.sum(table_ref[...], axis=0)
    fill = store_columns(columns_ref)

    def store(f, left, value, right):
        fill(f, left, value, right)
        value_ref[f] = value[COLS : COLS * (ROWS + 3)].reshape(ROWS + 2, COLS, CH)

    write_columns(
        store, table, fields_ref, (), params_ref, stats_ref, RSTD0, 0, 2, (TOP, LIVE, BOTTOM)
    )
    value_out = pltpu.make_async_copy(value_ref, value_hbm, sems.at[9])
    value_out.start()
    for copy in copies:
        copy.wait()
    conv(columns_ref, weight_ref, params_ref, 0, ROWS + 2, sum_ref)
    grad_ref[...] = sum_ref[...].astype(BF16).reshape(grad_ref.shape)
    value_out.wait()


def put_acts(turn, bundle_ref, other_ref, params_ref, out_ref):
    for strip, ref in enumerate((bundle_ref, other_ref)):
        for f in range(FRAMES):
            x = flat(ref[f, 6 + ROWS * turn : 6 + ROWS * (turn + 1)].astype(F32)).T
            for kt in range(min(3, FRAMES - f)):
                at = CH * (2 * sum(FRAMES - n for n in range(kt)) + strip * (FRAMES - kt) + f)
                y = x if kt == 0 else x * row(params_ref, TURN * turn + (PAIR1 if kt == 1 else PAIR2) + f + kt)
                out_ref[:, at : at + CH] = y.astype(BF16)


def kernel_terms(columns_ref, act_ref, kt):
    count = FRAMES - kt
    blocks = [
        columns_ref[:, kt:FRAMES, start : start + ROWS * COLS, :].reshape(2 * count * CH, 3 * CH)
        for start in (2 * COLS, COLS, 0)
    ]
    at = 2 * CH * sum(FRAMES - n for n in range(kt))
    return jnp.dot(
        act_ref[:, at : at + 2 * count * CH], jnp.concatenate(blocks, axis=1), preferred_element_type=F32
    )


def act_second_kernel(hand_ref, loss_ref, slope_ref, params_ref, stats_ref, out_ref, incoming_ref):
    gain = row(params_ref, GAIN)
    per_frame = []
    gain_part = row(stats_ref, GAIN_PART)
    shift_part = row(stats_ref, SHIFT_PART)
    for f in range(FRAMES):
        incoming = hand_ref[f].astype(F32) + loss_ref[f].astype(F32)
        incoming_ref[f] = incoming.astype(BF16)
        grad_act = flat(incoming[1 : 1 + ROWS]) * flat(slope_ref[0, f])
        live = row(params_ref, TURN + LIVE + f)
        plain = colsum(grad_act) * live
        times = colsum(grad_act * flat(slope_ref[1, f])) * live
        shift_part = shift_part + plain
        gain_part = gain_part + times
        per_frame.append(jnp.concatenate([plain * gain, times * gain], axis=0))
    rows = jnp.concatenate([pack_rows(per_frame), gain_part, shift_part], axis=0)
    out_ref[...] = jnp.broadcast_to(rows[None], out_ref.shape)


def weight_first_kernel(
    table_ref, params_ref, stats_ref, value_hbm, bundle_hbm, other_hbm,
    slope_ref, act_ref, first_ref,
    columns_ref, act_first_ref, value_ref, bundle_ref, other_ref, fields_ref, sems,
):
    copies = copy_in([(bundle_hbm, bundle_ref), (other_hbm, other_ref), (value_hbm, value_ref)], sems)
    table = jnp.sum(table_ref[...], axis=0)
    gain, shift = row(params_ref, GAIN), row(params_ref, SHIFT)
    copies[0].wait()
    for f in range(FRAMES):
        normed = flat(bundle_ref[f, 1 : 1 + ROWS].astype(F32)) - row(stats_ref, MEAN1 + f)
        normed = normed * row(stats_ref, RSTD1 + f)
        slope_ref[0, f] = act_slope(normed, gain, shift).reshape(ROWS, COLS, CH)
        slope_ref[1, f] = normed.reshape(ROWS, COLS, CH)
    copies[1].wait()
    put_acts(0, bundle_ref, other_ref, params_ref, act_first_ref)
    put_acts(1, bundle_ref, other_ref, params_ref, act_ref)
    for f in range(FRAMES):
        mean, rstd = row(stats_ref, MEAN0 + f), row(stats_ref, RSTD0 + f)
        for at, count, mask in ((0, 1, OTHER_TOP), (1, ROWS, LIVE), (1 + ROWS, 1, OTHER_BOTTOM)):
            pair = fields(
                other_ref[f, 14 + at : 14 + at + count], other_ref[f, 20 + at : 20 + at + count], mean, rstd,
                gain, shift, row(params_ref, mask + f),
            )
            for n in range(2):
                fields_ref[n, f, at : at + count] = pair[n].reshape(count, COLS, CH)
    write_columns(
        store_columns(columns_ref, (1,)), table, fields_ref, (), params_ref, stats_ref, RSTD0, 0, 1,
        (OTHER_TOP, LIVE, OTHER_BOTTOM),
    )
    copies[2].wait()
    rows = ROWS + 2
    column = iota(0, (rows * COLS, CH)) & (COLS - 1)
    fill = store_columns(columns_ref, (0,))
    for f in range(FRAMES):
        value = flat(value_ref[f].astype(F32))
        left = jnp.where(column == COLS - 1, 0.0, pltpu.roll(value, rows * COLS - 1, 0))
        right = jnp.where(column == 0, 0.0, pltpu.roll(value, 1, 0))
        fill(f, left.astype(BF16), value.astype(BF16), right.astype(BF16))
    for kt in range(3):
        terms = kernel_terms(columns_ref, act_first_ref, kt)
        for n in range(9):
            first_ref[9 * kt + n] = terms[:, n * CH : (n + 1) * CH].astype(first_ref.dtype)


def fields_second_kernel(
    incoming_ref, arrived_ref, bundle_hbm, other_hbm, params_ref, stats_ref, out_ref, bundle_ref, other_ref, sems,
):
    pre_part = slice(0, ROWS + 2)
    copies = copy_in(
        [(bundle_hbm.at[:, pre_part], bundle_ref), (other_hbm.at[:, pre_part], other_ref)], sems
    )
    for copy in copies:
        copy.wait()
    gain, shift = row(params_ref, GAIN), row(params_ref, SHIFT)
    for f in range(FRAMES):
        mean, rstd = row(stats_ref, MEAN1 + f), row(stats_ref, RSTD1 + f)
        for strip, pre_ref, come_ref, top, bottom in (
            (0, bundle_ref, incoming_ref, TURN + TOP, TURN + BOTTOM),
            (1, other_ref, arrived_ref, OTHER_TURN + OTHER_TOP, OTHER_TURN + OTHER_BOTTOM),
        ):
            for at, count, mask in ((0, 1, top), (1, ROWS, TURN + LIVE), (1 + ROWS, 1, bottom)):
                pair = fields(
                    pre_ref[f, at : at + count], come_ref[f, at : at + count], mean, rstd, gain, shift,
                    row(params_ref, mask + f),
                )
                for n in range(2):
                    out_ref[strip, n, f, at : at + count] = pair[n].reshape(count, COLS, CH)


def weight_second_kernel(
    scale, chunk, table_ref, fields_ref, params_ref, stats_ref, first_ref, act_ref,
    out_hbm, own_hbm, parts_ref, columns_ref, sum_ref, out_ref, sems,
):
    table = jnp.sum(table_ref[...], axis=0)
    parts_ref[...] = table[2:4] * scale
    for strip, top, bottom in ((0, TURN + TOP, TURN + BOTTOM), (1, OTHER_TURN + OTHER_TOP, OTHER_TURN + OTHER_BOTTOM)):
        write_columns(
            store_columns(columns_ref, (strip,)), table[0:2], fields_ref, (strip,), params_ref, stats_ref,
            RSTD1, 1, 1, (top, TURN + LIVE, bottom),
        )
    copy_own = pltpu.make_async_copy(columns_ref.at[0], own_hbm, sems.at[0])
    copy_own.start()
    second = row(params_ref, CORE) > 0.5
    filler = jnp.zeros((out_ref.shape[1] - chunk, CH), F32)
    chips = out_ref.shape[0]
    done = 0
    copies = [copy_own]
    for kt in range(3):
        terms = kernel_terms(columns_ref, act_ref, kt)
        for n in range(9 * kt, 9 * kt + 9):
            at = (n - 9 * kt) * CH
            sum_ref[n * CH : (n + 1) * CH] = first_ref[n].astype(F32) + terms[:, at : at + CH]
        begin = done
        while done < chips and 2 * (done + 1) * chunk <= 9 * (kt + 1) * CH:
            at = 2 * done * chunk
            mine = jnp.where(second, sum_ref[at + chunk : at + 2 * chunk], sum_ref[at : at + chunk])
            if filler.shape[0]:
                mine = jnp.concatenate([mine, filler], axis=0)
            out_ref[done] = mine.astype(BF16)
            done += 1
        if done > begin:
            send = pltpu.make_async_copy(out_ref.at[begin:done], out_hbm.at[begin:done], sems.at[1 + kt])
            send.start()
            copies.append(send)
    for copy in copies:
        copy.wait()


def conv_second_kernel(
    params_ref, columns_hbm, first_hbm, taps_ref, out_ref, weight_ref, columns_ref, first_ref, sum_ref, sems
):
    pairs = [(columns_hbm, columns_ref), (first_hbm, first_ref)] + weight_copies(taps_ref, weight_ref)
    for copy in copy_in(pairs, sems):
        copy.wait()
    conv(columns_ref, weight_ref, params_ref, 1, ROWS, sum_ref)
    out_ref[0] = first_ref[:, 1 : 1 + ROWS]
    out_ref[1] = sum_ref[...].astype(BF16).reshape(first_ref[:, 1 : 1 + ROWS].shape)


def total_kernel(scale, terms_ref, out_ref):
    chunk = out_ref.shape[0]
    total = jnp.sum(terms_ref[...].astype(F32), axis=0)
    out_ref[...] = (total[0:chunk] * scale).reshape(chunk, 1, CH)


def call(kernel, name, args, outs, scratch=(), specs="", flops=1_000_000):
    specs = specs or "v" * len(args)
    size = sum(a.size * a.dtype.itemsize for a in args)
    space = {"k": pltpu.VMEM, "h": pltpu.HBM}
    args = [pltpu.with_memory_space_constraint(a, space[x]) if x in space else a for a, x in zip(args, specs)]
    return pl.pallas_call(
        kernel,
        out_shape=tuple(outs),
        in_specs=[{"v": VMEM, "k": VMEM, "s": SMEM, "h": HBM}[x] for x in specs],
        out_specs=tuple(HBM if getattr(o, "memory_space", None) is pltpu.HBM else VMEM for o in outs),
        scratch_shapes=list(scratch),
        compiler_params=pltpu.CompilerParams(vmem_limit_bytes=24 * 1024 * 1024),
        cost_estimate=pl.CostEstimate(flops=flops, bytes_accessed=size, transcendentals=0),
        name=name,
    )(*args)


def shape(dims, dtype=F32):
    return jax.ShapeDtypeStruct(dims, dtype)


def kept(dims, dtype=F32):
    return pltpu.VMEM(dims, dtype)


def in_hbm(dims, dtype=F32):
    return pltpu.HBM(dims, dtype)


def local(activations, pre_norm, cot_first, loss_grad, frame_clip, weight, norm_gain, norm_shift):
    dp = lax.axis_size("dp")
    me = lax.axis_index("dp")
    cells = float(dp * ROWS * COLS * PER)
    chips, chunk = dp // 2, TAPS * CH // dp
    padded = -(-chunk // 8) * 8
    other = me ^ 1
    last = lax.axis_index("segment") == lax.axis_size("segment") - 1
    flags = [me != 0, me != dp - 1, other != 0, other != dp - 1, me & 1, last]
    flags = jnp.stack([x.astype(jnp.int32) for x in flags])
    pre, act = pre_norm[0], activations[0]
    cot, loss = cot_first[0], loss_grad[0]
    taps = weight[0].reshape(3, 9, CH, CH)
    edge = (FRAMES, ROWS + 2, COLS, CH)
    strip = (FRAMES, ROWS, COLS, CH)
    bundled = (FRAMES, 3 * (ROWS + 2) + 2 * ROWS, COLS, CH)
    mates = [(i, i ^ 1) for i in range(dp)]
    columns_of = lambda rows: (FRAMES, rows * COLS, 3 * CH)
    sems = lambda n: pltpu.SemaphoreType.DMA((n,))

    def exchange(table):
        return lax.all_to_all(table, "dp", 0, 0, tiled=True)

    table, head, tail, own, plain = call(
        functools.partial(sums_kernel, cells), "sums", (frame_clip, pre, cot, loss, norm_gain, norm_shift),
        (
            shape((dp, 4, CH)), shape(edge, BF16), shape(edge, BF16),
            kept((2,) + strip), kept((PARAM_ROWS, CH)),
        ),
        scratch=[
            pltpu.SMEM((1, 2, 1, FRAMES), jnp.int32), pltpu.VMEM((2,) + strip, BF16), pltpu.VMEM(strip, BF16), sems(13)
        ],
        specs="hhhhhh",
    )
    table = exchange(table)
    down = lax.ppermute(head, "dp", [(i + 1, i) for i in range(dp - 1)])
    up = lax.ppermute(tail, "dp", [(i, i + 1) for i in range(dp - 1)])

    table, stats = call(
        act_first_kernel, "act_first", (table, own, plain), (shape((dp, 2, CH)), kept((STAT_ROWS, CH))), specs="vkk"
    )
    table = exchange(table)

    first_fields, bundle, loss_rows, params = call(
        fields_first_kernel, "fields_first", (flags, up, down, plain, stats, pre, cot, loss, act),
        (
            kept((2, FRAMES, ROWS + 4, COLS, CH)), in_hbm(bundled, BF16),
            kept(edge, BF16), kept((PARAM_ROWS, CH)),
        ),
        scratch=[pltpu.VMEM(bundled, BF16), pltpu.VMEM(strip, BF16), sems(7)],
        specs="svvkkhhhh",
    )
    other_bundle = lax.ppermute(bundle, "dp", mates)

    weights = pltpu.VMEM((3, CH, 9 * CH), BF16)
    grad_first, value = call(
        conv_first_kernel, "conv_first", (table, first_fields, params, stats, taps),
        (shape(edge, BF16), in_hbm(edge, BF16)),
        scratch=[
            pltpu.VMEM(columns_of(ROWS + 4), BF16), weights, pltpu.VMEM(edge, BF16),
            pltpu.VMEM((FRAMES, (ROWS + 2) * COLS, CH), F32), sems(10),
        ],
        specs="vkkkh", flops=20_000_000_000,
    )
    count = lax.axis_size("segment")
    hand = lax.ppermute(grad_first, "segment", [(i + 1, i) for i in range(count - 1)])

    both = pltpu.VMEM((2,) + columns_of(ROWS + 2), BF16)
    acts_dims, taps_dims = (CH, 2 * 9 * CH), (TAPS, CH, CH)
    slope, acts, weight_first = call(
        weight_first_kernel, "weight_first", (table, params, stats, value, bundle, other_bundle),
        (kept((2,) + strip), kept(acts_dims, BF16), kept(taps_dims, BF16)),
        scratch=[both, pltpu.VMEM(acts_dims, BF16)]
        + [pltpu.VMEM(edge, BF16)] + [pltpu.VMEM(bundled, BF16)] * 2 + [pltpu.VMEM((2,) + edge, F32), sems(3)],
        specs="vkkhhh",
    )

    table, incoming = call(
        act_second_kernel, "act_second", (hand, loss_rows, slope, params, stats),
        (shape((dp, 4, CH)), shape(edge, BF16)), specs="vkkkk",
    )
    table = exchange(table)
    arrived = lax.ppermute(incoming, "dp", mates)
    (second_fields,) = call(
        fields_second_kernel, "fields_second", (incoming, arrived, bundle, other_bundle, params, stats),
        (kept((2, 2) + edge),), scratch=[pltpu.VMEM(edge, BF16)] * 2 + [sems(2)], specs="vvhhkk",
    )

    terms, columns, parts = call(
        functools.partial(weight_second_kernel, 1.0 / dp, chunk), "weight_second",
        (table, second_fields, params, stats, weight_first, acts),
        (in_hbm((chips, padded, CH), BF16), in_hbm(columns_of(ROWS + 2), BF16), shape((2, CH))),
        scratch=[
            both, pltpu.VMEM((TAPS * CH, CH), F32),
            pltpu.VMEM((chips, padded, CH), BF16), sems(4),
        ],
        specs="vkkkkk",
    )
    sides = [[2 * i + core for i in range(chips)] for core in range(2)]
    terms = lax.all_to_all(terms, "dp", 0, 0, axis_index_groups=sides, tiled=True)
    (grad_weight,) = call(
        functools.partial(total_kernel, 1.0 / dp), "total", (terms,), (shape((chunk, 1, CH)),)
    )
    (grad_inputs,) = call(
        conv_second_kernel, "conv_second", (params, columns, grad_first, taps),
        (shape((2, FRAMES, ROWS, COLS, CH), BF16),),
        scratch=[
            weights, pltpu.VMEM(columns_of(ROWS + 2), BF16), pltpu.VMEM(edge, BF16),
            pltpu.VMEM((FRAMES, ROWS * COLS, CH), F32), sems(11),
        ],
        specs="khhh",
    )
    width = CH // dp
    mine = lax.dynamic_slice_in_dim(parts, me * width, width, axis=1)
    return (grad_inputs[None], grad_weight.transpose(1, 0, 2), mine[0:1], mine[1:2])


def solution(mesh):
    in_specs = (
        P("segment", None, None, "dp", None, None),
        P("segment", None, None, "dp", None, None),
        P("segment", None, "dp", None, None),
        P(None, None, "dp", None, None),
        P("segment", None, "dp", None),
        P("segment", None, None),
        P("segment", None),
        P("segment", None),
    )
    out_specs = (
        P("segment", None, None, "dp", None, None),
        P("segment", "dp", None),
        P("segment", "dp"),
        P("segment", "dp"),
    )
    return jax.shard_map(local, mesh=mesh, in_specs=in_specs, out_specs=out_specs, check_vma=False)
```

```python
import functools
import jax
import jax.numpy as jnp
from jax import lax
from jax.experimental import pallas as pl
from jax.experimental.pallas import tpu as pltpu
from jax.sharding import PartitionSpec as P

F32, BF16 = jnp.float32, jnp.bfloat16
FRAMES, ROWS, COLS, CH = 4, 4, 32, 128
GROUPS, PER = 32, 4
TAPS = 27
EPS = 1e-05
VMEM = pl.BlockSpec(memory_space=pltpu.VMEM)
SMEM = pl.BlockSpec(memory_space=pltpu.SMEM)
HBM = pl.BlockSpec(memory_space=pltpu.HBM)

GAIN, SHIFT, CORE, LAST = 0, 1, 2, 3
TURN = 24
INV, LIVE, TOP, BOTTOM, PAIR1, PAIR2 = (8 + 4 * n for n in range(6))
OTHER_TOP, OTHER_BOTTOM = 56, 60
CLIPS = 64
OTHER_TURN = 16
PARAM_ROWS = 80
MEAN0, RSTD0, MEAN1, RSTD1, GAIN_PART, SHIFT_PART = 0, 4, 8, 12, 16, 17
STAT_ROWS = 24


def iota(dim, dims=(CH, CH)):
    return lax.broadcasted_iota(jnp.int32, dims, dim)


def split_dot(rows, marks):
    count = rows.shape[0]
    high = rows.astype(BF16)
    rest = rows - high.astype(F32)
    middle = rest.astype(BF16)
    low = (rest - middle.astype(F32)).astype(BF16)
    out = jnp.dot(
        jnp.concatenate([high.astype(F32), middle.astype(F32), low.astype(F32)], axis=0).astype(BF16),
        marks,
        preferred_element_type=F32,
    )
    return out[0:count] + out[count : 2 * count] + out[2 * count : 3 * count]


def pack_rows(per_frame):
    rows = jnp.concatenate(per_frame, axis=1)
    dims = (FRAMES * CH, CH)
    marks = (iota(1, dims) == (iota(0, dims) >> 2)).astype(F32).astype(BF16)
    return split_dot(rows, marks)


def unpack_rows(table, marks):
    total = split_dot(table, marks)
    return [total[:, f * CH : (f + 1) * CH] for f in range(FRAMES)]


def row(ref, at):
    return ref[at : at + 1]


def colsum(x):
    return jnp.sum(x, axis=0, keepdims=True)


def flat(x):
    return x.reshape(-1, CH)


def act_slope(normed, gain, shift):
    act = normed * gain + shift
    sigm = jax.nn.sigmoid(act)
    return sigm * (1.0 + act * (1.0 - sigm))


def copy_in(pairs, sems):
    copies = [pltpu.make_async_copy(src, dst, sems.at[n]) for n, (src, dst) in enumerate(pairs)]
    for copy in copies:
        copy.start()
    return copies


def sums_kernel(
    cells, odd_ref, clip_hbm, pre_ref, cot_ref, loss_ref, gain_ref, shift_ref,
    out_ref, inner_ref, outer_ref, own_ref, params_ref, clip_ref, held_ref, held_cot, sems,
):
    pairs = [
        (clip_hbm, clip_ref), (pre_ref, held_ref), (cot_ref, held_cot),
        (gain_ref, params_ref.at[GAIN : GAIN + 1]), (shift_ref, params_ref.at[SHIFT : SHIFT + 1]),
    ]
    odd = odd_ref[0]
    for ref, side in ((inner_ref, 1 - odd), (outer_ref, odd)):
        two, one = pl.ds(side * (ROWS - 2), 2), pl.ds(side * (ROWS - 1), 1)
        pairs += [
            (pre_ref.at[0, :, two], ref.at[:, 0:2]), (cot_ref.at[:, two], ref.at[:, 2:4]),
            (pre_ref.at[1, :, one], ref.at[:, 4:5]), (loss_ref.at[:, one], ref.at[:, 5:6]),
        ]
    copies = copy_in(pairs, sems)
    params_ref[SHIFT + 1 :] = jnp.zeros((PARAM_ROWS - SHIFT - 1, CH), F32)

    def put(at, scalar):
        params_ref[at : at + 1] = jnp.full((1, CH), scalar, F32)

    copies[0].wait()
    for t in range(2):
        clips = [clip_ref[0, t, 0, f] for f in range(FRAMES)]
        for f in range(FRAMES):
            count = jnp.int32(0)
            for other in range(FRAMES):
                count = count + (clips[other] == clips[f]).astype(jnp.int32)
            live = (clips[f] < FRAMES).astype(F32)
            base = TURN * t + f
            params_ref[base + INV : base + INV + 1] = 1.0 / jnp.full((1, CH), count.astype(F32) * cells, F32)
            put(base + LIVE, live)
            put(CLIPS + FRAMES * t + f, clips[f].astype(F32))
            for kt, at in ((1, PAIR1), (2, PAIR2)):
                pair = live * (clips[f - kt] == clips[f]).astype(F32) if f >= kt else live * 0.0
                put(base + at, pair)
    copies[1].wait()
    per_frame = []
    for f in range(FRAMES):
        rows = []
        for t in range(2):
            x = flat(held_ref[t, f].astype(F32))
            if t == 0:
                own_ref[0, f] = x.reshape(ROWS, COLS, CH)
            rows += [colsum(x), colsum(x * x)]
        per_frame.append(jnp.concatenate(rows, axis=0))
    out_ref[...] = jnp.broadcast_to(pack_rows(per_frame)[None], out_ref.shape)
    copies[2].wait()
    own_ref[1] = held_cot[...].astype(F32)
    for copy in copies[3:]:
        copy.wait()


def clip_marks(params_ref, turn):
    slot = iota(0) >> 5
    clips = [row(params_ref, CLIPS + FRAMES * turn + f) for f in range(FRAMES)]
    clip_of_row = jnp.where(
        slot == 0, clips[0], jnp.where(slot == 1, clips[1], jnp.where(slot == 2, clips[2], clips[3]))
    )
    same_group = (iota(0) & (GROUPS - 1)) == (iota(1) >> 2)
    blocks = [(same_group & (clip_of_row == clips[f])).astype(F32).astype(BF16) for f in range(FRAMES)]
    return jnp.concatenate(blocks, axis=1)


def act_first_kernel(table_ref, own_ref, params_ref, out_ref, stats_ref):
    table = jnp.sum(table_ref[...], axis=0)
    gain, shift = row(params_ref, GAIN), row(params_ref, SHIFT)
    for t, mean_at, rstd_at in ((0, MEAN0, RSTD0), (1, MEAN1, RSTD1)):
        total = unpack_rows(table[2 * t : 2 * t + 2], clip_marks(params_ref, t))
        for f in range(FRAMES):
            inverse = row(params_ref, TURN * t + INV + f)
            mean = total[f][0:1] * inverse
            var = total[f][1:2] * inverse - mean * mean
            stats_ref[mean_at + f : mean_at + f + 1] = mean
            stats_ref[rstd_at + f : rstd_at + f + 1] = 1.0 / jnp.sqrt(var + EPS)
    per_frame = []
    gain_part = jnp.zeros((1, CH), F32)
    shift_part = jnp.zeros((1, CH), F32)
    for f in range(FRAMES):
        normed = (flat(own_ref[0, f]) - row(stats_ref, MEAN0 + f)) * row(stats_ref, RSTD0 + f)
        grad_act = flat(own_ref[1, f]) * act_slope(normed, gain, shift)
        live = row(params_ref, LIVE + f)
        plain = colsum(grad_act) * live
        times = colsum(grad_act * normed) * live
        shift_part = shift_part + plain
        gain_part = gain_part + times
        per_frame.append(jnp.concatenate([plain * gain, times * gain], axis=0))
    stats_ref[GAIN_PART : GAIN_PART + 1] = gain_part
    stats_ref[SHIFT_PART : SHIFT_PART + 1] = shift_part
    stats_ref[SHIFT_PART + 1 :] = jnp.zeros((STAT_ROWS - SHIFT_PART - 1, CH), F32)
    out_ref[...] = jnp.broadcast_to(pack_rows(per_frame)[None], out_ref.shape)


def fields(pre, incoming, mean, rstd, gain, shift, mask):
    normed = (flat(pre.astype(F32)) - mean) * rstd
    scaled = flat(incoming.astype(F32)) * act_slope(normed, gain, shift) * gain
    rstd = rstd * mask
    return scaled * rstd, normed * rstd


def fields_first_kernel(
    flag_ref, inner_ref, outer_ref, plain_ref, stats_ref, pre_ref, cot_ref, loss_ref, act_ref,
    out_ref, bundle_hbm, loss_out_ref, params_ref, bundle_ref, held_loss, up_ref, down_ref, sems,
):
    copies = copy_in(
        [
            (pre_ref.at[0], bundle_ref.at[:, 15 : 15 + ROWS]), (cot_ref, bundle_ref.at[:, 21 : 21 + ROWS]),
            (loss_ref, held_loss), (pre_ref.at[1], bundle_ref.at[:, 1 : 1 + ROWS]),
            (act_ref.at[0], bundle_ref.at[:, 6 : 6 + ROWS]),
            (act_ref.at[1], bundle_ref.at[:, 6 + ROWS : 6 + 2 * ROWS]),
        ],
        sems,
    )

    @pl.when(flag_ref[4] == 0)
    def even():
        up_ref[...] = outer_ref[...]
        down_ref[...] = inner_ref[...]

    @pl.when(flag_ref[4] != 0)
    def odd():
        up_ref[...] = inner_ref[...]
        down_ref[...] = outer_ref[...]

    params_ref[...] = plain_ref[...]
    flag = [flag_ref[n].astype(F32) for n in range(6)]
    for at, n in ((CORE, 4), (LAST, 5)):
        params_ref[at : at + 1] = jnp.full((1, CH), flag[n], F32)
    for t in range(2):
        for f in range(FRAMES):
            live = plain_ref[TURN * t + LIVE + f : TURN * t + LIVE + f + 1]
            for at, n in (
                (TURN * t + TOP, 0), (TURN * t + BOTTOM, 1),
                (OTHER_TURN * t + OTHER_TOP, 2), (OTHER_TURN * t + OTHER_BOTTOM, 3),
            ):
                params_ref[at + f : at + f + 1] = live * flag[n]
    for at, edge, below in ((0, 4, 4), (14, 1, 0), (20, 3, 2)):
        bundle_ref[:, at : at + 1] = up_ref[:, edge : edge + 1]
        bundle_ref[:, at + 1 + ROWS : at + 2 + ROWS] = down_ref[:, below : below + 1]
    for copy in copies:
        copy.wait()
    bundle_out = pltpu.make_async_copy(bundle_ref, bundle_hbm, sems.at[6])
    bundle_out.start()
    gain, shift = row(params_ref, GAIN), row(params_ref, SHIFT)
    last = row(params_ref, LAST).reshape(1, 1, 1, CH)
    loss_out_ref[:, 0:1] = (up_ref[:, 5:6].astype(F32) * last).astype(BF16)
    loss_out_ref[:, 1 : 1 + ROWS] = (held_loss[...].astype(F32) * last).astype(BF16)
    loss_out_ref[:, 1 + ROWS : 2 + ROWS] = (down_ref[:, 5:6].astype(F32) * last).astype(BF16)
    for f in range(FRAMES):
        mean, rstd = row(stats_ref, MEAN0 + f), row(stats_ref, RSTD0 + f)
        for at, count, pre, cot, mask in (
            (0, 2, up_ref[f, 0:2], up_ref[f, 2:4], TOP),
            (2, ROWS, bundle_ref[f, 15 : 15 + ROWS], bundle_ref[f, 21 : 21 + ROWS], LIVE),
            (2 + ROWS, 2, down_ref[f, 0:2], down_ref[f, 2:4], BOTTOM),
        ):
            pair = fields(pre, cot, mean, rstd, gain, shift, row(params_ref, mask + f))
            for n in range(2):
                out_ref[n, f, at : at + count] = pair[n].reshape(count, COLS, CH)
    bundle_out.wait()


def write_columns(store, table, fields_ref, at_fields, params_ref, stats_ref, rstd_at, turn, halo, masks):
    total = unpack_rows(table, clip_marks(params_ref, turn))
    rows = ROWS + 2 * halo
    column = iota(0, (rows * COLS, CH)) & (COLS - 1)
    for f in range(FRAMES):
        inverse = row(params_ref, TURN * turn + INV + f)
        avg_a = total[f][0:1] * inverse * row(stats_ref, rstd_at + f)
        avg_b = total[f][1:2] * inverse
        pieces = []
        for mask, at, count in ((masks[0], 0, halo), (masks[1], halo, ROWS), (masks[2], halo + ROWS, halo)):
            scaled = flat(fields_ref[at_fields + (0, f, slice(at, at + count))])
            normed = flat(fields_ref[at_fields + (1, f, slice(at, at + count))])
            pieces.append(scaled - avg_a * row(params_ref, mask + f) - normed * avg_b)
        value = jnp.concatenate(pieces, axis=0)
        left = jnp.where(column == COLS - 1, 0.0, pltpu.roll(value, rows * COLS - 1, 0))
        right = jnp.where(column == 0, 0.0, pltpu.roll(value, 1, 0))
        store(f, left.astype(BF16), value.astype(BF16), right.astype(BF16))


def store_columns(ref, prefix=()):
    def store(f, left, value, right):
        for n, x in enumerate((left, value, right)):
            ref[prefix + (f, slice(None), slice(n * CH, (n + 1) * CH))] = x

    return store


def conv(columns_ref, weight_ref, params_ref, turn, rows, sum_ref):
    size = rows * COLS
    for kt in range(3):
        count = FRAMES - kt
        blocks = [
            columns_ref[kt:FRAMES, start : start + size, :].reshape(count * size, 3 * CH)
            for start in (2 * COLS, COLS, 0)
        ]
        part = lax.dot_general(
            jnp.concatenate(blocks, axis=1), weight_ref[kt], (((1,), (1,)), ((), ())), preferred_element_type=F32
        )
        for f in range(count):
            mine = part[f * size : (f + 1) * size]
            if kt:
                mine = mine * row(params_ref, TURN * turn + (PAIR1 if kt == 1 else PAIR2) + f + kt)
                sum_ref[f] = sum_ref[f] + mine
            else:
                sum_ref[f] = mine


def weight_copies(taps_ref, weight_ref):
    return [(taps_ref.at[:, n], weight_ref.at[:, :, n * CH : (n + 1) * CH]) for n in range(9)]


def conv_first_kernel(
    table_ref, fields_ref, params_ref, stats_ref, taps_hbm, grad_ref, value_hbm,
    columns_ref, taps_ref, weight_ref, value_ref, sum_ref, sems,
):
    (copy,) = copy_in([(taps_hbm, taps_ref)], sems)
    table = jnp.sum(table_ref[...], axis=0)
    fill = store_columns(columns_ref)

    def store(f, left, value, right):
        fill(f, left, value, right)
        value_ref[f] = value[COLS : COLS * (ROWS + 3)].reshape(ROWS + 2, COLS, CH)

    write_columns(
        store, table, fields_ref, (), params_ref, stats_ref, RSTD0, 0, 2, (TOP, LIVE, BOTTOM)
    )
    value_out = pltpu.make_async_copy(value_ref, value_hbm, sems.at[1])
    value_out.start()
    copy.wait()
    for kt in range(3):
        for n in range(9):
            weight_ref[kt, :, n * CH : (n + 1) * CH] = taps_ref[kt, n]
    conv(columns_ref, weight_ref, params_ref, 0, ROWS + 2, sum_ref)
    grad_ref[...] = sum_ref[...].astype(BF16).reshape(grad_ref.shape)
    value_out.wait()


def put_acts(turn, bundle_ref, other_ref, params_ref, out_ref):
    for strip, ref in enumerate((bundle_ref, other_ref)):
        for f in range(FRAMES):
            x = flat(ref[f, 6 + ROWS * turn : 6 + ROWS * (turn + 1)].astype(F32)).T
            for kt in range(min(3, FRAMES - f)):
                at = CH * (2 * sum(FRAMES - n for n in range(kt)) + strip * (FRAMES - kt) + f)
                y = x if kt == 0 else x * row(params_ref, TURN * turn + (PAIR1 if kt == 1 else PAIR2) + f + kt)
                out_ref[:, at : at + CH] = y.astype(BF16)


def kernel_terms(columns_ref, act_ref, kt):
    count = FRAMES - kt
    blocks = [
        columns_ref[:, kt:FRAMES, start : start + ROWS * COLS, :].reshape(2 * count * CH, 3 * CH)
        for start in (2 * COLS, COLS, 0)
    ]
    at = 2 * CH * sum(FRAMES - n for n in range(kt))
    return jnp.dot(
        act_ref[:, at : at + 2 * count * CH], jnp.concatenate(blocks, axis=1), preferred_element_type=F32
    )


def act_second_kernel(hand_ref, loss_ref, slope_ref, params_ref, stats_ref, out_ref, incoming_ref):
    gain = row(params_ref, GAIN)
    per_frame = []
    gain_part = row(stats_ref, GAIN_PART)
    shift_part = row(stats_ref, SHIFT_PART)
    for f in range(FRAMES):
        incoming = hand_ref[f].astype(F32) + loss_ref[f].astype(F32)
        incoming_ref[f] = incoming.astype(BF16)
        grad_act = flat(incoming[1 : 1 + ROWS]) * flat(slope_ref[0, f])
        live = row(params_ref, TURN + LIVE + f)
        plain = colsum(grad_act) * live
        times = colsum(grad_act * flat(slope_ref[1, f])) * live
        shift_part = shift_part + plain
        gain_part = gain_part + times
        per_frame.append(jnp.concatenate([plain * gain, times * gain], axis=0))
    rows = jnp.concatenate([pack_rows(per_frame), gain_part, shift_part], axis=0)
    out_ref[...] = jnp.broadcast_to(rows[None], out_ref.shape)


def weight_first_kernel(
    table_ref, params_ref, stats_ref, value_hbm, bundle_hbm, other_hbm,
    slope_ref, act_ref, first_ref,
    columns_ref, act_first_ref, value_ref, bundle_ref, other_ref, fields_ref, sems,
):
    copies = copy_in([(bundle_hbm, bundle_ref), (other_hbm, other_ref), (value_hbm, value_ref)], sems)
    table = jnp.sum(table_ref[...], axis=0)
    gain, shift = row(params_ref, GAIN), row(params_ref, SHIFT)
    copies[0].wait()
    for f in range(FRAMES):
        normed = flat(bundle_ref[f, 1 : 1 + ROWS].astype(F32)) - row(stats_ref, MEAN1 + f)
        normed = normed * row(stats_ref, RSTD1 + f)
        slope_ref[0, f] = act_slope(normed, gain, shift).reshape(ROWS, COLS, CH)
        slope_ref[1, f] = normed.reshape(ROWS, COLS, CH)
    copies[1].wait()
    put_acts(0, bundle_ref, other_ref, params_ref, act_first_ref)
    put_acts(1, bundle_ref, other_ref, params_ref, act_ref)
    for f in range(FRAMES):
        mean, rstd = row(stats_ref, MEAN0 + f), row(stats_ref, RSTD0 + f)
        for at, count, mask in ((0, 1, OTHER_TOP), (1, ROWS, LIVE), (1 + ROWS, 1, OTHER_BOTTOM)):
            pair = fields(
                other_ref[f, 14 + at : 14 + at + count], other_ref[f, 20 + at : 20 + at + count], mean, rstd,
                gain, shift, row(params_ref, mask + f),
            )
            for n in range(2):
                fields_ref[n, f, at : at + count] = pair[n].reshape(count, COLS, CH)
    write_columns(
        store_columns(columns_ref, (1,)), table, fields_ref, (), params_ref, stats_ref, RSTD0, 0, 1,
        (OTHER_TOP, LIVE, OTHER_BOTTOM),
    )
    copies[2].wait()
    rows = ROWS + 2
    column = iota(0, (rows * COLS, CH)) & (COLS - 1)
    fill = store_columns(columns_ref, (0,))
    for f in range(FRAMES):
        value = flat(value_ref[f].astype(F32))
        left = jnp.where(column == COLS - 1, 0.0, pltpu.roll(value, rows * COLS - 1, 0))
        right = jnp.where(column == 0, 0.0, pltpu.roll(value, 1, 0))
        fill(f, left.astype(BF16), value.astype(BF16), right.astype(BF16))
    for kt in range(3):
        terms = kernel_terms(columns_ref, act_first_ref, kt)
        for n in range(9):
            first_ref[9 * kt + n] = terms[:, n * CH : (n + 1) * CH].astype(first_ref.dtype)


def fields_second_kernel(
    incoming_ref, arrived_ref, bundle_hbm, other_hbm, params_ref, stats_ref, out_ref, bundle_ref, other_ref, sems,
):
    pre_part = slice(0, ROWS + 2)
    copies = copy_in(
        [(bundle_hbm.at[:, pre_part], bundle_ref), (other_hbm.at[:, pre_part], other_ref)], sems
    )
    for copy in copies:
        copy.wait()
    gain, shift = row(params_ref, GAIN), row(params_ref, SHIFT)
    for f in range(FRAMES):
        mean, rstd = row(stats_ref, MEAN1 + f), row(stats_ref, RSTD1 + f)
        for strip, pre_ref, come_ref, top, bottom in (
            (0, bundle_ref, incoming_ref, TURN + TOP, TURN + BOTTOM),
            (1, other_ref, arrived_ref, OTHER_TURN + OTHER_TOP, OTHER_TURN + OTHER_BOTTOM),
        ):
            for at, count, mask in ((0, 1, top), (1, ROWS, TURN + LIVE), (1 + ROWS, 1, bottom)):
                pair = fields(
                    pre_ref[f, at : at + count], come_ref[f, at : at + count], mean, rstd, gain, shift,
                    row(params_ref, mask + f),
                )
                for n in range(2):
                    out_ref[strip, n, f, at : at + count] = pair[n].reshape(count, COLS, CH)


def weight_second_kernel(
    scale, chunk, table_ref, fields_ref, params_ref, stats_ref, first_ref, act_ref,
    out_hbm, own_hbm, parts_ref, columns_ref, sum_ref, out_ref, sems,
):
    table = jnp.sum(table_ref[...], axis=0)
    parts_ref[...] = table[2:4] * scale
    for strip, top, bottom in ((0, TURN + TOP, TURN + BOTTOM), (1, OTHER_TURN + OTHER_TOP, OTHER_TURN + OTHER_BOTTOM)):
        write_columns(
            store_columns(columns_ref, (strip,)), table[0:2], fields_ref, (strip,), params_ref, stats_ref,
            RSTD1, 1, 1, (top, TURN + LIVE, bottom),
        )
    copy_own = pltpu.make_async_copy(columns_ref.at[0], own_hbm, sems.at[0])
    copy_own.start()
    second = row(params_ref, CORE) > 0.5
    filler = jnp.zeros((out_ref.shape[1] - chunk, CH), F32)
    chips = out_ref.shape[0]
    done = 0
    copies = [copy_own]
    for kt in range(3):
        terms = kernel_terms(columns_ref, act_ref, kt)
        for n in range(9 * kt, 9 * kt + 9):
            at = (n - 9 * kt) * CH
            sum_ref[n * CH : (n + 1) * CH] = first_ref[n].astype(F32) + terms[:, at : at + CH]
        begin = done
        while done < chips and 2 * (done + 1) * chunk <= 9 * (kt + 1) * CH:
            at = 2 * done * chunk
            mine = jnp.where(second, sum_ref[at + chunk : at + 2 * chunk], sum_ref[at : at + chunk])
            if filler.shape[0]:
                mine = jnp.concatenate([mine, filler], axis=0)
            out_ref[done] = mine.astype(BF16)
            done += 1
        if done > begin:
            send = pltpu.make_async_copy(out_ref.at[begin:done], out_hbm.at[begin:done], sems.at[1 + kt])
            send.start()
            copies.append(send)
    for copy in copies:
        copy.wait()


def conv_second_kernel(
    params_ref, columns_hbm, first_hbm, taps_ref, out_ref, weight_ref, columns_ref, first_ref, sum_ref, sems
):
    pairs = [(columns_hbm, columns_ref), (first_hbm, first_ref)] + weight_copies(taps_ref, weight_ref)
    for copy in copy_in(pairs, sems):
        copy.wait()
    conv(columns_ref, weight_ref, params_ref, 1, ROWS, sum_ref)
    out_ref[0] = first_ref[:, 1 : 1 + ROWS]
    out_ref[1] = sum_ref[...].astype(BF16).reshape(first_ref[:, 1 : 1 + ROWS].shape)


def total_kernel(scale, terms_ref, out_ref):
    chunk = out_ref.shape[0]
    total = jnp.sum(terms_ref[...].astype(F32), axis=0)
    out_ref[...] = (total[0:chunk] * scale).reshape(chunk, 1, CH)


def call(kernel, name, args, outs, scratch=(), specs="", flops=1_000_000):
    specs = specs or "v" * len(args)
    size = sum(a.size * a.dtype.itemsize for a in args)
    space = {"k": pltpu.VMEM, "h": pltpu.HBM}
    args = [pltpu.with_memory_space_constraint(a, space[x]) if x in space else a for a, x in zip(args, specs)]
    return pl.pallas_call(
        kernel,
        out_shape=tuple(outs),
        in_specs=[{"v": VMEM, "k": VMEM, "s": SMEM, "h": HBM}[x] for x in specs],
        out_specs=tuple(HBM if getattr(o, "memory_space", None) is pltpu.HBM else VMEM for o in outs),
        scratch_shapes=list(scratch),
        compiler_params=pltpu.CompilerParams(vmem_limit_bytes=24 * 1024 * 1024),
        cost_estimate=pl.CostEstimate(flops=flops, bytes_accessed=size, transcendentals=0),
        name=name,
    )(*args)


def shape(dims, dtype=F32):
    return jax.ShapeDtypeStruct(dims, dtype)


def kept(dims, dtype=F32):
    return pltpu.VMEM(dims, dtype)


def in_hbm(dims, dtype=F32):
    return pltpu.HBM(dims, dtype)


def local(activations, pre_norm, cot_first, loss_grad, frame_clip, weight, norm_gain, norm_shift):
    dp = lax.axis_size("dp")
    me = lax.axis_index("dp")
    cells = float(dp * ROWS * COLS * PER)
    chips, chunk = dp // 2, TAPS * CH // dp
    padded = -(-chunk // 8) * 8
    other = me ^ 1
    last = lax.axis_index("segment") == lax.axis_size("segment") - 1
    flags = [me != 0, me != dp - 1, other != 0, other != dp - 1, me & 1, last]
    flags = jnp.stack([x.astype(jnp.int32) for x in flags])
    pre, act = pre_norm[0], activations[0]
    cot, loss = cot_first[0], loss_grad[0]
    taps = weight[0].reshape(3, 9, CH, CH)
    edge = (FRAMES, ROWS + 2, COLS, CH)
    strip = (FRAMES, ROWS, COLS, CH)
    bundled = (FRAMES, 3 * (ROWS + 2) + 2 * ROWS, COLS, CH)
    mates = [(i, i ^ 1) for i in range(dp)]
    columns_of = lambda rows: (FRAMES, rows * COLS, 3 * CH)
    sems = lambda n: pltpu.SemaphoreType.DMA((n,))

    def exchange(table):
        return lax.all_to_all(table, "dp", 0, 0, tiled=True)

    table, inner, outer, own, plain = call(
        functools.partial(sums_kernel, cells), "sums", ((me & 1).reshape(1), frame_clip, pre, cot, loss, norm_gain, norm_shift),
        (
            shape((dp, 4, CH)), shape(edge, BF16), shape(edge, BF16),
            kept((2,) + strip), kept((PARAM_ROWS, CH)),
        ),
        scratch=[
            pltpu.SMEM((1, 2, 1, FRAMES), jnp.int32), pltpu.VMEM((2,) + strip, BF16), pltpu.VMEM(strip, BF16), sems(13)
        ],
        specs="shhhhhh",
    )
    table = exchange(table)
    inner = lax.ppermute(inner, "dp", mates)
    sides = [(i, i + 1) for i in range(1, dp - 1, 2)]
    outer = lax.ppermute(outer, "dp", sides + [(j, i) for i, j in sides])

    table, stats = call(
        act_first_kernel, "act_first", (table, own, plain), (shape((dp, 2, CH)), kept((STAT_ROWS, CH))), specs="vkk"
    )
    table = exchange(table)

    first_fields, bundle, loss_rows, params = call(
        fields_first_kernel, "fields_first", (flags, inner, outer, plain, stats, pre, cot, loss, act),
        (
            kept((2, FRAMES, ROWS + 4, COLS, CH)), in_hbm(bundled, BF16),
            kept(edge, BF16), kept((PARAM_ROWS, CH)),
        ),
        scratch=[pltpu.VMEM(bundled, BF16), pltpu.VMEM(strip, BF16)] + [pltpu.VMEM(edge, BF16)] * 2 + [sems(7)],
        specs="svvkkhhhh",
    )
    other_bundle = lax.ppermute(bundle, "dp", mates)

    weights = pltpu.VMEM((3, CH, 9 * CH), BF16)
    grad_first, value = call(
        conv_first_kernel, "conv_first", (table, first_fields, params, stats, taps),
        (shape(edge, BF16), in_hbm(edge, BF16)),
        scratch=[
            pltpu.VMEM(columns_of(ROWS + 4), BF16), pltpu.VMEM((3, 9, CH, CH), BF16), weights, pltpu.VMEM(edge, BF16),
            pltpu.VMEM((FRAMES, (ROWS + 2) * COLS, CH), F32), sems(2),
        ],
        specs="vkkkh", flops=20_000_000_000,
    )
    count = lax.axis_size("segment")
    hand = lax.ppermute(grad_first, "segment", [(i + 1, i) for i in range(count - 1)])

    both = pltpu.VMEM((2,) + columns_of(ROWS + 2), BF16)
    acts_dims, taps_dims = (CH, 2 * 9 * CH), (TAPS, CH, CH)
    slope, acts, weight_first = call(
        weight_first_kernel, "weight_first", (table, params, stats, value, bundle, other_bundle),
        (kept((2,) + strip), kept(acts_dims, BF16), kept(taps_dims, BF16)),
        scratch=[both, pltpu.VMEM(acts_dims, BF16)]
        + [pltpu.VMEM(edge, BF16)] + [pltpu.VMEM(bundled, BF16)] * 2 + [pltpu.VMEM((2,) + edge, F32), sems(3)],
        specs="vkkhhh",
    )

    table, incoming = call(
        act_second_kernel, "act_second", (hand, loss_rows, slope, params, stats),
        (shape((dp, 4, CH)), shape(edge, BF16)), specs="vkkkk",
    )
    table = exchange(table)
    arrived = lax.ppermute(incoming, "dp", mates)
    (second_fields,) = call(
        fields_second_kernel, "fields_second", (incoming, arrived, bundle, other_bundle, params, stats),
        (kept((2, 2) + edge),), scratch=[pltpu.VMEM(edge, BF16)] * 2 + [sems(2)], specs="vvhhkk",
    )

    terms, columns, parts = call(
        functools.partial(weight_second_kernel, 1.0 / dp, chunk), "weight_second",
        (table, second_fields, params, stats, weight_first, acts),
        (in_hbm((chips, padded, CH), BF16), in_hbm(columns_of(ROWS + 2), BF16), shape((2, CH))),
        scratch=[
            both, pltpu.VMEM((TAPS * CH, CH), F32),
            pltpu.VMEM((chips, padded, CH), BF16), sems(4),
        ],
        specs="vkkkkk",
    )
    sides = [[2 * i + core for i in range(chips)] for core in range(2)]
    terms = lax.all_to_all(terms, "dp", 0, 0, axis_index_groups=sides, tiled=True)
    (grad_weight,) = call(
        functools.partial(total_kernel, 1.0 / dp), "total", (terms,), (shape((chunk, 1, CH)),)
    )
    (grad_inputs,) = call(
        conv_second_kernel, "conv_second", (params, columns, grad_first, taps),
        (shape((2, FRAMES, ROWS, COLS, CH), BF16),),
        scratch=[
            weights, pltpu.VMEM(columns_of(ROWS + 2), BF16), pltpu.VMEM(edge, BF16),
            pltpu.VMEM((FRAMES, ROWS * COLS, CH), F32), sems(11),
        ],
        specs="khhh",
    )
    width = CH // dp
    mine = lax.dynamic_slice_in_dim(parts, me * width, width, axis=1)
    return (grad_inputs[None], grad_weight.transpose(1, 0, 2), mine[0:1], mine[1:2])


def solution(mesh):
    in_specs = (
        P("segment", None, None, "dp", None, None),
        P("segment", None, None, "dp", None, None),
        P("segment", None, "dp", None, None),
        P(None, None, "dp", None, None),
        P("segment", None, "dp", None),
        P("segment", None, None),
        P("segment", None),
        P("segment", None),
    )
    out_specs = (
        P("segment", None, None, "dp", None, None),
        P("segment", "dp", None),
        P("segment", "dp"),
        P("segment", "dp"),
    )
    return jax.shard_map(local, mesh=mesh, in_specs=in_specs, out_specs=out_specs, check_vma=False)
```

```python
import functools
import jax
import jax.numpy as jnp
from jax import lax
from jax.experimental import pallas as pl
from jax.experimental.pallas import tpu as pltpu
from jax.sharding import PartitionSpec as P

F32, BF16 = jnp.float32, jnp.bfloat16
FRAMES, ROWS, COLS, CH = 4, 4, 32, 128
GROUPS, PER = 32, 4
TAPS = 27
EPS = 1e-05
VMEM = pl.BlockSpec(memory_space=pltpu.VMEM)
SMEM = pl.BlockSpec(memory_space=pltpu.SMEM)
HBM = pl.BlockSpec(memory_space=pltpu.HBM)

GAIN, SHIFT, CORE, LAST = 0, 1, 2, 3
TURN = 24
INV, LIVE, TOP, BOTTOM, PAIR1, PAIR2 = (8 + 4 * n for n in range(6))
OTHER_TOP, OTHER_BOTTOM = 56, 60
CLIPS = 64
OTHER_TURN = 16
PARAM_ROWS = 80
MEAN0, RSTD0, MEAN1, RSTD1, GAIN_PART, SHIFT_PART = 0, 4, 8, 12, 16, 17
STAT_ROWS = 24


def iota(dim, dims=(CH, CH)):
    return lax.broadcasted_iota(jnp.int32, dims, dim)


def split_dot(rows, marks):
    count = rows.shape[0]
    high = rows.astype(BF16)
    rest = rows - high.astype(F32)
    middle = rest.astype(BF16)
    low = (rest - middle.astype(F32)).astype(BF16)
    out = jnp.dot(
        jnp.concatenate([high.astype(F32), middle.astype(F32), low.astype(F32)], axis=0).astype(BF16),
        marks,
        preferred_element_type=F32,
    )
    return out[0:count] + out[count : 2 * count] + out[2 * count : 3 * count]


def pack_rows(per_frame):
    rows = jnp.concatenate(per_frame, axis=1)
    dims = (FRAMES * CH, CH)
    marks = (iota(1, dims) == (iota(0, dims) >> 2)).astype(F32).astype(BF16)
    return split_dot(rows, marks)


def unpack_rows(table, marks):
    total = split_dot(table, marks)
    return [total[:, f * CH : (f + 1) * CH] for f in range(FRAMES)]


def row(ref, at):
    return ref[at : at + 1]


def colsum(x):
    return jnp.sum(x, axis=0, keepdims=True)


def flat(x):
    return x.reshape(-1, CH)


def act_slope(normed, gain, shift):
    act = normed * gain + shift
    sigm = jax.nn.sigmoid(act)
    return sigm * (1.0 + act * (1.0 - sigm))


def copy_in(pairs, sems):
    copies = [pltpu.make_async_copy(src, dst, sems.at[n]) for n, (src, dst) in enumerate(pairs)]
    for copy in copies:
        copy.start()
    return copies


def sums_kernel(
    cells, odd_ref, clip_hbm, pre_ref, cot_ref, loss_ref, gain_ref, shift_ref,
    out_ref, inner_ref, outer_ref, own_ref, params_ref, clip_ref, held_ref, held_cot, sems,
):
    pairs = [
        (clip_hbm, clip_ref), (pre_ref, held_ref), (cot_ref, held_cot),
        (gain_ref, params_ref.at[GAIN : GAIN + 1]), (shift_ref, params_ref.at[SHIFT : SHIFT + 1]),
    ]
    odd = odd_ref[0]
    for ref, side in ((inner_ref, 1 - odd), (outer_ref, odd)):
        two, one = pl.ds(side * (ROWS - 2), 2), pl.ds(side * (ROWS - 1), 1)
        pairs += [
            (pre_ref.at[0, :, two], ref.at[:, 0:2]), (cot_ref.at[:, two], ref.at[:, 2:4]),
            (pre_ref.at[1, :, one], ref.at[:, 4:5]), (loss_ref.at[:, one], ref.at[:, 5:6]),
        ]
    copies = copy_in(pairs, sems)
    params_ref[SHIFT + 1 :] = jnp.zeros((PARAM_ROWS - SHIFT - 1, CH), F32)

    def put(at, scalar):
        params_ref[at : at + 1] = jnp.full((1, CH), scalar, F32)

    copies[0].wait()
    for t in range(2):
        clips = [clip_ref[0, t, 0, f] for f in range(FRAMES)]
        for f in range(FRAMES):
            count = jnp.int32(0)
            for other in range(FRAMES):
                count = count + (clips[other] == clips[f]).astype(jnp.int32)
            live = (clips[f] < FRAMES).astype(F32)
            base = TURN * t + f
            params_ref[base + INV : base + INV + 1] = 1.0 / jnp.full((1, CH), count.astype(F32) * cells, F32)
            put(base + LIVE, live)
            put(CLIPS + FRAMES * t + f, clips[f].astype(F32))
            for kt, at in ((1, PAIR1), (2, PAIR2)):
                pair = live * (clips[f - kt] == clips[f]).astype(F32) if f >= kt else live * 0.0
                put(base + at, pair)
    copies[1].wait()
    per_frame = []
    for f in range(FRAMES):
        rows = []
        for t in range(2):
            x = flat(held_ref[t, f].astype(F32))
            if t == 0:
                own_ref[0, f] = x.reshape(ROWS, COLS, CH)
            rows += [colsum(x), colsum(x * x)]
        per_frame.append(jnp.concatenate(rows, axis=0))
    out_ref[...] = jnp.broadcast_to(pack_rows(per_frame)[None], out_ref.shape)
    copies[2].wait()
    own_ref[1] = held_cot[...].astype(F32)
    for copy in copies[3:]:
        copy.wait()


def clip_marks(params_ref, turn):
    slot = iota(0) >> 5
    clips = [row(params_ref, CLIPS + FRAMES * turn + f) for f in range(FRAMES)]
    clip_of_row = jnp.where(
        slot == 0, clips[0], jnp.where(slot == 1, clips[1], jnp.where(slot == 2, clips[2], clips[3]))
    )
    same_group = (iota(0) & (GROUPS - 1)) == (iota(1) >> 2)
    blocks = [(same_group & (clip_of_row == clips[f])).astype(F32).astype(BF16) for f in range(FRAMES)]
    return jnp.concatenate(blocks, axis=1)


def act_first_kernel(table_ref, own_ref, params_ref, out_ref, stats_ref):
    table = jnp.sum(table_ref[...], axis=0)
    gain, shift = row(params_ref, GAIN), row(params_ref, SHIFT)
    for t, mean_at, rstd_at in ((0, MEAN0, RSTD0), (1, MEAN1, RSTD1)):
        total = unpack_rows(table[2 * t : 2 * t + 2], clip_marks(params_ref, t))
        for f in range(FRAMES):
            inverse = row(params_ref, TURN * t + INV + f)
            mean = total[f][0:1] * inverse
            var = total[f][1:2] * inverse - mean * mean
            stats_ref[mean_at + f : mean_at + f + 1] = mean
            stats_ref[rstd_at + f : rstd_at + f + 1] = 1.0 / jnp.sqrt(var + EPS)
    per_frame = []
    gain_part = jnp.zeros((1, CH), F32)
    shift_part = jnp.zeros((1, CH), F32)
    for f in range(FRAMES):
        normed = (flat(own_ref[0, f]) - row(stats_ref, MEAN0 + f)) * row(stats_ref, RSTD0 + f)
        grad_act = flat(own_ref[1, f]) * act_slope(normed, gain, shift)
        live = row(params_ref, LIVE + f)
        plain = colsum(grad_act) * live
        times = colsum(grad_act * normed) * live
        shift_part = shift_part + plain
        gain_part = gain_part + times
        per_frame.append(jnp.concatenate([plain * gain, times * gain], axis=0))
    stats_ref[GAIN_PART : GAIN_PART + 1] = gain_part
    stats_ref[SHIFT_PART : SHIFT_PART + 1] = shift_part
    stats_ref[SHIFT_PART + 1 :] = jnp.zeros((STAT_ROWS - SHIFT_PART - 1, CH), F32)
    out_ref[...] = jnp.broadcast_to(pack_rows(per_frame)[None], out_ref.shape)


def fields(pre, incoming, mean, rstd, gain, shift, mask):
    normed = (flat(pre.astype(F32)) - mean) * rstd
    scaled = flat(incoming.astype(F32)) * act_slope(normed, gain, shift) * gain
    rstd = rstd * mask
    return scaled * rstd, normed * rstd


def fields_first_kernel(
    flag_ref, inner_ref, outer_ref, plain_ref, stats_ref, pre_ref, cot_ref, loss_ref, act_ref,
    out_ref, bundle_hbm, loss_out_ref, params_ref, bundle_ref, held_loss, up_ref, down_ref, sems,
):
    copies = copy_in(
        [
            (pre_ref.at[0], bundle_ref.at[:, 15 : 15 + ROWS]), (cot_ref, bundle_ref.at[:, 21 : 21 + ROWS]),
            (loss_ref, held_loss), (pre_ref.at[1], bundle_ref.at[:, 1 : 1 + ROWS]),
            (act_ref.at[0], bundle_ref.at[:, 6 : 6 + ROWS]),
            (act_ref.at[1], bundle_ref.at[:, 6 + ROWS : 6 + 2 * ROWS]),
        ],
        sems,
    )

    @pl.when(flag_ref[4] == 0)
    def even():
        up_ref[...] = outer_ref[...]
        down_ref[...] = inner_ref[...]

    @pl.when(flag_ref[4] != 0)
    def odd():
        up_ref[...] = inner_ref[...]
        down_ref[...] = outer_ref[...]

    params_ref[...] = plain_ref[...]
    flag = [flag_ref[n].astype(F32) for n in range(6)]
    for at, n in ((CORE, 4), (LAST, 5)):
        params_ref[at : at + 1] = jnp.full((1, CH), flag[n], F32)
    for t in range(2):
        for f in range(FRAMES):
            live = plain_ref[TURN * t + LIVE + f : TURN * t + LIVE + f + 1]
            for at, n in (
                (TURN * t + TOP, 0), (TURN * t + BOTTOM, 1),
                (OTHER_TURN * t + OTHER_TOP, 2), (OTHER_TURN * t + OTHER_BOTTOM, 3),
            ):
                params_ref[at + f : at + f + 1] = live * flag[n]
    for at, edge, below in ((0, 4, 4), (14, 1, 0), (20, 3, 2)):
        bundle_ref[:, at : at + 1] = up_ref[:, edge : edge + 1]
        bundle_ref[:, at + 1 + ROWS : at + 2 + ROWS] = down_ref[:, below : below + 1]
    for copy in copies:
        copy.wait()
    bundle_out = pltpu.make_async_copy(bundle_ref, bundle_hbm, sems.at[6])
    bundle_out.start()
    gain, shift = row(params_ref, GAIN), row(params_ref, SHIFT)
    last = row(params_ref, LAST).reshape(1, 1, 1, CH)
    loss_out_ref[:, 0:ROWS] = (held_loss[...].astype(F32) * last).astype(BF16)
    loss_out_ref[:, ROWS : ROWS + 1] = (outer_ref[:, 5:6].astype(F32) * last).astype(BF16)
    for f in range(FRAMES):
        mean, rstd = row(stats_ref, MEAN0 + f), row(stats_ref, RSTD0 + f)
        for at, count, pre, cot, mask in (
            (0, 2, up_ref[f, 0:2], up_ref[f, 2:4], TOP),
            (2, ROWS, bundle_ref[f, 15 : 15 + ROWS], bundle_ref[f, 21 : 21 + ROWS], LIVE),
            (2 + ROWS, 2, down_ref[f, 0:2], down_ref[f, 2:4], BOTTOM),
        ):
            pair = fields(pre, cot, mean, rstd, gain, shift, row(params_ref, mask + f))
            for n in range(2):
                out_ref[n, f, at : at + count] = pair[n].reshape(count, COLS, CH)
    bundle_out.wait()


def write_columns(store, table, fields_ref, at_fields, params_ref, stats_ref, rstd_at, turn, halo, masks):
    total = unpack_rows(table, clip_marks(params_ref, turn))
    rows = ROWS + 2 * halo
    column = iota(0, (rows * COLS, CH)) & (COLS - 1)
    for f in range(FRAMES):
        inverse = row(params_ref, TURN * turn + INV + f)
        avg_a = total[f][0:1] * inverse * row(stats_ref, rstd_at + f)
        avg_b = total[f][1:2] * inverse
        pieces = []
        for mask, at, count in ((masks[0], 0, halo), (masks[1], halo, ROWS), (masks[2], halo + ROWS, halo)):
            scaled = flat(fields_ref[at_fields + (0, f, slice(at, at + count))])
            normed = flat(fields_ref[at_fields + (1, f, slice(at, at + count))])
            pieces.append(scaled - avg_a * row(params_ref, mask + f) - normed * avg_b)
        value = jnp.concatenate(pieces, axis=0)
        left = jnp.where(column == COLS - 1, 0.0, pltpu.roll(value, rows * COLS - 1, 0))
        right = jnp.where(column == 0, 0.0, pltpu.roll(value, 1, 0))
        store(f, left.astype(BF16), value.astype(BF16), right.astype(BF16))


def store_columns(ref, prefix=()):
    def store(f, left, value, right):
        for n, x in enumerate((left, value, right)):
            ref[prefix + (f, slice(None), slice(n * CH, (n + 1) * CH))] = x

    return store


def conv(columns_ref, weight_ref, params_ref, turn, rows, sum_ref):
    size = rows * COLS
    for kt in range(3):
        count = FRAMES - kt
        part = None
        for dy in range(3):
            start = (2 - dy) * COLS
            term = lax.dot_general(
                columns_ref[kt:FRAMES, start : start + size, :].reshape(count * size, 3 * CH),
                weight_ref[kt, :, 3 * dy * CH : 3 * (dy + 1) * CH], (((1,), (1,)), ((), ())),
                preferred_element_type=F32,
            )
            part = term if part is None else part + term
        for f in range(count):
            mine = part[f * size : (f + 1) * size]
            if kt:
                mine = mine * row(params_ref, TURN * turn + (PAIR1 if kt == 1 else PAIR2) + f + kt)
                sum_ref[f] = sum_ref[f] + mine
            else:
                sum_ref[f] = mine


def weight_copies(taps_ref, weight_ref):
    return [(taps_ref.at[:, n], weight_ref.at[:, :, n * CH : (n + 1) * CH]) for n in range(9)]


def conv_first_kernel(
    table_ref, fields_ref, params_ref, stats_ref, taps_hbm, grad_ref, value_hbm,
    columns_ref, taps_ref, weight_ref, value_ref, sum_ref, sems,
):
    (copy,) = copy_in([(taps_hbm, taps_ref)], sems)
    table = jnp.sum(table_ref[...], axis=0)
    fill = store_columns(columns_ref)

    def store(f, left, value, right):
        fill(f, left, value, right)
        value_ref[f] = value[COLS : COLS * (ROWS + 3)].reshape(ROWS + 2, COLS, CH)

    write_columns(
        store, table, fields_ref, (), params_ref, stats_ref, RSTD0, 0, 2, (TOP, LIVE, BOTTOM)
    )
    value_out = pltpu.make_async_copy(value_ref, value_hbm, sems.at[1])
    value_out.start()
    copy.wait()
    for kt in range(3):
        for n in range(9):
            weight_ref[kt, :, n * CH : (n + 1) * CH] = taps_ref[kt, n]
    conv(columns_ref, weight_ref, params_ref, 0, ROWS + 2, sum_ref)
    second = row(params_ref, CORE) > 0.5
    for f in range(FRAMES):
        grad_ref[f, 0:ROWS] = sum_ref[f, COLS : COLS * (ROWS + 1)].astype(BF16).reshape(ROWS, COLS, CH)
        outer = jnp.where(second, sum_ref[f, COLS * (ROWS + 1) : COLS * (ROWS + 2)], sum_ref[f, 0:COLS])
        grad_ref[f, ROWS : ROWS + 1] = outer.astype(BF16).reshape(1, COLS, CH)
    value_out.wait()


def put_acts(turn, bundle_ref, other_ref, params_ref, out_ref):
    for strip, ref in enumerate((bundle_ref, other_ref)):
        for f in range(FRAMES):
            x = flat(ref[f, 6 + ROWS * turn : 6 + ROWS * (turn + 1)].astype(F32)).T
            for kt in range(min(3, FRAMES - f)):
                at = CH * (2 * sum(FRAMES - n for n in range(kt)) + strip * (FRAMES - kt) + f)
                y = x if kt == 0 else x * row(params_ref, TURN * turn + (PAIR1 if kt == 1 else PAIR2) + f + kt)
                out_ref[:, at : at + CH] = y.astype(BF16)


def kernel_terms(columns_ref, act_ref, kt):
    count = FRAMES - kt
    blocks = [
        columns_ref[:, kt:FRAMES, start : start + ROWS * COLS, :].reshape(2 * count * CH, 3 * CH)
        for start in (2 * COLS, COLS, 0)
    ]
    at = 2 * CH * sum(FRAMES - n for n in range(kt))
    return jnp.dot(
        act_ref[:, at : at + 2 * count * CH], jnp.concatenate(blocks, axis=1), preferred_element_type=F32
    )


def act_second_kernel(hand_ref, loss_ref, slope_ref, params_ref, stats_ref, out_ref, incoming_ref):
    gain = row(params_ref, GAIN)
    per_frame = []
    gain_part = row(stats_ref, GAIN_PART)
    shift_part = row(stats_ref, SHIFT_PART)
    for f in range(FRAMES):
        incoming = hand_ref[f].astype(F32) + loss_ref[f].astype(F32)
        incoming_ref[f] = incoming.astype(BF16)
        grad_act = flat(incoming[0:ROWS]) * flat(slope_ref[0, f])
        live = row(params_ref, TURN + LIVE + f)
        plain = colsum(grad_act) * live
        times = colsum(grad_act * flat(slope_ref[1, f])) * live
        shift_part = shift_part + plain
        gain_part = gain_part + times
        per_frame.append(jnp.concatenate([plain * gain, times * gain], axis=0))
    rows = jnp.concatenate([pack_rows(per_frame), gain_part, shift_part], axis=0)
    out_ref[...] = jnp.broadcast_to(rows[None], out_ref.shape)


def weight_first_kernel(
    table_ref, params_ref, stats_ref, value_hbm, bundle_hbm, other_hbm,
    slope_ref, act_ref, first_ref,
    columns_ref, act_first_ref, value_ref, bundle_ref, other_ref, fields_ref, sems,
):
    copies = copy_in([(bundle_hbm, bundle_ref), (other_hbm, other_ref), (value_hbm, value_ref)], sems)
    table = jnp.sum(table_ref[...], axis=0)
    gain, shift = row(params_ref, GAIN), row(params_ref, SHIFT)
    copies[0].wait()
    for f in range(FRAMES):
        normed = flat(bundle_ref[f, 1 : 1 + ROWS].astype(F32)) - row(stats_ref, MEAN1 + f)
        normed = normed * row(stats_ref, RSTD1 + f)
        slope_ref[0, f] = act_slope(normed, gain, shift).reshape(ROWS, COLS, CH)
        slope_ref[1, f] = normed.reshape(ROWS, COLS, CH)
    copies[1].wait()
    put_acts(0, bundle_ref, other_ref, params_ref, act_first_ref)
    put_acts(1, bundle_ref, other_ref, params_ref, act_ref)
    for f in range(FRAMES):
        mean, rstd = row(stats_ref, MEAN0 + f), row(stats_ref, RSTD0 + f)
        for at, count, mask in ((0, 1, OTHER_TOP), (1, ROWS, LIVE), (1 + ROWS, 1, OTHER_BOTTOM)):
            pair = fields(
                other_ref[f, 14 + at : 14 + at + count], other_ref[f, 20 + at : 20 + at + count], mean, rstd,
                gain, shift, row(params_ref, mask + f),
            )
            for n in range(2):
                fields_ref[n, f, at : at + count] = pair[n].reshape(count, COLS, CH)
    write_columns(
        store_columns(columns_ref, (1,)), table, fields_ref, (), params_ref, stats_ref, RSTD0, 0, 1,
        (OTHER_TOP, LIVE, OTHER_BOTTOM),
    )
    copies[2].wait()
    rows = ROWS + 2
    column = iota(0, (rows * COLS, CH)) & (COLS - 1)
    fill = store_columns(columns_ref, (0,))
    for f in range(FRAMES):
        value = flat(value_ref[f].astype(F32))
        left = jnp.where(column == COLS - 1, 0.0, pltpu.roll(value, rows * COLS - 1, 0))
        right = jnp.where(column == 0, 0.0, pltpu.roll(value, 1, 0))
        fill(f, left.astype(BF16), value.astype(BF16), right.astype(BF16))
    for kt in range(3):
        terms = kernel_terms(columns_ref, act_first_ref, kt)
        for n in range(9):
            first_ref[9 * kt + n] = terms[:, n * CH : (n + 1) * CH].astype(first_ref.dtype)


def fields_second_kernel(
    incoming_ref, arrived_ref, bundle_hbm, other_hbm, params_ref, stats_ref, out_ref, bundle_ref, other_ref, sems,
):
    pre_part = slice(0, ROWS + 2)
    copies = copy_in(
        [(bundle_hbm.at[:, pre_part], bundle_ref), (other_hbm.at[:, pre_part], other_ref)], sems
    )
    for copy in copies:
        copy.wait()
    gain, shift = row(params_ref, GAIN), row(params_ref, SHIFT)
    second = (row(params_ref, CORE) > 0.5).reshape(1, 1, CH)
    for f in range(FRAMES):
        mean, rstd = row(stats_ref, MEAN1 + f), row(stats_ref, RSTD1 + f)
        mine, others = incoming_ref[f].astype(F32), arrived_ref[f].astype(F32)
        far, near = slice(ROWS, ROWS + 1), slice(0, 1)
        end = slice(ROWS - 1, ROWS)
        for strip, pre_ref, top, own, bottom, top_mask, bottom_mask in (
            (
                0, bundle_ref, jnp.where(second, others[end], mine[far]), mine[0:ROWS],
                jnp.where(second, mine[far], others[near]), TURN + TOP, TURN + BOTTOM,
            ),
            (
                1, other_ref, jnp.where(second, others[far], mine[end]), others[0:ROWS],
                jnp.where(second, mine[near], others[far]), OTHER_TURN + OTHER_TOP, OTHER_TURN + OTHER_BOTTOM,
            ),
        ):
            for at, count, come, mask in (
                (0, 1, top, top_mask), (1, ROWS, own, TURN + LIVE), (1 + ROWS, 1, bottom, bottom_mask)
            ):
                pair = fields(
                    pre_ref[f, at : at + count], come, mean, rstd, gain, shift, row(params_ref, mask + f)
                )
                for n in range(2):
                    out_ref[strip, n, f, at : at + count] = pair[n].reshape(count, COLS, CH)


def weight_second_kernel(
    scale, chunk, table_ref, fields_ref, params_ref, stats_ref, first_ref, act_ref,
    out_hbm, own_hbm, parts_ref, columns_ref, sum_ref, out_ref, sems,
):
    table = jnp.sum(table_ref[...], axis=0)
    parts_ref[...] = table[2:4] * scale
    for strip, top, bottom in ((0, TURN + TOP, TURN + BOTTOM), (1, OTHER_TURN + OTHER_TOP, OTHER_TURN + OTHER_BOTTOM)):
        write_columns(
            store_columns(columns_ref, (strip,)), table[0:2], fields_ref, (strip,), params_ref, stats_ref,
            RSTD1, 1, 1, (top, TURN + LIVE, bottom),
        )
    copy_own = pltpu.make_async_copy(columns_ref.at[0], own_hbm, sems.at[0])
    copy_own.start()
    second = row(params_ref, CORE) > 0.5
    filler = jnp.zeros((out_ref.shape[1] - chunk, CH), F32)
    chips = out_ref.shape[0]
    done = 0
    copies = [copy_own]
    for kt in range(3):
        terms = kernel_terms(columns_ref, act_ref, kt)
        for n in range(9 * kt, 9 * kt + 9):
            at = (n - 9 * kt) * CH
            sum_ref[n * CH : (n + 1) * CH] = first_ref[n].astype(F32) + terms[:, at : at + CH]
        begin = done
        while done < chips and 2 * (done + 1) * chunk <= 9 * (kt + 1) * CH:
            at = 2 * done * chunk
            mine = jnp.where(second, sum_ref[at + chunk : at + 2 * chunk], sum_ref[at : at + chunk])
            if filler.shape[0]:
                mine = jnp.concatenate([mine, filler], axis=0)
            out_ref[done] = mine.astype(BF16)
            done += 1
        if done > begin:
            send = pltpu.make_async_copy(out_ref.at[begin:done], out_hbm.at[begin:done], sems.at[1 + kt])
            send.start()
            copies.append(send)
    for copy in copies:
        copy.wait()


def conv_second_kernel(
    params_ref, columns_hbm, first_hbm, taps_ref, out_ref, weight_ref, columns_ref, first_ref, sum_ref, sems
):
    pairs = [(columns_hbm, columns_ref), (first_hbm, first_ref)] + weight_copies(taps_ref, weight_ref)
    for copy in copy_in(pairs, sems):
        copy.wait()
    conv(columns_ref, weight_ref, params_ref, 1, ROWS, sum_ref)
    out_ref[0] = first_ref[:, 0:ROWS]
    out_ref[1] = sum_ref[...].astype(BF16).reshape(first_ref[:, 0:ROWS].shape)


def total_kernel(scale, terms_ref, out_ref):
    chunk = out_ref.shape[0]
    total = jnp.sum(terms_ref[...].astype(F32), axis=0)
    out_ref[...] = (total[0:chunk] * scale).reshape(chunk, 1, CH)


def call(kernel, name, args, outs, scratch=(), specs="", flops=1_000_000):
    specs = specs or "v" * len(args)
    size = sum(a.size * a.dtype.itemsize for a in args)
    space = {"k": pltpu.VMEM, "h": pltpu.HBM}
    args = [pltpu.with_memory_space_constraint(a, space[x]) if x in space else a for a, x in zip(args, specs)]
    return pl.pallas_call(
        kernel,
        out_shape=tuple(outs),
        in_specs=[{"v": VMEM, "k": VMEM, "s": SMEM, "h": HBM}[x] for x in specs],
        out_specs=tuple(HBM if getattr(o, "memory_space", None) is pltpu.HBM else VMEM for o in outs),
        scratch_shapes=list(scratch),
        compiler_params=pltpu.CompilerParams(vmem_limit_bytes=24 * 1024 * 1024),
        cost_estimate=pl.CostEstimate(flops=flops, bytes_accessed=size, transcendentals=0),
        name=name,
    )(*args)


def shape(dims, dtype=F32):
    return jax.ShapeDtypeStruct(dims, dtype)


def kept(dims, dtype=F32):
    return pltpu.VMEM(dims, dtype)


def in_hbm(dims, dtype=F32):
    return pltpu.HBM(dims, dtype)


def local(activations, pre_norm, cot_first, loss_grad, frame_clip, weight, norm_gain, norm_shift):
    dp = lax.axis_size("dp")
    me = lax.axis_index("dp")
    cells = float(dp * ROWS * COLS * PER)
    chips, chunk = dp // 2, TAPS * CH // dp
    padded = -(-chunk // 8) * 8
    other = me ^ 1
    last = lax.axis_index("segment") == lax.axis_size("segment") - 1
    flags = [me != 0, me != dp - 1, other != 0, other != dp - 1, me & 1, last]
    flags = jnp.stack([x.astype(jnp.int32) for x in flags])
    pre, act = pre_norm[0], activations[0]
    cot, loss = cot_first[0], loss_grad[0]
    taps = weight[0].reshape(3, 9, CH, CH)
    edge = (FRAMES, ROWS + 2, COLS, CH)
    handed = (FRAMES, ROWS + 1, COLS, CH)
    strip = (FRAMES, ROWS, COLS, CH)
    bundled = (FRAMES, 3 * (ROWS + 2) + 2 * ROWS, COLS, CH)
    mates = [(i, i ^ 1) for i in range(dp)]
    columns_of = lambda rows: (FRAMES, rows * COLS, 3 * CH)
    sems = lambda n: pltpu.SemaphoreType.DMA((n,))

    def exchange(table):
        return lax.all_to_all(table, "dp", 0, 0, tiled=True)

    table, inner, outer, own, plain = call(
        functools.partial(sums_kernel, cells), "sums", ((me & 1).reshape(1), frame_clip, pre, cot, loss, norm_gain, norm_shift),
        (
            shape((dp, 4, CH)), shape(edge, BF16), shape(edge, BF16),
            kept((2,) + strip), kept((PARAM_ROWS, CH)),
        ),
        scratch=[
            pltpu.SMEM((1, 2, 1, FRAMES), jnp.int32), pltpu.VMEM((2,) + strip, BF16), pltpu.VMEM(strip, BF16), sems(13)
        ],
        specs="shhhhhh",
    )
    table = exchange(table)
    inner = lax.ppermute(inner, "dp", mates)
    sides = [(i, i + 1) for i in range(1, dp - 1, 2)]
    outer = lax.ppermute(outer, "dp", sides + [(j, i) for i, j in sides])

    table, stats = call(
        act_first_kernel, "act_first", (table, own, plain), (shape((dp, 2, CH)), kept((STAT_ROWS, CH))), specs="vkk"
    )
    table = exchange(table)

    first_fields, bundle, loss_rows, params = call(
        fields_first_kernel, "fields_first", (flags, inner, outer, plain, stats, pre, cot, loss, act),
        (
            kept((2, FRAMES, ROWS + 4, COLS, CH)), in_hbm(bundled, BF16),
            kept(handed, BF16), kept((PARAM_ROWS, CH)),
        ),
        scratch=[pltpu.VMEM(bundled, BF16), pltpu.VMEM(strip, BF16)] + [pltpu.VMEM(edge, BF16)] * 2 + [sems(7)],
        specs="svvkkhhhh",
    )
    other_bundle = lax.ppermute(bundle, "dp", mates)

    weights = pltpu.VMEM((3, CH, 9 * CH), BF16)
    grad_first, value = call(
        conv_first_kernel, "conv_first", (table, first_fields, params, stats, taps),
        (shape(handed, BF16), in_hbm(edge, BF16)),
        scratch=[
            pltpu.VMEM(columns_of(ROWS + 4), BF16), pltpu.VMEM((3, 9, CH, CH), BF16), weights, pltpu.VMEM(edge, BF16),
            pltpu.VMEM((FRAMES, (ROWS + 2) * COLS, CH), F32), sems(2),
        ],
        specs="vkkkh", flops=20_000_000_000,
    )
    count = lax.axis_size("segment")
    hand = lax.ppermute(grad_first, "segment", [(i + 1, i) for i in range(count - 1)])

    both = pltpu.VMEM((2,) + columns_of(ROWS + 2), BF16)
    acts_dims, taps_dims = (CH, 2 * 9 * CH), (TAPS, CH, CH)
    slope, acts, weight_first = call(
        weight_first_kernel, "weight_first", (table, params, stats, value, bundle, other_bundle),
        (kept((2,) + strip), kept(acts_dims, BF16), kept(taps_dims, BF16)),
        scratch=[both, pltpu.VMEM(acts_dims, BF16)]
        + [pltpu.VMEM(edge, BF16)] + [pltpu.VMEM(bundled, BF16)] * 2 + [pltpu.VMEM((2,) + edge, F32), sems(3)],
        specs="vkkhhh",
    )

    table, incoming = call(
        act_second_kernel, "act_second", (hand, loss_rows, slope, params, stats),
        (shape((dp, 4, CH)), shape(handed, BF16)), specs="vkkkk",
    )
    table = exchange(table)
    arrived = lax.ppermute(incoming, "dp", mates)
    (second_fields,) = call(
        fields_second_kernel, "fields_second", (incoming, arrived, bundle, other_bundle, params, stats),
        (kept((2, 2) + edge),), scratch=[pltpu.VMEM(edge, BF16)] * 2 + [sems(2)], specs="vvhhkk",
    )

    terms, columns, parts = call(
        functools.partial(weight_second_kernel, 1.0 / dp, chunk), "weight_second",
        (table, second_fields, params, stats, weight_first, acts),
        (in_hbm((chips, padded, CH), BF16), in_hbm(columns_of(ROWS + 2), BF16), shape((2, CH))),
        scratch=[
            both, pltpu.VMEM((TAPS * CH, CH), F32),
            pltpu.VMEM((chips, padded, CH), BF16), sems(4),
        ],
        specs="vkkkkk",
    )
    sides = [[2 * i + core for i in range(chips)] for core in range(2)]
    terms = lax.all_to_all(terms, "dp", 0, 0, axis_index_groups=sides, tiled=True)
    (grad_weight,) = call(
        functools.partial(total_kernel, 1.0 / dp), "total", (terms,), (shape((chunk, 1, CH)),)
    )
    (grad_inputs,) = call(
        conv_second_kernel, "conv_second", (params, columns, grad_first, taps),
        (shape((2, FRAMES, ROWS, COLS, CH), BF16),),
        scratch=[
            weights, pltpu.VMEM(columns_of(ROWS + 2), BF16), pltpu.VMEM(handed, BF16),
            pltpu.VMEM((FRAMES, ROWS * COLS, CH), F32), sems(11),
        ],
        specs="khhh",
    )
    width = CH // dp
    mine = lax.dynamic_slice_in_dim(parts, me * width, width, axis=1)
    return (grad_inputs[None], grad_weight.transpose(1, 0, 2), mine[0:1], mine[1:2])


def solution(mesh):
    in_specs = (
        P("segment", None, None, "dp", None, None),
        P("segment", None, None, "dp", None, None),
        P("segment", None, "dp", None, None),
        P(None, None, "dp", None, None),
        P("segment", None, "dp", None),
        P("segment", None, None),
        P("segment", None),
        P("segment", None),
    )
    out_specs = (
        P("segment", None, None, "dp", None, None),
        P("segment", "dp", None),
        P("segment", "dp"),
        P("segment", "dp"),
    )
    return jax.shard_map(local, mesh=mesh, in_specs=in_specs, out_specs=out_specs, check_vma=False)
```

```python
import functools
import jax
import jax.numpy as jnp
from jax import lax
from jax.experimental import pallas as pl
from jax.experimental.pallas import tpu as pltpu
from jax.sharding import PartitionSpec as P

F32, BF16 = jnp.float32, jnp.bfloat16
FRAMES, ROWS, COLS, CH = 4, 4, 32, 128
GROUPS, PER = 32, 4
TAPS = 27
EPS = 1e-05
VMEM = pl.BlockSpec(memory_space=pltpu.VMEM)
SMEM = pl.BlockSpec(memory_space=pltpu.SMEM)
HBM = pl.BlockSpec(memory_space=pltpu.HBM)

GAIN, SHIFT, CORE, LAST = 0, 1, 2, 3
TURN = 24
INV, LIVE, TOP, BOTTOM, PAIR1, PAIR2 = (8 + 4 * n for n in range(6))
OTHER_TOP, OTHER_BOTTOM = 56, 60
CLIPS = 64
OTHER_TURN = 16
PARAM_ROWS = 80
MEAN0, RSTD0, MEAN1, RSTD1, GAIN_PART, SHIFT_PART = 0, 4, 8, 12, 16, 17
STAT_ROWS = 24


def iota(dim, dims=(CH, CH)):
    return lax.broadcasted_iota(jnp.int32, dims, dim)


def split_dot(rows, marks):
    count = rows.shape[0]
    high = rows.astype(BF16)
    rest = rows - high.astype(F32)
    middle = rest.astype(BF16)
    low = (rest - middle.astype(F32)).astype(BF16)
    out = jnp.dot(
        jnp.concatenate([high.astype(F32), middle.astype(F32), low.astype(F32)], axis=0).astype(BF16),
        marks,
        preferred_element_type=F32,
    )
    return out[0:count] + out[count : 2 * count] + out[2 * count : 3 * count]


def pack_rows(per_frame):
    rows = jnp.concatenate(per_frame, axis=1)
    dims = (FRAMES * CH, CH)
    marks = (iota(1, dims) == (iota(0, dims) >> 2)).astype(F32).astype(BF16)
    return split_dot(rows, marks)


def unpack_rows(table, marks):
    total = split_dot(table, marks)
    return [total[:, f * CH : (f + 1) * CH] for f in range(FRAMES)]


def row(ref, at):
    return ref[at : at + 1]


def colsum(x):
    return jnp.sum(x, axis=0, keepdims=True)


def flat(x):
    return x.reshape(-1, CH)


def act_slope(normed, gain, shift):
    act = normed * gain + shift
    sigm = jax.nn.sigmoid(act)
    return sigm * (1.0 + act * (1.0 - sigm))


def copy_in(pairs, sems):
    copies = [pltpu.make_async_copy(src, dst, sems.at[n]) for n, (src, dst) in enumerate(pairs)]
    for copy in copies:
        copy.start()
    return copies


def sums_kernel(
    cells, odd_ref, clip_hbm, pre_ref, cot_ref, loss_ref, gain_ref, shift_ref,
    out_ref, inner_ref, outer_ref, own_ref, params_ref, clip_ref, held_ref, held_cot, sems,
):
    pairs = [
        (clip_hbm, clip_ref), (pre_ref, held_ref), (cot_ref, held_cot),
        (gain_ref, params_ref.at[GAIN : GAIN + 1]), (shift_ref, params_ref.at[SHIFT : SHIFT + 1]),
    ]
    odd = odd_ref[0]
    for ref, side in ((inner_ref, 1 - odd), (outer_ref, odd)):
        two, one = pl.ds(side * (ROWS - 2), 2), pl.ds(side * (ROWS - 1), 1)
        pairs += [
            (pre_ref.at[0, :, two], ref.at[:, 0:2]), (cot_ref.at[:, two], ref.at[:, 2:4]),
            (pre_ref.at[1, :, one], ref.at[:, 4:5]), (loss_ref.at[:, one], ref.at[:, 5:6]),
        ]
    copies = copy_in(pairs, sems)
    params_ref[SHIFT + 1 :] = jnp.zeros((PARAM_ROWS - SHIFT - 1, CH), F32)

    def put(at, scalar):
        params_ref[at : at + 1] = jnp.full((1, CH), scalar, F32)

    copies[0].wait()
    for t in range(2):
        clips = [clip_ref[0, t, 0, f] for f in range(FRAMES)]
        for f in range(FRAMES):
            count = jnp.int32(0)
            for other in range(FRAMES):
                count = count + (clips[other] == clips[f]).astype(jnp.int32)
            live = (clips[f] < FRAMES).astype(F32)
            base = TURN * t + f
            params_ref[base + INV : base + INV + 1] = 1.0 / jnp.full((1, CH), count.astype(F32) * cells, F32)
            put(base + LIVE, live)
            put(CLIPS + FRAMES * t + f, clips[f].astype(F32))
            for kt, at in ((1, PAIR1), (2, PAIR2)):
                pair = live * (clips[f - kt] == clips[f]).astype(F32) if f >= kt else live * 0.0
                put(base + at, pair)
    copies[1].wait()
    per_frame = []
    for f in range(FRAMES):
        rows = []
        for t in range(2):
            x = flat(held_ref[t, f].astype(F32))
            if t == 0:
                own_ref[0, f] = x.reshape(ROWS, COLS, CH)
            rows += [colsum(x), colsum(x * x)]
        per_frame.append(jnp.concatenate(rows, axis=0))
    out_ref[...] = jnp.broadcast_to(pack_rows(per_frame)[None], out_ref.shape)
    copies[2].wait()
    own_ref[1] = held_cot[...].astype(F32)
    for copy in copies[3:]:
        copy.wait()


def clip_marks(params_ref, turn):
    slot = iota(0) >> 5
    clips = [row(params_ref, CLIPS + FRAMES * turn + f) for f in range(FRAMES)]
    clip_of_row = jnp.where(
        slot == 0, clips[0], jnp.where(slot == 1, clips[1], jnp.where(slot == 2, clips[2], clips[3]))
    )
    same_group = (iota(0) & (GROUPS - 1)) == (iota(1) >> 2)
    blocks = [(same_group & (clip_of_row == clips[f])).astype(F32).astype(BF16) for f in range(FRAMES)]
    return jnp.concatenate(blocks, axis=1)


def act_first_kernel(table_ref, own_ref, params_ref, out_ref, stats_ref):
    table = jnp.sum(table_ref[...], axis=0)
    gain, shift = row(params_ref, GAIN), row(params_ref, SHIFT)
    for t, mean_at, rstd_at in ((0, MEAN0, RSTD0), (1, MEAN1, RSTD1)):
        total = unpack_rows(table[2 * t : 2 * t + 2], clip_marks(params_ref, t))
        for f in range(FRAMES):
            inverse = row(params_ref, TURN * t + INV + f)
            mean = total[f][0:1] * inverse
            var = total[f][1:2] * inverse - mean * mean
            stats_ref[mean_at + f : mean_at + f + 1] = mean
            stats_ref[rstd_at + f : rstd_at + f + 1] = 1.0 / jnp.sqrt(var + EPS)
    per_frame = []
    gain_part = jnp.zeros((1, CH), F32)
    shift_part = jnp.zeros((1, CH), F32)
    for f in range(FRAMES):
        normed = (flat(own_ref[0, f]) - row(stats_ref, MEAN0 + f)) * row(stats_ref, RSTD0 + f)
        grad_act = flat(own_ref[1, f]) * act_slope(normed, gain, shift)
        live = row(params_ref, LIVE + f)
        plain = colsum(grad_act) * live
        times = colsum(grad_act * normed) * live
        shift_part = shift_part + plain
        gain_part = gain_part + times
        per_frame.append(jnp.concatenate([plain * gain, times * gain], axis=0))
    stats_ref[GAIN_PART : GAIN_PART + 1] = gain_part
    stats_ref[SHIFT_PART : SHIFT_PART + 1] = shift_part
    stats_ref[SHIFT_PART + 1 :] = jnp.zeros((STAT_ROWS - SHIFT_PART - 1, CH), F32)
    out_ref[...] = jnp.broadcast_to(pack_rows(per_frame)[None], out_ref.shape)


def fields(pre, incoming, mean, rstd, gain, shift, mask):
    normed = (flat(pre.astype(F32)) - mean) * rstd
    scaled = flat(incoming.astype(F32)) * act_slope(normed, gain, shift) * gain
    rstd = rstd * mask
    return scaled * rstd, normed * rstd


def fields_first_kernel(
    flag_ref, inner_ref, outer_ref, plain_ref, stats_ref, pre_ref, cot_ref, loss_ref, act_ref,
    out_ref, bundle_hbm, loss_out_ref, params_ref, bundle_ref, held_loss, up_ref, down_ref, sems,
):
    copies = copy_in(
        [
            (pre_ref.at[0], bundle_ref.at[:, 15 : 15 + ROWS]), (cot_ref, bundle_ref.at[:, 21 : 21 + ROWS]),
            (loss_ref, held_loss), (pre_ref.at[1], bundle_ref.at[:, 1 : 1 + ROWS]),
            (act_ref.at[0], bundle_ref.at[:, 6 : 6 + ROWS]),
            (act_ref.at[1], bundle_ref.at[:, 6 + ROWS : 6 + 2 * ROWS]),
        ],
        sems,
    )

    @pl.when(flag_ref[4] == 0)
    def even():
        up_ref[...] = outer_ref[...]
        down_ref[...] = inner_ref[...]

    @pl.when(flag_ref[4] != 0)
    def odd():
        up_ref[...] = inner_ref[...]
        down_ref[...] = outer_ref[...]

    params_ref[...] = plain_ref[...]
    flag = [flag_ref[n].astype(F32) for n in range(6)]
    for at, n in ((CORE, 4), (LAST, 5)):
        params_ref[at : at + 1] = jnp.full((1, CH), flag[n], F32)
    for t in range(2):
        for f in range(FRAMES):
            live = plain_ref[TURN * t + LIVE + f : TURN * t + LIVE + f + 1]
            for at, n in (
                (TURN * t + TOP, 0), (TURN * t + BOTTOM, 1),
                (OTHER_TURN * t + OTHER_TOP, 2), (OTHER_TURN * t + OTHER_BOTTOM, 3),
            ):
                params_ref[at + f : at + f + 1] = live * flag[n]
    for at, edge, below in ((0, 4, 4), (14, 1, 0), (20, 3, 2)):
        bundle_ref[:, at : at + 1] = up_ref[:, edge : edge + 1]
        bundle_ref[:, at + 1 + ROWS : at + 2 + ROWS] = down_ref[:, below : below + 1]
    for copy in copies:
        copy.wait()
    bundle_out = pltpu.make_async_copy(bundle_ref, bundle_hbm, sems.at[6])
    bundle_out.start()
    gain, shift = row(params_ref, GAIN), row(params_ref, SHIFT)
    last = row(params_ref, LAST).reshape(1, 1, 1, CH)
    loss_out_ref[:, 0:ROWS] = (held_loss[...].astype(F32) * last).astype(BF16)
    loss_out_ref[:, ROWS : ROWS + 1] = (outer_ref[:, 5:6].astype(F32) * last).astype(BF16)
    for f in range(FRAMES):
        mean, rstd = row(stats_ref, MEAN0 + f), row(stats_ref, RSTD0 + f)
        for at, count, pre, cot, mask in (
            (0, 2, up_ref[f, 0:2], up_ref[f, 2:4], TOP),
            (2, ROWS, bundle_ref[f, 15 : 15 + ROWS], bundle_ref[f, 21 : 21 + ROWS], LIVE),
            (2 + ROWS, 2, down_ref[f, 0:2], down_ref[f, 2:4], BOTTOM),
        ):
            pair = fields(pre, cot, mean, rstd, gain, shift, row(params_ref, mask + f))
            for n in range(2):
                out_ref[n, f, at : at + count] = pair[n].reshape(count, COLS, CH)
    bundle_out.wait()


def write_columns(store, table, fields_ref, at_fields, params_ref, stats_ref, rstd_at, turn, halo, masks):
    total = unpack_rows(table, clip_marks(params_ref, turn))
    rows = ROWS + 2 * halo
    column = iota(0, (rows * COLS, CH)) & (COLS - 1)
    for f in range(FRAMES):
        inverse = row(params_ref, TURN * turn + INV + f)
        avg_a = total[f][0:1] * inverse * row(stats_ref, rstd_at + f)
        avg_b = total[f][1:2] * inverse
        pieces = []
        for mask, at, count in ((masks[0], 0, halo), (masks[1], halo, ROWS), (masks[2], halo + ROWS, halo)):
            scaled = flat(fields_ref[at_fields + (0, f, slice(at, at + count))])
            normed = flat(fields_ref[at_fields + (1, f, slice(at, at + count))])
            pieces.append(scaled - avg_a * row(params_ref, mask + f) - normed * avg_b)
        value = jnp.concatenate(pieces, axis=0)
        left = jnp.where(column == COLS - 1, 0.0, pltpu.roll(value, rows * COLS - 1, 0))
        right = jnp.where(column == 0, 0.0, pltpu.roll(value, 1, 0))
        store(f, left.astype(BF16), value.astype(BF16), right.astype(BF16))


def store_columns(ref, prefix=()):
    def store(f, left, value, right):
        for n, x in enumerate((left, value, right)):
            ref[prefix + (f, slice(None), slice(n * CH, (n + 1) * CH))] = x

    return store


def conv(columns_ref, weight_ref, params_ref, turn, rows, sum_ref):
    size = rows * COLS
    for kt in range(3):
        count = FRAMES - kt
        part = None
        for dy in range(3):
            start = (2 - dy) * COLS
            term = lax.dot_general(
                columns_ref[kt:FRAMES, start : start + size, :].reshape(count * size, 3 * CH),
                weight_ref[kt, :, 3 * dy * CH : 3 * (dy + 1) * CH], (((1,), (1,)), ((), ())),
                preferred_element_type=F32,
            )
            part = term if part is None else part + term
        for f in range(count):
            mine = part[f * size : (f + 1) * size]
            if kt:
                mine = mine * row(params_ref, TURN * turn + (PAIR1 if kt == 1 else PAIR2) + f + kt)
                sum_ref[f] = sum_ref[f] + mine
            else:
                sum_ref[f] = mine


def weight_copies(taps_ref, weight_ref):
    return [(taps_ref.at[:, n], weight_ref.at[:, :, n * CH : (n + 1) * CH]) for n in range(9)]


def conv_first_kernel(
    table_ref, fields_ref, params_ref, stats_ref, taps_hbm, grad_ref, value_hbm,
    columns_ref, taps_ref, weight_ref, value_ref, sum_ref, sems,
):
    (copy,) = copy_in([(taps_hbm, taps_ref)], sems)
    table = jnp.sum(table_ref[...], axis=0)
    fill = store_columns(columns_ref)

    def store(f, left, value, right):
        fill(f, left, value, right)
        value_ref[f] = value[COLS : COLS * (ROWS + 3)].reshape(ROWS + 2, COLS, CH)

    write_columns(
        store, table, fields_ref, (), params_ref, stats_ref, RSTD0, 0, 2, (TOP, LIVE, BOTTOM)
    )
    value_out = pltpu.make_async_copy(value_ref, value_hbm, sems.at[1])
    value_out.start()
    copy.wait()
    for kt in range(3):
        for n in range(9):
            weight_ref[kt, :, n * CH : (n + 1) * CH] = taps_ref[kt, n]
    conv(columns_ref, weight_ref, params_ref, 0, ROWS + 2, sum_ref)
    second = row(params_ref, CORE) > 0.5
    for f in range(FRAMES):
        grad_ref[f, 0:ROWS] = sum_ref[f, COLS : COLS * (ROWS + 1)].astype(BF16).reshape(ROWS, COLS, CH)
        outer = jnp.where(second, sum_ref[f, COLS * (ROWS + 1) : COLS * (ROWS + 2)], sum_ref[f, 0:COLS])
        grad_ref[f, ROWS : ROWS + 1] = outer.astype(BF16).reshape(1, COLS, CH)
    value_out.wait()


def put_acts(turn, bundle_ref, other_ref, params_ref, out_ref):
    for strip, ref in enumerate((bundle_ref, other_ref)):
        for f in range(FRAMES):
            x = flat(ref[f, 6 + ROWS * turn : 6 + ROWS * (turn + 1)].astype(F32)).T
            for kt in range(min(3, FRAMES - f)):
                at = CH * (2 * sum(FRAMES - n for n in range(kt)) + strip * (FRAMES - kt) + f)
                y = x if kt == 0 else x * row(params_ref, TURN * turn + (PAIR1 if kt == 1 else PAIR2) + f + kt)
                out_ref[:, at : at + CH] = y.astype(BF16)


def kernel_terms(columns_ref, act_ref, kt):
    count = FRAMES - kt
    blocks = [
        columns_ref[:, kt:FRAMES, start : start + ROWS * COLS, :].reshape(2 * count * CH, 3 * CH)
        for start in (2 * COLS, COLS, 0)
    ]
    at = 2 * CH * sum(FRAMES - n for n in range(kt))
    return jnp.dot(
        act_ref[:, at : at + 2 * count * CH], jnp.concatenate(blocks, axis=1), preferred_element_type=F32
    )


def act_second_kernel(hand_ref, loss_ref, slope_ref, params_ref, stats_ref, out_ref, incoming_ref):
    gain = row(params_ref, GAIN)
    per_frame = []
    gain_part = row(stats_ref, GAIN_PART)
    shift_part = row(stats_ref, SHIFT_PART)
    for f in range(FRAMES):
        incoming = hand_ref[f].astype(F32) + loss_ref[f].astype(F32)
        incoming_ref[f] = incoming.astype(BF16)
        grad_act = flat(incoming[0:ROWS]) * flat(slope_ref[0, f])
        live = row(params_ref, TURN + LIVE + f)
        plain = colsum(grad_act) * live
        times = colsum(grad_act * flat(slope_ref[1, f])) * live
        shift_part = shift_part + plain
        gain_part = gain_part + times
        per_frame.append(jnp.concatenate([plain * gain, times * gain], axis=0))
    rows = jnp.concatenate([pack_rows(per_frame), gain_part, shift_part], axis=0)
    out_ref[...] = jnp.broadcast_to(rows[None], out_ref.shape)


def weight_first_kernel(
    table_ref, params_ref, stats_ref, value_hbm, bundle_hbm, other_hbm,
    slope_ref, act_ref, first_ref,
    columns_ref, act_first_ref, value_ref, bundle_ref, other_ref, fields_ref, sems,
):
    copies = copy_in([(bundle_hbm, bundle_ref), (other_hbm, other_ref), (value_hbm, value_ref)], sems)
    table = jnp.sum(table_ref[...], axis=0)
    gain, shift = row(params_ref, GAIN), row(params_ref, SHIFT)
    copies[0].wait()
    for f in range(FRAMES):
        normed = flat(bundle_ref[f, 1 : 1 + ROWS].astype(F32)) - row(stats_ref, MEAN1 + f)
        normed = normed * row(stats_ref, RSTD1 + f)
        slope_ref[0, f] = act_slope(normed, gain, shift).reshape(ROWS, COLS, CH)
        slope_ref[1, f] = normed.reshape(ROWS, COLS, CH)
    copies[1].wait()
    put_acts(0, bundle_ref, other_ref, params_ref, act_first_ref)
    put_acts(1, bundle_ref, other_ref, params_ref, act_ref)
    for f in range(FRAMES):
        mean, rstd = row(stats_ref, MEAN0 + f), row(stats_ref, RSTD0 + f)
        for at, count, mask in ((0, 1, OTHER_TOP), (1, ROWS, LIVE), (1 + ROWS, 1, OTHER_BOTTOM)):
            pair = fields(
                other_ref[f, 14 + at : 14 + at + count], other_ref[f, 20 + at : 20 + at + count], mean, rstd,
                gain, shift, row(params_ref, mask + f),
            )
            for n in range(2):
                fields_ref[n, f, at : at + count] = pair[n].reshape(count, COLS, CH)
    write_columns(
        store_columns(columns_ref, (1,)), table, fields_ref, (), params_ref, stats_ref, RSTD0, 0, 1,
        (OTHER_TOP, LIVE, OTHER_BOTTOM),
    )
    copies[2].wait()
    rows = ROWS + 2
    column = iota(0, (rows * COLS, CH)) & (COLS - 1)
    fill = store_columns(columns_ref, (0,))
    for f in range(FRAMES):
        value = flat(value_ref[f].astype(F32))
        left = jnp.where(column == COLS - 1, 0.0, pltpu.roll(value, rows * COLS - 1, 0))
        right = jnp.where(column == 0, 0.0, pltpu.roll(value, 1, 0))
        fill(f, left.astype(BF16), value.astype(BF16), right.astype(BF16))
    for kt in range(3):
        terms = kernel_terms(columns_ref, act_first_ref, kt)
        for n in range(9):
            first_ref[9 * kt + n] = terms[:, n * CH : (n + 1) * CH].astype(first_ref.dtype)


def fields_second_kernel(
    incoming_ref, arrived_ref, bundle_hbm, other_hbm, params_ref, stats_ref, out_ref, bundle_ref, other_ref, sems,
):
    pre_part = slice(0, ROWS + 2)
    copies = copy_in(
        [(bundle_hbm.at[:, pre_part], bundle_ref), (other_hbm.at[:, pre_part], other_ref)], sems
    )
    for copy in copies:
        copy.wait()
    gain, shift = row(params_ref, GAIN), row(params_ref, SHIFT)
    second = (row(params_ref, CORE) > 0.5).reshape(1, 1, CH)
    for f in range(FRAMES):
        mean, rstd = row(stats_ref, MEAN1 + f), row(stats_ref, RSTD1 + f)
        mine, others = incoming_ref[f].astype(F32), arrived_ref[f].astype(F32)
        far, near = slice(ROWS, ROWS + 1), slice(0, 1)
        end = slice(ROWS - 1, ROWS)
        for strip, pre_ref, top, own, bottom, top_mask, bottom_mask in (
            (
                0, bundle_ref, jnp.where(second, others[end], mine[far]), mine[0:ROWS],
                jnp.where(second, mine[far], others[near]), TURN + TOP, TURN + BOTTOM,
            ),
            (
                1, other_ref, jnp.where(second, others[far], mine[end]), others[0:ROWS],
                jnp.where(second, mine[near], others[far]), OTHER_TURN + OTHER_TOP, OTHER_TURN + OTHER_BOTTOM,
            ),
        ):
            for at, count, come, mask in (
                (0, 1, top, top_mask), (1, ROWS, own, TURN + LIVE), (1 + ROWS, 1, bottom, bottom_mask)
            ):
                pair = fields(
                    pre_ref[f, at : at + count], come, mean, rstd, gain, shift, row(params_ref, mask + f)
                )
                for n in range(2):
                    out_ref[strip, n, f, at : at + count] = pair[n].reshape(count, COLS, CH)


def weight_second_kernel(
    scale, chunk, table_ref, fields_ref, params_ref, stats_ref, first_ref, act_ref,
    out_hbm, own_hbm, parts_ref, columns_ref, sum_ref, out_ref, sems,
):
    table = jnp.sum(table_ref[...], axis=0)
    parts_ref[...] = table[2:4] * scale
    for strip, top, bottom in ((0, TURN + TOP, TURN + BOTTOM), (1, OTHER_TURN + OTHER_TOP, OTHER_TURN + OTHER_BOTTOM)):
        write_columns(
            store_columns(columns_ref, (strip,)), table[0:2], fields_ref, (strip,), params_ref, stats_ref,
            RSTD1, 1, 1, (top, TURN + LIVE, bottom),
        )
    copy_own = pltpu.make_async_copy(columns_ref.at[0], own_hbm, sems.at[0])
    copy_own.start()
    second = row(params_ref, CORE) > 0.5
    chips = TAPS * CH // (2 * chunk)
    padded = out_ref.shape[0] // chips
    filler = [jnp.zeros((padded - chunk, CH), F32)] if padded > chunk else []
    done = 0
    copies = [copy_own]
    for kt in range(3):
        terms = kernel_terms(columns_ref, act_ref, kt)
        for n in range(9 * kt, 9 * kt + 9):
            at = (n - 9 * kt) * CH
            sum_ref[n * CH : (n + 1) * CH] = first_ref[n].astype(F32) + terms[:, at : at + CH]
        begin = done
        while done < chips and 2 * (done + 2) * chunk <= 9 * (kt + 1) * CH:
            pieces = []
            for at in (2 * done * chunk, 2 * (done + 1) * chunk):
                pieces.append(jnp.where(second, sum_ref[at + chunk : at + 2 * chunk], sum_ref[at : at + chunk]))
                pieces += filler
            out_ref[done * padded : (done + 2) * padded] = jnp.concatenate(pieces, axis=0).astype(BF16)
            done += 2
        if done > begin:
            rows = slice(begin * padded, done * padded)
            send = pltpu.make_async_copy(out_ref.at[rows], out_hbm.at[rows], sems.at[1 + kt])
            send.start()
            copies.append(send)
    for copy in copies:
        copy.wait()


def conv_second_kernel(
    params_ref, columns_hbm, first_hbm, taps_ref, out_ref, weight_ref, columns_ref, first_ref, sum_ref, sems
):
    pairs = [(columns_hbm, columns_ref), (first_hbm, first_ref)] + weight_copies(taps_ref, weight_ref)
    for copy in copy_in(pairs, sems):
        copy.wait()
    conv(columns_ref, weight_ref, params_ref, 1, ROWS, sum_ref)
    out_ref[0] = first_ref[:, 0:ROWS]
    out_ref[1] = sum_ref[...].astype(BF16).reshape(first_ref[:, 0:ROWS].shape)


def total_kernel(scale, terms_ref, out_ref):
    chunk = out_ref.shape[0]
    total = jnp.sum(terms_ref[...].astype(F32), axis=0)
    out_ref[...] = (total[0:chunk] * scale).reshape(chunk, 1, CH)


def call(kernel, name, args, outs, scratch=(), specs="", flops=1_000_000):
    specs = specs or "v" * len(args)
    size = sum(a.size * a.dtype.itemsize for a in args)
    space = {"k": pltpu.VMEM, "h": pltpu.HBM}
    args = [pltpu.with_memory_space_constraint(a, space[x]) if x in space else a for a, x in zip(args, specs)]
    return pl.pallas_call(
        kernel,
        out_shape=tuple(outs),
        in_specs=[{"v": VMEM, "k": VMEM, "s": SMEM, "h": HBM}[x] for x in specs],
        out_specs=tuple(HBM if getattr(o, "memory_space", None) is pltpu.HBM else VMEM for o in outs),
        scratch_shapes=list(scratch),
        compiler_params=pltpu.CompilerParams(vmem_limit_bytes=24 * 1024 * 1024),
        cost_estimate=pl.CostEstimate(flops=flops, bytes_accessed=size, transcendentals=0),
        name=name,
    )(*args)


def shape(dims, dtype=F32):
    return jax.ShapeDtypeStruct(dims, dtype)


def kept(dims, dtype=F32):
    return pltpu.VMEM(dims, dtype)


def in_hbm(dims, dtype=F32):
    return pltpu.HBM(dims, dtype)


def local(activations, pre_norm, cot_first, loss_grad, frame_clip, weight, norm_gain, norm_shift):
    dp = lax.axis_size("dp")
    me = lax.axis_index("dp")
    cells = float(dp * ROWS * COLS * PER)
    chips, chunk = dp // 2, TAPS * CH // dp
    padded = -(-chunk // 8) * 8
    other = me ^ 1
    last = lax.axis_index("segment") == lax.axis_size("segment") - 1
    flags = [me != 0, me != dp - 1, other != 0, other != dp - 1, me & 1, last]
    flags = jnp.stack([x.astype(jnp.int32) for x in flags])
    pre, act = pre_norm[0], activations[0]
    cot, loss = cot_first[0], loss_grad[0]
    taps = weight[0].reshape(3, 9, CH, CH)
    edge = (FRAMES, ROWS + 2, COLS, CH)
    handed = (FRAMES, ROWS + 1, COLS, CH)
    strip = (FRAMES, ROWS, COLS, CH)
    bundled = (FRAMES, 3 * (ROWS + 2) + 2 * ROWS, COLS, CH)
    mates = [(i, i ^ 1) for i in range(dp)]
    columns_of = lambda rows: (FRAMES, rows * COLS, 3 * CH)
    sems = lambda n: pltpu.SemaphoreType.DMA((n,))

    def exchange(table):
        return lax.all_to_all(table, "dp", 0, 0, tiled=True)

    table, inner, outer, own, plain = call(
        functools.partial(sums_kernel, cells), "sums", ((me & 1).reshape(1), frame_clip, pre, cot, loss, norm_gain, norm_shift),
        (
            shape((dp, 4, CH)), shape(edge, BF16), shape(edge, BF16),
            kept((2,) + strip), kept((PARAM_ROWS, CH)),
        ),
        scratch=[
            pltpu.SMEM((1, 2, 1, FRAMES), jnp.int32), pltpu.VMEM((2,) + strip, BF16), pltpu.VMEM(strip, BF16), sems(13)
        ],
        specs="shhhhhh",
    )
    table = exchange(table)
    inner = lax.ppermute(inner, "dp", mates)
    sides = [(i, i + 1) for i in range(1, dp - 1, 2)]
    outer = lax.ppermute(outer, "dp", sides + [(j, i) for i, j in sides])

    table, stats = call(
        act_first_kernel, "act_first", (table, own, plain), (shape((dp, 2, CH)), kept((STAT_ROWS, CH))), specs="vkk"
    )
    table = exchange(table)

    first_fields, bundle, loss_rows, params = call(
        fields_first_kernel, "fields_first", (flags, inner, outer, plain, stats, pre, cot, loss, act),
        (
            kept((2, FRAMES, ROWS + 4, COLS, CH)), in_hbm(bundled, BF16),
            kept(handed, BF16), kept((PARAM_ROWS, CH)),
        ),
        scratch=[pltpu.VMEM(bundled, BF16), pltpu.VMEM(strip, BF16)] + [pltpu.VMEM(edge, BF16)] * 2 + [sems(7)],
        specs="svvkkhhhh",
    )
    other_bundle = lax.ppermute(bundle, "dp", mates)

    weights = pltpu.VMEM((3, CH, 9 * CH), BF16)
    grad_first, value = call(
        conv_first_kernel, "conv_first", (table, first_fields, params, stats, taps),
        (shape(handed, BF16), in_hbm(edge, BF16)),
        scratch=[
            pltpu.VMEM(columns_of(ROWS + 4), BF16), pltpu.VMEM((3, 9, CH, CH), BF16), weights, pltpu.VMEM(edge, BF16),
            pltpu.VMEM((FRAMES, (ROWS + 2) * COLS, CH), F32), sems(2),
        ],
        specs="vkkkh", flops=20_000_000_000,
    )
    count = lax.axis_size("segment")
    hand = lax.ppermute(grad_first, "segment", [(i + 1, i) for i in range(count - 1)])

    both = pltpu.VMEM((2,) + columns_of(ROWS + 2), BF16)
    acts_dims, taps_dims = (CH, 2 * 9 * CH), (TAPS, CH, CH)
    slope, acts, weight_first = call(
        weight_first_kernel, "weight_first", (table, params, stats, value, bundle, other_bundle),
        (kept((2,) + strip), kept(acts_dims, BF16), kept(taps_dims, BF16)),
        scratch=[both, pltpu.VMEM(acts_dims, BF16)]
        + [pltpu.VMEM(edge, BF16)] + [pltpu.VMEM(bundled, BF16)] * 2 + [pltpu.VMEM((2,) + edge, F32), sems(3)],
        specs="vkkhhh",
    )

    table, incoming = call(
        act_second_kernel, "act_second", (hand, loss_rows, slope, params, stats),
        (shape((dp, 4, CH)), shape(handed, BF16)), specs="vkkkk",
    )
    table = exchange(table)
    arrived = lax.ppermute(incoming, "dp", mates)
    (second_fields,) = call(
        fields_second_kernel, "fields_second", (incoming, arrived, bundle, other_bundle, params, stats),
        (kept((2, 2) + edge),), scratch=[pltpu.VMEM(edge, BF16)] * 2 + [sems(2)], specs="vvhhkk",
    )

    terms, columns, parts = call(
        functools.partial(weight_second_kernel, 1.0 / dp, chunk), "weight_second",
        (table, second_fields, params, stats, weight_first, acts),
        (in_hbm((chips * padded, CH), BF16), in_hbm(columns_of(ROWS + 2), BF16), shape((2, CH))),
        scratch=[
            both, pltpu.VMEM((TAPS * CH, CH), F32),
            pltpu.VMEM((chips * padded, CH), BF16), sems(4),
        ],
        specs="vkkkkk",
    )
    sides = [[2 * i + core for i in range(chips)] for core in range(2)]
    terms = terms.reshape(chips, padded, CH)
    terms = lax.all_to_all(terms, "dp", 0, 0, axis_index_groups=sides, tiled=True)
    (grad_weight,) = call(
        functools.partial(total_kernel, 1.0 / dp), "total", (terms,), (shape((chunk, 1, CH)),)
    )
    (grad_inputs,) = call(
        conv_second_kernel, "conv_second", (params, columns, grad_first, taps),
        (shape((2, FRAMES, ROWS, COLS, CH), BF16),),
        scratch=[
            weights, pltpu.VMEM(columns_of(ROWS + 2), BF16), pltpu.VMEM(handed, BF16),
            pltpu.VMEM((FRAMES, ROWS * COLS, CH), F32), sems(11),
        ],
        specs="khhh",
    )
    width = CH // dp
    mine = lax.dynamic_slice_in_dim(parts, me * width, width, axis=1)
    return (grad_inputs[None], grad_weight.transpose(1, 0, 2), mine[0:1], mine[1:2])


def solution(mesh):
    in_specs = (
        P("segment", None, None, "dp", None, None),
        P("segment", None, None, "dp", None, None),
        P("segment", None, "dp", None, None),
        P(None, None, "dp", None, None),
        P("segment", None, "dp", None),
        P("segment", None, None),
        P("segment", None),
        P("segment", None),
    )
    out_specs = (
        P("segment", None, None, "dp", None, None),
        P("segment", "dp", None),
        P("segment", "dp"),
        P("segment", "dp"),
    )
    return jax.shard_map(local, mesh=mesh, in_specs=in_specs, out_specs=out_specs, check_vma=False)
```
